32 devices in a mesh: section: 4 (over y, x), dp: 8 (over z, core).
Axes of the slice: x: 2, y: 2, z: 4, core: 2. Of those that a mesh axis runs over, the one named last changes fastest.
Arguments:
- inputs: bfloat16 [32, 32, 960], P('dp', None, 'section'), may hold values from -6 to 6
- cotangent: bfloat16 [32, 32, 960], P('dp', None, 'section'), may hold values from -6 to 6
- first_gain: float32 [4, 960], P('section'), may hold values from 0.5 to 1.5
- w_query: bfloat16 [4, 960, 960], P('section'), may hold values from -0.1875 to 0.1875
- w_key: bfloat16 [4, 960, 320], P('section'), may hold values from -0.1875 to 0.1875
- w_value: bfloat16 [4, 960, 320], P('section'), may hold values from -0.1875 to 0.1875
- w_output: bfloat16 [4, 960, 960], P('section'), may hold values from -0.5 to 0.5
- second_gain: float32 [4, 960], P('section'), may hold values from 0.5 to 1.5
- w_gate: bfloat16 [4, 960, 2560], P('section'), may hold values from -0.1875 to 0.1875
- w_up: bfloat16 [4, 960, 2560], P('section'), may hold values from -0.1875 to 0.1875
- w_down: bfloat16 [4, 2560, 960], P('section'), may hold values from -0.125 to 0.125
Outputs:
- section_outputs: float32 [32, 32, 960], P('dp', None, 'section')
- delta_inputs: float32 [32, 32, 960], P('dp', None, 'section')
- delta_first: float32 [4, 960], P('section', 'dp')
- delta_query: float32 [4, 960, 960], P('section', 'dp')
- delta_key: float32 [4, 960, 320], P('section', 'dp')
- delta_value: float32 [4, 960, 320], P('section', 'dp')
- delta_output: float32 [4, 960, 960], P('section', 'dp')
- delta_second: float32 [4, 960], P('section', 'dp')
- delta_gate: float32 [4, 960, 2560], P('section', 'dp')
- delta_up: float32 [4, 960, 2560], P('section', 'dp')
- delta_down: float32 [4, 2560, 960], P('section', None, 'dp')
- global_norm: float32 [], replicated
The draws below stay inside these ranges and needn't reach their ends.
All inputs are finite; a program needn't handle non-finite values.
Results may differ from the reference program's by a relative error of at most 0.025.
Values may be sent and summed in bfloat16 or wider, within the bound.
No kernel may reach another device: no remote copies, remote signals or barrier semaphores. Data moves between devices by JAX's collectives and lax.ppermute only.
A program may use at most 256 MiB of HBM per device.

```python
import jax
import jax.numpy as jnp
from jax import lax

D = 960
HEADS = 15
KV_HEADS = 5
HEAD = 64
FF = 2560
SEQ = 32
SEQS = 32
SECTIONS = 4
N_SECTION = 4


def level_of(key, extent, shards, least, high):
    factor_of = 1.0
    for position, blocks in shards:
        draws = jax.random.uniform(jax.random.fold_in(jax.random.fold_in(key, 6), position), (blocks,), jnp.float32, least / len(shards), high / len(shards))
        factor_of = factor_of * jnp.repeat(jnp.exp(draws), extent[position] // blocks).reshape((-1,) + (1,) * (len(extent) - 1 - position))
    return factor_of


def bell_draw(stream_key, dims, deviation, bound, pieces=(), held_as=jnp.bfloat16):
    array = deviation * jax.random.normal(stream_key, dims, jnp.float32)
    if pieces:
        array = array * level_of(stream_key, dims, pieces, -0.22, 0.18)
    return jnp.clip(array, -bound, bound).astype(held_as)


def setup_inputs(seed: int = 0) -> dict:
    arg_keys = jax.random.split(jax.random.key(seed), 12)
    inputs = bell_draw(arg_keys[0], (SEQS, SEQ, D), 1.0, 6.0, ((0, 8), (2, 4)))
    cotangent = bell_draw(arg_keys[1], (SEQS, SEQ, D), 1.0, 6.0, ((0, 8), (2, 4)))
    first_gain = jnp.clip(1.0 + 0.1 * jax.random.normal(arg_keys[2], (SECTIONS, D), jnp.float32), 0.5, 1.5)
    w_query = bell_draw(arg_keys[3], (SECTIONS, D, D), D ** -0.5, 0.1875, ((0, 4),))
    w_key = bell_draw(arg_keys[4], (SECTIONS, D, KV_HEADS * HEAD), D ** -0.5, 0.1875, ((0, 4),))
    w_value = bell_draw(arg_keys[5], (SECTIONS, D, KV_HEADS * HEAD), D ** -0.5, 0.1875, ((0, 4),))
    w_output = bell_draw(arg_keys[6], (SECTIONS, D, D), (D // 8) ** -0.5, 0.5, ((0, 4),))
    second_gain = jnp.clip(1.0 + 0.1 * jax.random.normal(arg_keys[7], (SECTIONS, D), jnp.float32), 0.5, 1.5)
    w_gate = bell_draw(arg_keys[8], (SECTIONS, D, FF), D ** -0.5, 0.1875, ((0, 4),))
    w_up = bell_draw(arg_keys[9], (SECTIONS, D, FF), D ** -0.5, 0.1875, ((0, 4),))
    w_down = bell_draw(arg_keys[10], (SECTIONS, FF, D), FF ** -0.5, 0.125, ((0, 4),))
    return {"inputs": inputs, "cotangent": cotangent, "first_gain": first_gain, "w_query": w_query, "w_key": w_key, "w_value": w_value, "w_output": w_output, "second_gain": second_gain, "w_gate": w_gate, "w_up": w_up, "w_down": w_down}


@jax.custom_vjp
def low(v):
    return lax.optimization_barrier(v.astype(jnp.bfloat16)).astype(jnp.float32)

@jax.custom_vjp
def low_back(v):
    return v

def low_keep(v):
    return (low(v), None)

def low_pass(kept, grad):
    return (grad,)

def back_keep(v):
    return (v, None)

def back_low(kept, grad):
    return (low(grad),)
low.defvjp(low_keep, low_pass)
low_back.defvjp(back_keep, back_low)
EPSILON = 1e-05
THETA = 10000.0
HIGHEST = lax.Precision.HIGHEST

def project(left, right):
    return jnp.einsum('btd,df->btf', left, right, precision=HIGHEST)

def rotate_half(tensor):
    half = tensor.shape[-1] // 2
    return jnp.concatenate([-tensor[..., half:], tensor[..., :half]], axis=-1)

def rotary_tables(length):
    half = HEAD // 2
    frequency = THETA ** (-(jnp.arange(half, dtype=jnp.float32) * 2.0 / HEAD))
    angles = jnp.arange(length, dtype=jnp.float32)[:, None] * frequency[None, :]
    angles = jnp.concatenate([angles, angles], axis=-1)
    return (jnp.cos(angles)[:, None, :], jnp.sin(angles)[:, None, :])

def block(residual, params):
    first_gain, w_query, w_key, w_value, w_output, second_gain, w_gate, w_up, w_down = params
    batch, length, width = residual.shape
    group = HEADS // KV_HEADS
    cosine, sine = rotary_tables(length)
    positions = jnp.arange(length)
    causal = positions[:, None] >= positions[None, :]
    first_scale = lax.rsqrt(lax.optimization_barrier(jnp.mean(residual * residual, axis=-1, keepdims=True)) + EPSILON)
    normed = low(residual * first_scale * first_gain)
    query = low_back(project(normed, w_query)).reshape(batch, length, HEADS, HEAD)
    keys = low_back(project(normed, w_key)).reshape(batch, length, KV_HEADS, HEAD)
    values = low(low_back(project(normed, w_value))).reshape(batch, length, KV_HEADS, HEAD)
    query_turned = low(query * cosine + rotate_half(query) * sine).reshape(batch, length, KV_HEADS, group, HEAD)
    keys_turned = low(keys * cosine + rotate_half(keys) * sine)
    scores = jnp.einsum('bqgrd,bkgd->bgrqk', query_turned, keys_turned, precision=HIGHEST)
    scores = low_back(scores * HEAD ** (-0.5))
    scores = jnp.where(causal, scores, -1e+30)
    chances = low(jax.nn.softmax(scores, axis=-1))
    context = jnp.einsum('bgrqk,bkgd->bqgrd', chances, values, precision=HIGHEST)
    context = low(low_back(context.reshape(batch, length, width)))
    middle = residual + low_back(project(context, w_output))
    second_scale = lax.rsqrt(lax.optimization_barrier(jnp.mean(middle * middle, axis=-1, keepdims=True)) + EPSILON)
    second_normed = low(middle * second_scale * second_gain)
    gate = low_back(project(second_normed, w_gate))
    up = low_back(project(second_normed, w_up))
    activation = low(gate * jax.nn.sigmoid(gate) * up)
    return middle + low_back(project(activation, w_down))

def forward(residual, params):
    stepped = jax.checkpoint(block)
    for section in range(N_SECTION):
        own = tuple((item[section] for item in params))
        if section > 0:
            residual = low(low_back(residual))
        residual = stepped(residual, own)
        residual = stepped(residual, own)
    return residual

def reference(inputs, cotangent, first_gain, w_query, w_key, w_value, w_output, second_gain, w_gate, w_up, w_down):
    params = tuple((item.astype(jnp.float32) for item in (first_gain, w_query, w_key, w_value, w_output, second_gain, w_gate, w_up, w_down)))
    group_size = 1
    for count in range(1, SEQS + 1):
        if SEQS % count == 0 and count * SEQ <= 4096:
            group_size = count
    groups = SEQS // group_size
    residuals = inputs.astype(jnp.float32).reshape(groups, group_size, SEQ, D)
    slopes = cotangent.astype(jnp.float32).reshape(groups, group_size, SEQ, D)

    def accumulate(totals, pair):
        residual, slope = pair
        result, pullback = jax.vjp(forward, residual, params)
        back_residual, back_params = pullback(slope)
        return (jax.tree.map(jnp.add, totals, back_params), (result, back_residual))
    zeros = tuple((jnp.zeros_like(item) for item in params))
    totals, (results, backs) = lax.scan(accumulate, zeros, (residuals, slopes))
    squares = sum((jnp.sum(item * item) for item in totals))
    return (results.reshape(SEQS, SEQ, D), backs.reshape(SEQS, SEQ, D), totals[0], totals[1], totals[2], totals[3], totals[4], totals[5], totals[6], totals[7], totals[8], jnp.sqrt(squares))
```

```python
import functools

import jax
import jax.numpy as jnp
import numpy as np
from jax import lax
from jax.experimental import pallas as pl
from jax.experimental.pallas import tpu as pltpu
from jax.sharding import PartitionSpec as P

HEADS = 15
KV_HEADS = 5
HEAD = 64
EPSILON = 1e-05
THETA = 10000.0
LANES = 128
PIECES = 2
BAND = 1024
BF = jnp.bfloat16
F32 = jnp.float32
QUERY = HEADS * HEAD
PAIR = KV_HEADS * HEAD
JOINED = QUERY + 2 * PAIR + HEAD
CHUNKS = (HEADS + 1) // 2
MEGA = 2**20


def dot(left, right):
    return jnp.dot(left, right, preferred_element_type=F32)


def dot_last(left, right):
    return lax.dot_general(left, right, (((1,), (1,)), ((), ())), preferred_element_type=F32)


def dot_first(left, right):
    return lax.dot_general(left, right, (((0,), (0,)), ((), ())), preferred_element_type=F32)


def rotary_tables(length, rows):
    half = HEAD // 2
    frequency = THETA ** (-(np.arange(half, dtype=np.float64) * 2.0 / HEAD))
    angles = np.arange(length, dtype=np.float64)[:, None] * frequency[None, :]
    angles = np.concatenate([angles] * (LANES // half), axis=-1)
    sign = np.where(np.arange(LANES) % HEAD < half, -1.0, 1.0)
    copies = (rows // length, 1)
    return (
        np.tile(np.cos(angles), copies).astype(np.float32),
        np.tile(np.sin(angles) * sign, copies).astype(np.float32),
    )


def lane_index(rows):
    return lax.broadcasted_iota(jnp.int32, (rows, LANES), 1)


def half_turned(chunk, first_half):
    return jnp.where(first_half, pltpu.roll(chunk, LANES - HEAD // 2, 1), pltpu.roll(chunk, HEAD // 2, 1))


def mean_scale(residual):
    return lax.rsqrt(jnp.mean(residual * residual, axis=-1, keepdims=True) + EPSILON)


def group_of(head):
    return head // (HEADS // KV_HEADS)


def chunk_heads(chunk):
    return [head for head in (2 * chunk, 2 * chunk + 1) if head < HEADS]


def spread_groups(chunks, first_lane, lower):
    low, high = {}, {}
    for group in range(KV_HEADS):
        column = first_lane + group * HEAD
        chunk = chunks[column // LANES]
        swapped = pltpu.roll(chunk, HEAD, 1)
        here, there = (chunk, swapped) if column % LANES == 0 else (swapped, chunk)
        low[group] = jnp.where(lower, here, 0.0).astype(BF)
        high[group] = jnp.where(lower, 0.0, there).astype(BF)
    return low, high


def chunk_operand(spread, chunk):
    return [spread[head % 2][group_of(head)] for head in chunk_heads(chunk)]


LEFTS = ("normed", "context", "second")


def wide_views(wide, width):
    return [wide.at[pl.ds(i * width, width)] for i in range(3)]


def tall_views(tall, hidden, width):
    return [tall.at[pl.ds(i * hidden, size)] for i, size in enumerate((hidden, hidden, hidden, width))]


def stash_widths(hidden):
    return {
        "query": CHUNKS * LANES,
        "keys": KV_HEADS * 2 * LANES,
        "values": KV_HEADS * 2 * LANES,
        "chances": CHUNKS * 2 * LANES,
        "gate_factor": hidden,
        "up_factor": hidden,
    }


def stash_shape(rows, hidden):
    return (2, rows, sum(stash_widths(hidden).values()))


def views(ref, widths, app):
    starts, start = {}, 0
    for name, width in widths.items():
        starts[name] = start
        start += -(-width // LANES) * LANES

    def get(name, low=0, high=None):
        high = widths[name] if high is None else high
        return ref[app, :, starts[name] + low : starts[name] + high]

    def put(name, value, low=0):
        ref[app, :, starts[name] + low : starts[name] + low + value.shape[1]] = value

    return get, put


def assembled(pieces):
    return jnp.concatenate([piece[...] for piece in pieces], axis=1)


def forward_kernel(tick, rows, length, hidden, old, count, section, gain_one, gain_two, cosine, sine, *rest):
    x, rest = rest[:count], rest[count:]
    (wide, tall, vqkv), (result, leaving), rest = rest[:3], rest[3 + old : 5 + old], rest[8 + old :]
    stash, sums, *left_out, left, left_sems = rest
    width = result.shape[1]
    vg, vu, _ = wide_views(wide, width)
    vd, _, _, vo = tall_views(tall, hidden, width)
    piece = hidden // PIECES

    @pl.when(section[0] == tick)
    def run():
        lanes = lane_index(rows)
        lower = lanes < HEAD
        first_half = lax.rem(lanes, HEAD) < HEAD // 2
        token = lax.broadcasted_iota(jnp.int32, (rows, rows), 0)
        other = lax.broadcasted_iota(jnp.int32, (rows, rows), 1)
        seen = jnp.logical_and(token <= other, lax.div(other, length) == lax.div(token, length))
        cos, sin = cosine[...], sine[...]
        residual = assembled(x).astype(F32)
        writes = []
        for app in range(2):
            def give(name, value, app=app):
                i = LEFTS.index(name)
                left[i, app] = value
                write = pltpu.make_async_copy(left.at[i, app], left_out[i].at[app], left_sems.at[i, app])
                write.start()
                writes.append(write)

            get, put = views(stash, stash_widths(hidden), app)
            sums[0, app] = residual
            normed = (residual * mean_scale(residual) * gain_one[...]).astype(BF)
            give("normed", normed)
            joined = dot(normed, vqkv[...])
            chunks = [joined[:, i * LANES : (i + 1) * LANES] for i in range(JOINED // LANES)]
            turned = (QUERY + PAIR) // LANES
            for i in range(turned):
                chunks[i] = chunks[i] * cos + half_turned(chunks[i], first_half) * sin
            queries = [chunk.astype(BF) for chunk in chunks[:CHUNKS]]
            keys = spread_groups(chunks, QUERY, lower)
            values = spread_groups(chunks, QUERY + PAIR, lower)
            for name, (low, high) in (("keys", keys), ("values", values)):
                for group in range(KV_HEADS):
                    at = 2 * group * LANES
                    put(name, low[group], at)
                    put(name, high[group], at + LANES)
            contexts = []
            for c in range(CHUNKS):
                put("query", queries[c], c * LANES)
                key_side, value_side = chunk_operand(keys, c), chunk_operand(values, c)
                if len(key_side) == 1:
                    key_side = key_side + [jnp.zeros_like(key_side[0])]
                    value_side = value_side + [jnp.zeros_like(value_side[0])]
                parts = []
                for side in range(2):
                    at = (2 * c + side) * LANES
                    if 2 * c + side >= HEADS:
                        parts.append(jnp.zeros((rows, rows), BF))
                        continue
                    scores = dot_last(key_side[side], queries[c]) * HEAD ** (-0.5)
                    scores = jnp.where(seen, scores, -1e30)
                    highest = jnp.max(scores, axis=0, keepdims=True)
                    powers = jnp.exp(scores - highest)
                    total = jnp.sum(powers, axis=0, keepdims=True)
                    parts.append((powers * (1.0 / total)).astype(BF))
                    put("chances", parts[side], at)
                contexts.append(dot_first(jnp.concatenate(parts, axis=0), jnp.concatenate(value_side, axis=0)).astype(BF))
            context = jnp.concatenate(contexts, axis=1)[:, :QUERY]
            give("context", context)
            middle = residual + dot(context, vo[...])
            sums[1, app] = middle
            second = (middle * mean_scale(middle) * gain_two[...]).astype(BF)
            give("second", second)
            total = middle
            for i in range(PIECES):
                cols = slice(i * piece, (i + 1) * piece)
                gate = dot(second, vg[:, cols])
                up = dot(second, vu[:, cols])
                sigma = jax.nn.sigmoid(gate)
                linear = gate * sigma
                put("gate_factor", (up * (sigma + linear * (1.0 - sigma))).astype(BF), i * piece)
                put("up_factor", linear.astype(BF), i * piece)
                total = total + dot((linear * up).astype(BF), vd[cols])
            residual = total
        result[...] = residual
        leaving[...] = residual.astype(BF)
        for write in writes:
            write.wait()


def vmem():
    return pl.BlockSpec(memory_space=pltpu.VMEM)


def anywhere():
    return pl.BlockSpec(memory_space=pl.ANY)


def pinned(arrays):
    return [pltpu.with_memory_space_constraint(array, pltpu.HBM) for array in arrays]


def resident(arrays):
    return [pltpu.with_memory_space_constraint(array, pltpu.VMEM) for array in arrays]


def vmem_like(arrays):
    return [pltpu.VMEM(array.shape, array.dtype) for array in arrays]


def forward_pass(tick, section, x, gains, tables, weights, stash, lefts, length, hidden):
    rows, width = x[0].shape[0], weights[1].shape[1]
    held = [*weights, *stash]
    count = len(x)
    outs = pl.pallas_call(
        functools.partial(forward_kernel, tick, rows, length, hidden, len(stash) + len(lefts), count),
        out_shape=[
            jax.ShapeDtypeStruct((rows, width), F32),
            jax.ShapeDtypeStruct((rows, width), BF),
        ]
        + vmem_like(weights)
        + [pltpu.VMEM(stash_shape(rows, hidden), BF), pltpu.VMEM((2, 2, rows, width), F32)]
        + [pltpu.HBM((2, rows, width), BF)] * len(LEFTS),
        in_specs=[pl.BlockSpec(memory_space=pltpu.SMEM)]
        + [vmem()] * (4 + count + len(held))
        + [pl.BlockSpec(memory_space=pltpu.HBM)] * len(lefts),
        out_specs=[vmem()] * 7 + [pl.BlockSpec(memory_space=pltpu.HBM)] * len(LEFTS),
        scratch_shapes=[
            pltpu.VMEM((len(LEFTS), 2, rows, width), BF),
            pltpu.SemaphoreType.DMA((len(LEFTS), 2)),
        ],
        input_output_aliases={5 + count + i: 2 + i for i in range(len(held) + len(lefts))},
        compiler_params=pltpu.CompilerParams(vmem_limit_bytes=16 * MEGA),
        name="forward_pass",
    )(section, *resident((*gains, *tables, *x, *held)), *pinned(lefts))
    return outs[0], outs[1], outs[2:5], outs[5:7], outs[7:]


SLOPES = {"branch": QUERY, "attend": JOINED, "first": QUERY, "second": QUERY}
SLOPES_WIDTH = sum(-(-width // LANES) * LANES for width in SLOPES.values())


def backward_kernel(tick, rows, length, hidden, old, count, section, gain_one, gain_two, cosine, sine, *rest):
    slope_in, rest = rest[:count], rest[count:]
    (wot, wqkvt, wide, tall, stash, sums), rest = rest[:6], rest[6 + old :]
    entering, leaving, _, _, _, _, made, mixer_out, vot, vqkvt, mixers, sems, mixer_sems = rest
    width = entering.shape[1]
    _, _, vdt = wide_views(wide, width)
    _, vgt, vut, _ = tall_views(tall, hidden, width)
    piece = hidden // PIECES

    @pl.when(section[0] == tick)
    def run():
        lanes = lane_index(rows)
        lower = lanes < HEAD
        first_half = lax.rem(lanes, HEAD) < HEAD // 2
        cos, sin = cosine[...], sine[...]
        copies = [
            pltpu.make_async_copy(wot, vot, sems.at[0]),
            pltpu.make_async_copy(wqkvt, vqkvt, sems.at[1]),
        ]
        for copy in copies:
            copy.start()
        slope = assembled(slope_in).astype(F32)
        writes = []
        for app in (1, 0):
            get, _ = views(stash, stash_widths(hidden), app)
            _, put = views(made, SLOPES, app)
            mixer = slope.astype(BF)
            mixers[app] = mixer
            writes.append(pltpu.make_async_copy(mixers.at[app], mixer_out.at[app], mixer_sems.at[app]))
            writes[-1].start()
            back = None
            for i in range(PIECES):
                cols = slice(i * piece, (i + 1) * piece)
                active = dot(mixer, vdt[:, cols])
                gate = (active * get("gate_factor", i * piece, (i + 1) * piece).astype(F32)).astype(BF)
                up = (active * get("up_factor", i * piece, (i + 1) * piece).astype(F32)).astype(BF)
                part = dot(gate, vgt[cols]) + dot(up, vut[cols])
                back = part if back is None else back + part
            middle = sums[1, app]
            scale = mean_scale(middle)
            shaped = back * gain_two[...]
            inner = jnp.mean(shaped * middle, axis=-1, keepdims=True)
            put("second", (back * middle * scale).astype(BF))
            middle_slope = slope + scale * shaped - middle * (scale * scale * scale * inner)
            branch = middle_slope.astype(BF)
            put("branch", branch)
            if app == 1:
                copies[0].wait()
            context_slope = dot(branch, vot[...])
            query_back, key_back, value_back = [], {}, {}
            for c in range(CHUNKS):
                here = slice(c * LANES, (c + 1) * LANES)
                piece_slope = context_slope[:, here]
                rounded = piece_slope.astype(BF)
                sides = range(len(chunk_heads(c)))

                def operand(name):
                    places = [
                        2 * c + side if name == "chances" else 2 * group_of(2 * c + side) + side for side in sides
                    ]
                    return jnp.concatenate(
                        [get(name, place * LANES, (place + 1) * LANES) for place in places], axis=0
                    )

                chances = operand("chances")
                slopes_here = dot_last(operand("values"), rounded)
                scores = []
                for side in sides:
                    band = slice(side * rows, (side + 1) * rows)
                    chance, chance_slope = chances[band].astype(F32), slopes_here[band]
                    inner = jnp.sum(chance * chance_slope, axis=0, keepdims=True)
                    scores.append((chance * (chance_slope - inner)).astype(BF))
                score = jnp.concatenate(scores, axis=0)
                query_back.append(dot_first(score, operand("keys")))
                key_part = dot(score, get("query", c * LANES, (c + 1) * LANES))
                value_part = dot(chances, rounded)
                for head in chunk_heads(c):
                    side, group = head % 2, group_of(head)
                    band = slice(side * rows, (side + 1) * rows)
                    for store, part in ((key_back, key_part), (value_back, value_part)):
                        item = part[band]
                        store[group, side] = store[group, side] + item if (group, side) in store else item

            def gathered(store, group, up_half):
                low, high = store[group, 0], store[group, 1]
                if up_half:
                    return pltpu.roll(low, HEAD, 1) + high
                return low + pltpu.roll(high, HEAD, 1)

            chunks = query_back + [None] * (JOINED // LANES - CHUNKS)
            for store, start in ((key_back, QUERY), (value_back, QUERY + PAIR)):
                for group in range(KV_HEADS):
                    at, offset = divmod(start + group * HEAD, LANES)
                    item = gathered(store, group, offset > 0)
                    if offset == 0:
                        chunks[at] = jnp.where(lower, item, 0.0)
                    else:
                        chunks[at] = jnp.where(lower, chunks[at], item)
            for i in range((QUERY + PAIR) // LANES):
                chunks[i] = (chunks[i] * cos - half_turned(chunks[i], first_half) * sin) * HEAD ** (-0.5)
            attend = jnp.concatenate([chunk.astype(BF) for chunk in chunks], axis=1)
            put("attend", attend)
            if app == 1:
                copies[1].wait()
            back = dot(attend, vqkvt[...])
            residual = sums[0, app]
            scale = mean_scale(residual)
            shaped = back * gain_one[...]
            inner = jnp.mean(shaped * residual, axis=-1, keepdims=True)
            put("first", (back * residual * scale).astype(BF))
            slope = middle_slope + scale * shaped - residual * (scale * scale * scale * inner)
        entering[...] = slope
        leaving[...] = slope.astype(BF)
        for write in writes:
            write.wait()


def backward_pass(tick, section, slope, gains, tables, stash, streamed, weights, made, mixers, length, hidden, behind):
    rows, width = slope[0].shape[0], weights[1].shape[1]
    held = [*weights, *stash, *made]
    count = len(slope)
    outs = pl.pallas_call(
        functools.partial(backward_kernel, tick, rows, length, hidden, len(made) + len(mixers) + len(behind), count),
        out_shape=[
            jax.ShapeDtypeStruct((rows, width), F32),
            jax.ShapeDtypeStruct((rows, width), BF),
        ]
        + vmem_like([*weights, *stash])
        + [pltpu.VMEM((2, rows, SLOPES_WIDTH), BF), pltpu.HBM((2, rows, width), BF)],
        in_specs=[pl.BlockSpec(memory_space=pltpu.SMEM)]
        + [vmem()] * (4 + count)
        + [pl.BlockSpec(memory_space=pltpu.HBM)] * 2
        + [vmem()] * len(held)
        + [pl.BlockSpec(memory_space=pltpu.HBM)] * len(mixers)
        + [pl.BlockSpec(memory_space=pl.ANY)] * len(behind),
        out_specs=[vmem()] * 7 + [pl.BlockSpec(memory_space=pltpu.HBM)],
        scratch_shapes=[pltpu.VMEM(w.shape, BF) for w in streamed]
        + [pltpu.VMEM((2, rows, width), BF)]
        + [pltpu.SemaphoreType.DMA((2,))] * 2,
        input_output_aliases={7 + count + i: 2 + i for i in range(len(held) + len(mixers))},
        compiler_params=pltpu.CompilerParams(vmem_limit_bytes=16 * MEGA),
        name="backward_pass",
    )(section, *resident((*gains, *tables, *slope)), *pinned(streamed), *resident(held), *pinned(mixers), *behind)
    return outs[0], outs[1], outs[2:4], outs[4:6], outs[6:7], outs[7:]


def turn(source, target, row=0, column=0):
    depth, width = source.shape
    for start in range(0, width, LANES):
        stop = min(start + LANES, width)
        target[row + start : row + stop, column : column + depth] = source[:, start:stop].T


def load_kernel(wq, wkt, wvt, wo, wg, wu, wdt, wide, tall, vqkv, wqkvt, sq, vqkvt, sems, out_sem):
    width, pair = wq.shape[0], wkt.shape[0]
    vg, vu, vdt = wide_views(wide, width)
    vd, _, _, vo = tall_views(tall, wg.shape[1], width)
    copies = [
        pltpu.make_async_copy(source, target, sems.at[i])
        for i, (source, target) in enumerate(
            (
                (wq, sq),
                (wkt, vqkvt.at[pl.ds(width, pair)]),
                (wvt, vqkvt.at[pl.ds(width + pair, pair)]),
                (wdt, vdt),
                (wo, vo),
                (wg, vg),
                (wu, vu),
            )
        )
    ]
    for copy in copies:
        copy.start()
    vqkvt[width + 2 * pair :] = jnp.zeros((HEAD, width), BF)
    for copy in copies[:3]:
        copy.wait()
    vqkv[:, :width] = sq[...]
    vqkv[:, width:] = vqkvt[width:, :].T
    turn(sq, vqkvt)
    out = pltpu.make_async_copy(vqkvt, wqkvt, out_sem)
    out.start()
    copies[3].wait()
    turn(vdt, vd)
    for copy in copies[4:]:
        copy.wait()
    out.wait()


def load(wq, wkt, wvt, wo, wg, wu, wdt):
    width, hidden = wg.shape
    *weights, joined_back = pl.pallas_call(
        load_kernel,
        out_shape=[
            pltpu.VMEM((3 * width, hidden), BF),
            pltpu.VMEM((3 * hidden + width, width), BF),
            pltpu.VMEM((width, JOINED), BF),
            pltpu.HBM((JOINED, width), BF),
        ],
        in_specs=[pl.BlockSpec(memory_space=pltpu.HBM)] * 7,
        out_specs=[vmem()] * 3 + [pl.BlockSpec(memory_space=pltpu.HBM)],
        scratch_shapes=[
            pltpu.VMEM(wq.shape, BF),
            pltpu.VMEM((JOINED, width), BF),
            pltpu.SemaphoreType.DMA((7,)),
            pltpu.SemaphoreType.DMA,
        ],
        compiler_params=pltpu.CompilerParams(vmem_limit_bytes=16 * MEGA),
        name="load_weights",
    )(*pinned((wq, wkt, wvt, wo, wg, wu, wdt)))
    return weights, joined_back


def turn_kernel(hidden, wide, tall, *rest):
    wot, vot, sem = rest[-3:]
    width = wot.shape[0]
    vg, vu, _ = wide_views(wide, width)
    _, vgt, vut, vo = tall_views(tall, hidden, width)
    vot[:, :width] = vo[...].T
    vot[:, width:] = jnp.zeros((width, HEAD), BF)
    out = pltpu.make_async_copy(vot, wot, sem)
    out.start()
    turn(vg, vgt)
    turn(vu, vut)
    out.wait()


def turned(wide, tall):
    hidden, width = wide.shape[1], tall.shape[1]
    return pl.pallas_call(
        functools.partial(turn_kernel, hidden),
        out_shape=vmem_like((wide, tall)) + [pltpu.HBM((width, CHUNKS * LANES), BF)],
        in_specs=[vmem()] * 2,
        out_specs=[vmem()] * 2 + [pl.BlockSpec(memory_space=pltpu.HBM)],
        scratch_shapes=[pltpu.VMEM((width, CHUNKS * LANES), BF), pltpu.SemaphoreType.DMA],
        input_output_aliases={0: 0, 1: 1},
        compiler_params=pltpu.CompilerParams(vmem_limit_bytes=16 * MEGA),
        name="turn_weights",
    )(*resident((wide, tall)))


def parts_kernel(normed, context, made, out, stage, sems):
    rows = normed.shape[0] * normed.shape[1]
    edge = QUERY + 2 * PAIR
    gets = [views(made, SLOPES, app)[0] for app in range(2)]
    attend, branch, first, second = (
        jnp.concatenate([get(name) for get in gets], axis=0) for name in ("attend", "branch", "first", "second")
    )

    def flat(ref):
        return ref[...].reshape(rows, ref.shape[2])

    half = 6 * LANES
    bounds = (0, half, JOINED, stage.shape[1])
    copies = [
        pltpu.make_async_copy(stage.at[:, pl.ds(low, high - low)], out.at[:, pl.ds(low, high - low)], sems.at[i])
        for i, (low, high) in enumerate(zip(bounds[:-1], bounds[1:]))
    ]
    left, right = flat(normed), attend
    stage[:, :half] = dot_first(left, right[:, :half]).astype(BF)
    copies[0].start()
    stage[:, half:JOINED] = dot_first(left, right[:, half:]).astype(BF)
    lanes = lax.broadcasted_iota(jnp.int32, (rows, HEAD), 1)
    gains = dot_first(first, (lanes == 0).astype(BF)) + dot_first(second, (lanes == 1).astype(BF))
    stage[:, edge:JOINED] = gains.astype(BF)
    copies[1].start()
    stage[:, JOINED : JOINED + QUERY] = dot_first(flat(context), branch).astype(BF)
    stage[:, JOINED + QUERY :] = jnp.zeros((QUERY, HEAD), BF)
    copies[2].start()
    for copy in copies:
        copy.wait()


def parts(normed, context, made):
    shape = (QUERY, JOINED + QUERY + HEAD)
    return pl.pallas_call(
        parts_kernel,
        out_shape=pltpu.HBM(shape, BF),
        in_specs=[vmem()] * 3,
        out_specs=pl.BlockSpec(memory_space=pltpu.HBM),
        scratch_shapes=[pltpu.VMEM(shape, BF), pltpu.SemaphoreType.DMA((3,))],
        compiler_params=pltpu.CompilerParams(vmem_limit_bytes=16 * MEGA),
        cost_estimate=pl.CostEstimate(flops=4 * shape[0] * shape[1] * normed.shape[0] * normed.shape[1], bytes_accessed=4 * shape[0] * shape[1], transcendentals=0),
        name="attention_parts",
    )(*resident((normed, context, made)))


def factors_kernel(second, wg, wu, gate_factor, up_factor, active):
    step = 256
    for i in range(second.shape[0] // step):
        band = slice(i * step, (i + 1) * step)
        block = second[band]
        gate = dot(block, wg[...])
        up = dot(block, wu[...])
        sigma = jax.nn.sigmoid(gate)
        linear = gate * sigma
        gate_factor[band] = (up * (sigma + linear * (1.0 - sigma))).astype(BF)
        up_factor[band] = linear.astype(BF)
        active[band] = (linear * up).astype(BF)


def factors(second, wg, wu):
    rows, width = second.shape
    hidden = wg.shape[1]
    block, piece = 512, 512
    wide = pl.BlockSpec((block, piece), lambda i, j: (j, i))
    weight = pl.BlockSpec((width, piece), lambda i, j: (0, i))
    return pl.pallas_call(
        factors_kernel,
        grid=(hidden // piece, rows // block),
        out_shape=[jax.ShapeDtypeStruct((rows, hidden), BF)] * 3,
        in_specs=[
            pl.BlockSpec((block, width), lambda i, j: (j, 0)),
            weight,
            weight,
        ],
        out_specs=[wide] * 3,
        compiler_params=pltpu.CompilerParams(vmem_limit_bytes=16 * MEGA),
        cost_estimate=pl.CostEstimate(flops=4 * rows * width * hidden, bytes_accessed=8 * rows * hidden, transcendentals=rows * hidden),
        name="feed_factors",
    )(second, wg, wu)


def feed_kernel(own, last, mixer, second, chosen, wdt, gate_factor, up_factor, active, *rest):
    earlier, (gate, up, down, squares) = rest[:-4], rest[-4:]
    blocks = mixer[...]
    mine = dot_last(chosen[...], blocks).astype(BF)
    second_own = dot_last(chosen[...], second[...]).astype(BF)
    piece = 512
    total = None
    for i in range(wdt.shape[1] // piece):
        cols = slice(i * piece, (i + 1) * piece)
        slope = dot(blocks, wdt[:, cols])
        gate_slope = (slope * gate_factor[:, cols].astype(F32)).astype(BF)
        up_slope = (slope * up_factor[:, cols].astype(F32)).astype(BF)
        parts = (dot(second_own, gate_slope), dot(second_own, up_slope), dot(mine, active[:, cols]))
        for k, (ref, part) in enumerate(zip((gate, up, down), parts)):
            part = part[:own]
            if earlier:
                part = part + earlier[k][:, cols]
            ref[:, cols] = part
            if last:
                square = jnp.sum(part * part, axis=0, keepdims=True)
                total = square if total is None else total + square
    squares[...] = total if last else jnp.zeros_like(squares)


def feed(own, last, mixer, second, chosen, wdt, made, earlier):
    hidden = wdt.shape[1]
    operands = (mixer, second, chosen, wdt, *made, *earlier)
    return pl.pallas_call(
        functools.partial(feed_kernel, own, last),
        out_shape=[jax.ShapeDtypeStruct((own, hidden), F32)] * 3 + [jax.ShapeDtypeStruct((1, 512), F32)],
        in_specs=[vmem()] * len(operands),
        out_specs=[vmem()] * 4,
        compiler_params=pltpu.CompilerParams(vmem_limit_bytes=16 * MEGA),
        cost_estimate=pl.CostEstimate(flops=2 * (mixer.shape[0] + 3 * own) * wdt.size, bytes_accessed=8 * mixer.shape[0] * hidden, transcendentals=0),
        name="feed_gradient",
    )(*resident(operands))


def after(value, *tokens):
    return lax.optimization_barrier((value,) + tokens)[0]


def gathered_at(block, axis, target):
    count = lax.axis_size(axis)
    pieces = [block if s == target else lax.ppermute(block, axis, [(s, target)]) for s in range(count)]
    return pieces


def spread_from(whole, axis, source):
    count = lax.axis_size(axis)
    width = whole.shape[1] // count
    columns = [whole[:, s * width : (s + 1) * width] for s in range(count)]
    mine = jnp.where(lax.axis_index(axis) == source, columns[source], jnp.zeros_like(columns[source]))
    for s in range(count):
        if s != source:
            mine = mine + lax.ppermute(columns[s], axis, [(source, s)])
    return mine


class LineGather:
    def __init__(self, block, axis):
        self.axis, self.count = axis, lax.axis_size(axis)
        self.line, self.step = self.count // 2, 0
        self.held = [block] + [None] * (self.line - 1)
        self.moving = (block, block)

    def advance(self, *tokens):
        ahead = [(i, i + 2) for i in range(self.count - 2)]
        self.step += 1
        below, above = self.moving
        if tokens:
            below, above, *_ = lax.optimization_barrier((below, above, *tokens))
        below = lax.ppermute(below, self.axis, ahead)
        above = lax.ppermute(above, self.axis, [(b, a) for a, b in ahead])
        self.moving = (below, above)
        for k, item in ((self.step, below), (self.line - self.step, above)):
            self.held[k] = item if self.held[k] is None else self.held[k] + item

    def finish(self):
        while self.step < self.line - 1:
            self.advance()
        mine = jnp.concatenate(self.held)
        other = lax.ppermute(mine, self.axis, [(i, i ^ 1) for i in range(self.count)])
        bands = [slice(start, start + BAND) for start in range(0, mine.shape[0], BAND)]
        return [half[band] for half in (mine, other) for band in bands]


def summed(value, axis):
    count, distance = lax.axis_size(axis), 1
    while distance < count:
        value = value + lax.ppermute(value, axis, [(i, i ^ distance) for i in range(count)])
        distance *= 2
    return value


def per_device(
    inputs, cotangent, first_gain, w_query, w_key, w_value, w_output, second_gain, w_gate, w_up, w_down
):
    sections = lax.axis_size("section")
    replicas = lax.axis_size("dp")
    section = lax.axis_index("section")
    micro, length, part = inputs.shape
    rows, width = micro * length, part * sections
    hidden = w_gate.shape[2]
    own = width // replicas
    w_query, w_key, w_value, w_output = w_query[0], w_key[0], w_value[0], w_output[0]
    w_gate, w_up, w_down = w_gate[0], w_up[0], w_down[0]
    gains = (first_gain, second_gain)
    tables = tuple(jnp.asarray(table) for table in rotary_tables(length, rows))
    place = section.astype(jnp.int32).reshape(1)
    w_query, place = lax.optimization_barrier((w_query, place))
    own_rows = -(-own // 16) * 16
    at = lax.broadcasted_iota(jnp.int32, (own_rows, width), 0)
    chosen = jnp.logical_and(
        lax.broadcasted_iota(jnp.int32, (own_rows, width), 1) == at + own * lax.axis_index("dp"), at < own
    ).astype(BF)

    x = gathered_at(inputs.reshape(rows, part), "section", 0)
    w_down = w_down.T
    weights, joined_back = load(w_query, w_key.T, w_value.T, w_output, w_gate, w_up, w_down)
    last_slope = gathered_at(cotangent.reshape(rows, part), "section", sections - 1)

    stash = lefts = ()
    for t in range(sections):
        final, leaving, weights, stash, lefts = forward_pass(
            t, place, x, gains, tables, weights, stash, lefts, length, hidden
        )
        if t < sections - 1:
            x = [lax.ppermute(leaving, "section", [(t, t + 1)])]
        if t == 0:
            *changed, output_back = turned(*weights[:2])
            weights = [*changed, weights[2]]
    normed, context, second = lefts
    streamed = (output_back, joined_back)
    weights = weights[:2]

    slope = last_slope
    made = mixers = behind = ()
    for t in reversed(range(sections)):
        entering, leaving, weights, stash, made, mixers = backward_pass(
            t, place, slope, gains, tables, stash, streamed, weights, made, mixers, length, hidden, behind
        )
        if t > 0:
            slope = [lax.ppermute(leaving, "section", [(t, t - 1)])]
        if t == sections - 1:
            outputs = spread_from(after(final, leaving).astype(BF), "section", sections - 1)
        if t > 0:
            if t == sections - 1:
                second_all = lax.all_gather(after(second.reshape(2 * rows, width), leaving), "dp", axis=0, tiled=True)
    slopes = made
    bands = [slice(start, start + BAND) for start in range(0, 2 * rows * replicas, BAND)]
    second_all = [second_all[band] for band in bands]
    mixer_all = lax.all_gather(mixers[0].reshape(2 * rows, width), "dp", axis=0, tiled=True)
    mixer_all = [mixer_all[band] for band in bands]
    delta_inputs = spread_from(leaving, "section", 0)
    terms = parts(normed, context, slopes[0])
    reduced = lax.psum_scatter(terms, "dp", scatter_dimension=0, tiled=True).astype(F32)
    made = [factors(second, w_gate, w_up) for second in second_all]
    feed_parts = ()
    for i, (mixer, second, item) in enumerate(zip(mixer_all, second_all, made)):
        last = i == len(made) - 1
        *feed_parts, squares = feed(own, last, mixer, second, chosen, w_down, item, feed_parts)
    gate, up, down = feed_parts
    total = jnp.sum(squares) + jnp.sum(reduced * reduced)
    total = summed(summed(total.reshape(1), "dp"), "section")
    edge = QUERY + 2 * PAIR
    return (
        outputs.astype(F32).reshape(micro, length, part),
        delta_inputs.astype(F32).reshape(micro, length, part),
        reduced[:, edge][None],
        reduced[:, :QUERY][None],
        reduced[:, QUERY : QUERY + PAIR][None],
        reduced[:, QUERY + PAIR : edge][None],
        reduced[:, JOINED : JOINED + QUERY][None],
        reduced[:, edge + 1][None],
        gate[None],
        up[None],
        down.T[None],
        jnp.sqrt(total).reshape(()),
    )


def solution(mesh):
    stacked = P("section", None, None)
    rows = P("section", "dp", None)
    return jax.shard_map(
        per_device,
        mesh=mesh,
        in_specs=(P("dp", None, "section"),) * 2
        + (P("section", None),)
        + (stacked,) * 4
        + (P("section", None),)
        + (stacked,) * 3,
        out_specs=(P("dp", None, "section"),) * 2
        + (P("section", "dp"),)
        + (rows,) * 4
        + (P("section", "dp"),)
        + (rows,) * 2
        + (P("section", None, "dp"), P()),
        check_vma=False,
    )
```

```python
import functools

import jax
import jax.numpy as jnp
import numpy as np
from jax import lax
from jax.experimental import pallas as pl
from jax.experimental.pallas import tpu as pltpu
from jax.sharding import PartitionSpec as P

HEADS = 15
KV_HEADS = 5
HEAD = 64
EPSILON = 1e-05
THETA = 10000.0
LANES = 128
PIECES = 2
BAND = 1024
BF = jnp.bfloat16
F32 = jnp.float32
QUERY = HEADS * HEAD
PAIR = KV_HEADS * HEAD
JOINED = QUERY + 2 * PAIR + HEAD
CHUNKS = (HEADS + 1) // 2
MEGA = 2**20


def dot(left, right):
    return jnp.dot(left, right, preferred_element_type=F32)


def dot_last(left, right):
    return lax.dot_general(left, right, (((1,), (1,)), ((), ())), preferred_element_type=F32)


def dot_first(left, right):
    return lax.dot_general(left, right, (((0,), (0,)), ((), ())), preferred_element_type=F32)


def rotary_tables(length, rows):
    half = HEAD // 2
    frequency = THETA ** (-(np.arange(half, dtype=np.float64) * 2.0 / HEAD))
    angles = np.arange(length, dtype=np.float64)[:, None] * frequency[None, :]
    angles = np.concatenate([angles] * (LANES // half), axis=-1)
    sign = np.where(np.arange(LANES) % HEAD < half, -1.0, 1.0)
    copies = (rows // length, 1)
    return (
        np.tile(np.cos(angles), copies).astype(np.float32),
        np.tile(np.sin(angles) * sign, copies).astype(np.float32),
    )


def lane_index(rows):
    return lax.broadcasted_iota(jnp.int32, (rows, LANES), 1)


def half_turned(chunk, first_half):
    return jnp.where(first_half, pltpu.roll(chunk, LANES - HEAD // 2, 1), pltpu.roll(chunk, HEAD // 2, 1))


def mean_scale(residual):
    return lax.rsqrt(jnp.mean(residual * residual, axis=-1, keepdims=True) + EPSILON)


def group_of(head):
    return head // (HEADS // KV_HEADS)


def chunk_heads(chunk):
    return [head for head in (2 * chunk, 2 * chunk + 1) if head < HEADS]


def spread_groups(chunks, first_lane, lower):
    low, high = {}, {}
    for group in range(KV_HEADS):
        column = first_lane + group * HEAD
        chunk = chunks[column // LANES]
        swapped = pltpu.roll(chunk, HEAD, 1)
        here, there = (chunk, swapped) if column % LANES == 0 else (swapped, chunk)
        low[group] = jnp.where(lower, here, 0.0).astype(BF)
        high[group] = jnp.where(lower, 0.0, there).astype(BF)
    return low, high


def chunk_operand(spread, chunk):
    return [spread[head % 2][group_of(head)] for head in chunk_heads(chunk)]


LEFTS = ("normed", "context", "second")


def halves(ref, *sizes):
    starts = [sum(sizes[:i]) for i in range(len(sizes))]
    return [ref.at[pl.ds(start, size)] for start, size in zip(starts, sizes)]


def stash_widths(hidden):
    return {
        "query": CHUNKS * LANES,
        "keys": KV_HEADS * 2 * LANES,
        "values": KV_HEADS * 2 * LANES,
        "chances": CHUNKS * 2 * LANES,
        "gate_factor": hidden,
        "up_factor": hidden,
    }


def stash_shape(rows, hidden):
    return (2, rows, sum(stash_widths(hidden).values()))


def views(ref, widths, app):
    starts, start = {}, 0
    for name, width in widths.items():
        starts[name] = start
        start += -(-width // LANES) * LANES

    def get(name, low=0, high=None):
        high = widths[name] if high is None else high
        return ref[app, :, starts[name] + low : starts[name] + high]

    def put(name, value, low=0):
        ref[app, :, starts[name] + low : starts[name] + low + value.shape[1]] = value

    return get, put


def assembled(pieces):
    return jnp.concatenate([piece[...] for piece in pieces], axis=1)


def forward_kernel(tick, rows, length, hidden, old, count, section, gain_one, gain_two, cosine, sine, *rest):
    x, rest = rest[:count], rest[count:]
    (wide, tall, vqkv), (result, leaving) = rest[:3], rest[old : old + 2]
    stash, sums, *left_out, left, left_sems = rest[-7:]
    width = result.shape[1]
    vg, vu, _ = halves(wide, width, width, width)
    vd, _, _, vo = halves(tall, hidden, hidden, hidden, width)
    piece = hidden // PIECES

    @pl.when(section[0] == tick)
    def run():
        lanes = lane_index(rows)
        lower = lanes < HEAD
        first_half = lax.rem(lanes, HEAD) < HEAD // 2
        token = lax.broadcasted_iota(jnp.int32, (rows, rows), 0)
        other = lax.broadcasted_iota(jnp.int32, (rows, rows), 1)
        seen = jnp.logical_and(token <= other, lax.div(other, length) == lax.div(token, length))
        cos, sin = cosine[...], sine[...]
        residual = assembled(x).astype(F32)
        writes = []
        for app in range(2):
            def give(name, value, app=app):
                i = LEFTS.index(name)
                left[i, app] = value
                write = pltpu.make_async_copy(left.at[i, app], left_out[i].at[app], left_sems.at[i, app])
                write.start()
                writes.append(write)

            get, put = views(stash, stash_widths(hidden), app)
            sums[0, app] = residual
            normed = (residual * mean_scale(residual) * gain_one[...]).astype(BF)
            give("normed", normed)
            joined = dot(normed, vqkv[...])
            chunks = [joined[:, i * LANES : (i + 1) * LANES] for i in range(JOINED // LANES)]
            turned = (QUERY + PAIR) // LANES
            for i in range(turned):
                chunks[i] = chunks[i] * cos + half_turned(chunks[i], first_half) * sin
            queries = [chunk.astype(BF) for chunk in chunks[:CHUNKS]]
            keys = spread_groups(chunks, QUERY, lower)
            values = spread_groups(chunks, QUERY + PAIR, lower)
            for name, (low, high) in (("keys", keys), ("values", values)):
                for group in range(KV_HEADS):
                    at = 2 * group * LANES
                    put(name, low[group], at)
                    put(name, high[group], at + LANES)
            contexts = []
            for c in range(CHUNKS):
                put("query", queries[c], c * LANES)
                key_side, value_side = chunk_operand(keys, c), chunk_operand(values, c)
                if len(key_side) == 1:
                    key_side = key_side + [jnp.zeros_like(key_side[0])]
                    value_side = value_side + [jnp.zeros_like(value_side[0])]
                parts = []
                for side in range(2):
                    at = (2 * c + side) * LANES
                    if 2 * c + side >= HEADS:
                        parts.append(jnp.zeros((rows, rows), BF))
                        continue
                    scores = dot_last(key_side[side], queries[c]) * HEAD ** (-0.5)
                    scores = jnp.where(seen, scores, -1e30)
                    highest = jnp.max(scores, axis=0, keepdims=True)
                    powers = jnp.exp(scores - highest)
                    total = jnp.sum(powers, axis=0, keepdims=True)
                    parts.append((powers * (1.0 / total)).astype(BF))
                    put("chances", parts[side], at)
                contexts.append(dot_first(jnp.concatenate(parts, axis=0), jnp.concatenate(value_side, axis=0)).astype(BF))
            context = jnp.concatenate(contexts, axis=1)[:, :QUERY]
            give("context", context)
            middle = residual + dot(context, vo[...])
            sums[1, app] = middle
            second = (middle * mean_scale(middle) * gain_two[...]).astype(BF)
            give("second", second)
            total = middle
            for i in range(PIECES):
                cols = slice(i * piece, (i + 1) * piece)
                gate = dot(second, vg[:, cols])
                up = dot(second, vu[:, cols])
                sigma = jax.nn.sigmoid(gate)
                linear = gate * sigma
                put("gate_factor", (up * (sigma + linear * (1.0 - sigma))).astype(BF), i * piece)
                put("up_factor", linear.astype(BF), i * piece)
                total = total + dot((linear * up).astype(BF), vd[cols])
            residual = total
        result[...] = residual
        leaving[...] = residual.astype(BF)
        for write in writes:
            write.wait()


def vmem():
    return pl.BlockSpec(memory_space=pltpu.VMEM)


def anywhere():
    return pl.BlockSpec(memory_space=pl.ANY)


def pinned(arrays):
    return [pltpu.with_memory_space_constraint(array, pltpu.HBM) for array in arrays]


def resident(arrays):
    return [pltpu.with_memory_space_constraint(array, pltpu.VMEM) for array in arrays]


def vmem_like(arrays):
    return [pltpu.VMEM(array.shape, array.dtype) for array in arrays]


def forward_pass(tick, section, x, gains, tables, weights, stash, lefts, length, hidden):
    rows, width = x[0].shape[0], weights[1].shape[1]
    held = [*weights, *stash]
    count = len(x)
    outs = pl.pallas_call(
        functools.partial(forward_kernel, tick, rows, length, hidden, len(held) + len(lefts), count),
        out_shape=[
            jax.ShapeDtypeStruct((rows, width), F32),
            jax.ShapeDtypeStruct((rows, width), BF),
        ]
        + vmem_like(weights)
        + [pltpu.VMEM(stash_shape(rows, hidden), BF), pltpu.VMEM((2, 2, rows, width), F32)]
        + [pltpu.HBM((2, rows, width), BF)] * len(LEFTS),
        in_specs=[pl.BlockSpec(memory_space=pltpu.SMEM)]
        + [vmem()] * (4 + count + len(held))
        + [pl.BlockSpec(memory_space=pltpu.HBM)] * len(lefts),
        out_specs=[vmem()] * (4 + len(weights)) + [pl.BlockSpec(memory_space=pltpu.HBM)] * len(LEFTS),
        scratch_shapes=[
            pltpu.VMEM((len(LEFTS), 2, rows, width), BF),
            pltpu.SemaphoreType.DMA((len(LEFTS), 2)),
        ],
        input_output_aliases={5 + count + i: 2 + i for i in range(len(held) + len(lefts))},
        compiler_params=pltpu.CompilerParams(vmem_limit_bytes=16 * MEGA),
        name="forward_pass",
    )(section, *resident((*gains, *tables, *x, *held)), *pinned(lefts))
    first = 2 + len(weights)
    return outs[0], outs[1], outs[2:first], outs[first : first + 2], outs[first + 2 :]


SLOPES = {"branch": QUERY, "attend": JOINED, "first": QUERY, "second": QUERY}
SLOPES_WIDTH = sum(-(-width // LANES) * LANES for width in SLOPES.values())


def backward_kernel(tick, rows, length, hidden, old, count, saves, section, gain_one, gain_two, cosine, sine, *rest):
    slope_in, rest = rest[:count], rest[count:]
    (wot, wqkvt, wide, tall, stash, sums), rest = rest[:6], rest[6 + old :]
    entering, leaving, _, _, _, _, made, mixer_out, *far, vot, vqkvt, mixers, sems, mixer_sems, far_sems = rest
    near = (stash, sums, made)
    saving = [pltpu.make_async_copy(near[i], far[i], far_sems.at[i]) for i in range(3)] if saves else []
    for copy in saving[:2]:
        copy.start()
    width = entering.shape[1]
    if saves:
        _, _, vdt = halves(wide, width, width, width)
        _, vgt, vut, _ = halves(tall, hidden, hidden, hidden, width)
    else:
        vdt, (vgt, vut) = wide, halves(tall, hidden, hidden)
    piece = hidden // PIECES

    @pl.when(section[0] == tick)
    def run():
        lanes = lane_index(rows)
        lower = lanes < HEAD
        first_half = lax.rem(lanes, HEAD) < HEAD // 2
        cos, sin = cosine[...], sine[...]
        copies = [
            pltpu.make_async_copy(wot, vot, sems.at[0]),
            pltpu.make_async_copy(wqkvt, vqkvt, sems.at[1]),
        ]
        for copy in copies:
            copy.start()
        slope = assembled(slope_in).astype(F32)
        writes = []
        for app in (1, 0):
            get, _ = views(stash, stash_widths(hidden), app)
            _, put = views(made, SLOPES, app)
            mixer = slope.astype(BF)
            mixers[app] = mixer
            writes.append(pltpu.make_async_copy(mixers.at[app], mixer_out.at[app], mixer_sems.at[app]))
            writes[-1].start()
            back = None
            for i in range(PIECES):
                cols = slice(i * piece, (i + 1) * piece)
                active = dot(mixer, vdt[:, cols])
                gate = (active * get("gate_factor", i * piece, (i + 1) * piece).astype(F32)).astype(BF)
                up = (active * get("up_factor", i * piece, (i + 1) * piece).astype(F32)).astype(BF)
                part = dot(gate, vgt[cols]) + dot(up, vut[cols])
                back = part if back is None else back + part
            middle = sums[1, app]
            scale = mean_scale(middle)
            shaped = back * gain_two[...]
            inner = jnp.mean(shaped * middle, axis=-1, keepdims=True)
            put("second", (back * middle * scale).astype(BF))
            middle_slope = slope + scale * shaped - middle * (scale * scale * scale * inner)
            branch = middle_slope.astype(BF)
            put("branch", branch)
            if app == 1:
                copies[0].wait()
            context_slope = dot(branch, vot[...])
            query_back, key_back, value_back = [], {}, {}
            for c in range(CHUNKS):
                here = slice(c * LANES, (c + 1) * LANES)
                piece_slope = context_slope[:, here]
                rounded = piece_slope.astype(BF)
                sides = range(len(chunk_heads(c)))

                def operand(name):
                    places = [
                        2 * c + side if name == "chances" else 2 * group_of(2 * c + side) + side for side in sides
                    ]
                    return jnp.concatenate(
                        [get(name, place * LANES, (place + 1) * LANES) for place in places], axis=0
                    )

                chances = operand("chances")
                slopes_here = dot_last(operand("values"), rounded)
                scores = []
                for side in sides:
                    band = slice(side * rows, (side + 1) * rows)
                    chance, chance_slope = chances[band].astype(F32), slopes_here[band]
                    inner = jnp.sum(chance * chance_slope, axis=0, keepdims=True)
                    scores.append((chance * (chance_slope - inner)).astype(BF))
                score = jnp.concatenate(scores, axis=0)
                query_back.append(dot_first(score, operand("keys")))
                key_part = dot(score, get("query", c * LANES, (c + 1) * LANES))
                value_part = dot(chances, rounded)
                for head in chunk_heads(c):
                    side, group = head % 2, group_of(head)
                    band = slice(side * rows, (side + 1) * rows)
                    for store, part in ((key_back, key_part), (value_back, value_part)):
                        item = part[band]
                        store[group, side] = store[group, side] + item if (group, side) in store else item

            def gathered(store, group, up_half):
                low, high = store[group, 0], store[group, 1]
                if up_half:
                    return pltpu.roll(low, HEAD, 1) + high
                return low + pltpu.roll(high, HEAD, 1)

            chunks = query_back + [None] * (JOINED // LANES - CHUNKS)
            for store, start in ((key_back, QUERY), (value_back, QUERY + PAIR)):
                for group in range(KV_HEADS):
                    at, offset = divmod(start + group * HEAD, LANES)
                    item = gathered(store, group, offset > 0)
                    if offset == 0:
                        chunks[at] = jnp.where(lower, item, 0.0)
                    else:
                        chunks[at] = jnp.where(lower, chunks[at], item)
            for i in range((QUERY + PAIR) // LANES):
                chunks[i] = (chunks[i] * cos - half_turned(chunks[i], first_half) * sin) * HEAD ** (-0.5)
            attend = jnp.concatenate([chunk.astype(BF) for chunk in chunks], axis=1)
            put("attend", attend)
            if app == 1:
                copies[1].wait()
            back = dot(attend, vqkvt[...])
            residual = sums[0, app]
            scale = mean_scale(residual)
            shaped = back * gain_one[...]
            inner = jnp.mean(shaped * residual, axis=-1, keepdims=True)
            put("first", (back * residual * scale).astype(BF))
            slope = middle_slope + scale * shaped - residual * (scale * scale * scale * inner)
        entering[...] = slope
        leaving[...] = slope.astype(BF)
        for write in writes:
            write.wait()

    for copy in saving[2:]:
        copy.start()
    for copy in saving:
        copy.wait()


def backward_pass(tick, section, slope, gains, tables, stash, streamed, weights, made, mixers, length, hidden, saves):
    rows, width = slope[0].shape[0], weights[1].shape[1]
    held = [*weights, *stash, *made]
    count = len(slope)
    outs = pl.pallas_call(
        functools.partial(backward_kernel, tick, rows, length, hidden, len(made) + len(mixers), count, saves),
        out_shape=[
            jax.ShapeDtypeStruct((rows, width), F32),
            jax.ShapeDtypeStruct((rows, width), BF),
        ]
        + vmem_like([*weights, *stash])
        + [pltpu.VMEM((2, rows, SLOPES_WIDTH), BF), pltpu.HBM((2, rows, width), BF)]
        + (
            [pltpu.HBM(array.shape, array.dtype) for array in stash] + [pltpu.HBM((2, rows, SLOPES_WIDTH), BF)]
            if saves
            else []
        ),
        in_specs=[pl.BlockSpec(memory_space=pltpu.SMEM)]
        + [vmem()] * (4 + count)
        + [pl.BlockSpec(memory_space=pltpu.HBM)] * 2
        + [vmem()] * len(held)
        + [pl.BlockSpec(memory_space=pltpu.HBM)] * len(mixers),
        out_specs=[vmem()] * 7 + [pl.BlockSpec(memory_space=pltpu.HBM)] * (4 if saves else 1),
        scratch_shapes=[pltpu.VMEM(w.shape, BF) for w in streamed]
        + [pltpu.VMEM((2, rows, width), BF)]
        + [pltpu.SemaphoreType.DMA((2,))] * 2
        + [pltpu.SemaphoreType.DMA((3,))],
        input_output_aliases={7 + count + i: 2 + i for i in range(len(held) + len(mixers))},
        compiler_params=pltpu.CompilerParams(vmem_limit_bytes=16 * MEGA),
        name="backward_pass",
    )(section, *resident((*gains, *tables, *slope)), *pinned(streamed), *resident(held), *pinned(mixers))
    return outs[0], outs[1], outs[2:4], outs[4:6], outs[6:7], outs[7:8], outs[8:]


def turn(source, target, row=0, column=0):
    depth, width = source.shape
    for start in range(0, width, LANES):
        stop = min(start + LANES, width)
        target[row + start : row + stop, column : column + depth] = source[:, start:stop].T


def load_kernel(wq, wkt, wvt, wo, wg, wu, wdt, wide, tall, vqkv, wqkvt, sq, vqkvt, sems, out_sem):
    width, pair = wq.shape[0], wkt.shape[0]
    vg, vu, vdt = halves(wide, width, width, width)
    vd, _, _, vo = halves(tall, *[wg.shape[1]] * 3, width)
    copies = [
        pltpu.make_async_copy(source, target, sems.at[i])
        for i, (source, target) in enumerate(
            (
                (wq, sq),
                (wkt, vqkvt.at[pl.ds(width, pair)]),
                (wvt, vqkvt.at[pl.ds(width + pair, pair)]),
                (wdt, vdt),
                (wo, vo),
                (wg, vg),
                (wu, vu),
            )
        )
    ]
    for copy in copies:
        copy.start()
    vqkvt[width + 2 * pair :] = jnp.zeros((HEAD, width), BF)
    for copy in copies[:3]:
        copy.wait()
    vqkv[:, :width] = sq[...]
    vqkv[:, width:] = vqkvt[width:, :].T
    turn(sq, vqkvt)
    out = pltpu.make_async_copy(vqkvt, wqkvt, out_sem)
    out.start()
    copies[3].wait()
    turn(vdt, vd)
    for copy in copies[4:]:
        copy.wait()
    out.wait()


def load(wq, wkt, wvt, wo, wg, wu, wdt):
    width, hidden = wg.shape
    *weights, joined_back = pl.pallas_call(
        load_kernel,
        out_shape=[
            pltpu.VMEM((3 * width, hidden), BF),
            pltpu.VMEM((3 * hidden + width, width), BF),
            pltpu.VMEM((width, JOINED), BF),
            pltpu.HBM((JOINED, width), BF),
        ],
        in_specs=[pl.BlockSpec(memory_space=pltpu.HBM)] * 7,
        out_specs=[vmem()] * 3 + [pl.BlockSpec(memory_space=pltpu.HBM)],
        scratch_shapes=[
            pltpu.VMEM(wq.shape, BF),
            pltpu.VMEM((JOINED, width), BF),
            pltpu.SemaphoreType.DMA((7,)),
            pltpu.SemaphoreType.DMA,
        ],
        compiler_params=pltpu.CompilerParams(vmem_limit_bytes=16 * MEGA),
        name="load_weights",
    )(*pinned((wq, wkt, wvt, wo, wg, wu, wdt)))
    return weights, joined_back


def turn_kernel(wide, tall, wide_out, tall_out, wot, wback, vot, sems):
    hidden, width = wide.shape[1], tall.shape[1]
    vg, vu, _ = halves(wide, width, width, width)
    _, vgt, vut, vo = halves(tall, hidden, hidden, hidden, width)
    copies = [
        pltpu.make_async_copy(source, target, sems.at[i])
        for i, (source, target) in enumerate(zip((vot, vgt, vut), [wot] + halves(wback, hidden, hidden)))
    ]
    vot[:, :width] = vo[...].T
    vot[:, width:] = jnp.zeros((width, HEAD), BF)
    copies[0].start()
    for source, target, copy in zip((vg, vu), (vgt, vut), copies[1:]):
        turn(source, target)
        copy.start()
    for copy in copies:
        copy.wait()


def turned(wide, tall):
    hidden, width = wide.shape[1], tall.shape[1]
    back = (2 * hidden, width)
    return pl.pallas_call(
        turn_kernel,
        out_shape=vmem_like((wide, tall))
        + [pltpu.HBM((width, CHUNKS * LANES), BF), pltpu.HBM(back, BF)],
        in_specs=[vmem()] * 2,
        out_specs=[vmem()] * 2 + [pl.BlockSpec(memory_space=pltpu.HBM)] * 2,
        scratch_shapes=[
            pltpu.VMEM((width, CHUNKS * LANES), BF),
            pltpu.SemaphoreType.DMA((3,)),
        ],
        input_output_aliases={0: 0, 1: 1},
        compiler_params=pltpu.CompilerParams(vmem_limit_bytes=16 * MEGA),
        name="turn_weights",
    )(*resident((wide, tall)))


def moved_kernel(count, *refs):
    copies = [
        pltpu.make_async_copy(refs[i], refs[count + i], refs[-1].at[i]) for i in range(count)
    ]
    for copy in copies:
        copy.start()
    for copy in copies:
        copy.wait()


def moved(arrays, inward):
    count = len(arrays)
    near, far = (vmem(), pltpu.VMEM), (pl.BlockSpec(memory_space=pltpu.HBM), pltpu.HBM)
    (source, _), (target, place) = (far, near) if inward else (near, far)
    return pl.pallas_call(
        functools.partial(moved_kernel, count),
        out_shape=[place(array.shape, array.dtype) for array in arrays],
        in_specs=[source] * count,
        out_specs=[target] * count,
        scratch_shapes=[pltpu.SemaphoreType.DMA((count,))],
        compiler_params=pltpu.CompilerParams(vmem_limit_bytes=16 * MEGA),
        cost_estimate=pl.CostEstimate(
            flops=0, bytes_accessed=2 * sum(array.size * array.dtype.itemsize for array in arrays), transcendentals=0
        ),
        name="restored" if inward else "saved",
    )(*(pinned if inward else resident)(arrays))


def parts_kernel(normed, context, made, out, stage, sems):
    rows = normed.shape[0] * normed.shape[1]
    edge = QUERY + 2 * PAIR
    gets = [views(made, SLOPES, app)[0] for app in range(2)]
    attend, branch, first, second = (
        jnp.concatenate([get(name) for get in gets], axis=0) for name in ("attend", "branch", "first", "second")
    )

    def flat(ref):
        return ref[...].reshape(rows, ref.shape[2])

    half = 6 * LANES
    bounds = (0, half, JOINED, stage.shape[1])
    copies = [
        pltpu.make_async_copy(stage.at[:, pl.ds(low, high - low)], out.at[:, pl.ds(low, high - low)], sems.at[i])
        for i, (low, high) in enumerate(zip(bounds[:-1], bounds[1:]))
    ]
    left, right = flat(normed), attend
    stage[:, :half] = dot_first(left, right[:, :half]).astype(BF)
    copies[0].start()
    stage[:, half:JOINED] = dot_first(left, right[:, half:]).astype(BF)
    lanes = lax.broadcasted_iota(jnp.int32, (rows, HEAD), 1)
    gains = dot_first(first, (lanes == 0).astype(BF)) + dot_first(second, (lanes == 1).astype(BF))
    stage[:, edge:JOINED] = gains.astype(BF)
    copies[1].start()
    stage[:, JOINED : JOINED + QUERY] = dot_first(flat(context), branch).astype(BF)
    stage[:, JOINED + QUERY :] = jnp.zeros((QUERY, HEAD), BF)
    copies[2].start()
    for copy in copies:
        copy.wait()


def parts(normed, context, made):
    shape = (QUERY, JOINED + QUERY + HEAD)
    return pl.pallas_call(
        parts_kernel,
        out_shape=pltpu.HBM(shape, BF),
        in_specs=[vmem()] * 3,
        out_specs=pl.BlockSpec(memory_space=pltpu.HBM),
        scratch_shapes=[pltpu.VMEM(shape, BF), pltpu.SemaphoreType.DMA((3,))],
        compiler_params=pltpu.CompilerParams(vmem_limit_bytes=16 * MEGA),
        cost_estimate=pl.CostEstimate(flops=4 * shape[0] * shape[1] * normed.shape[0] * normed.shape[1], bytes_accessed=4 * shape[0] * shape[1], transcendentals=0),
        name="attention_parts",
    )(*resident((normed, context, made)))


def factors_kernel(second, wg, wu, gate_factor, up_factor, active):
    step = 256
    for i in range(second.shape[0] // step):
        band = slice(i * step, (i + 1) * step)
        block = second[band]
        gate = dot(block, wg[...])
        up = dot(block, wu[...])
        sigma = jax.nn.sigmoid(gate)
        linear = gate * sigma
        gate_factor[band] = (up * (sigma + linear * (1.0 - sigma))).astype(BF)
        up_factor[band] = linear.astype(BF)
        active[band] = (linear * up).astype(BF)


def factors(second, wg, wu):
    rows, width = second.shape
    hidden = wg.shape[1]
    block, piece = 512, 512
    wide = pl.BlockSpec((block, piece), lambda i, j: (j, i))
    weight = pl.BlockSpec((width, piece), lambda i, j: (0, i))
    return pl.pallas_call(
        factors_kernel,
        grid=(hidden // piece, rows // block),
        out_shape=[pltpu.HBM((rows, hidden), BF)] * 3,
        in_specs=[
            pl.BlockSpec((block, width), lambda i, j: (j, 0)),
            weight,
            weight,
        ],
        out_specs=[wide] * 3,
        compiler_params=pltpu.CompilerParams(vmem_limit_bytes=16 * MEGA),
        cost_estimate=pl.CostEstimate(flops=4 * rows * width * hidden, bytes_accessed=8 * rows * hidden, transcendentals=rows * hidden),
        name="feed_factors",
    )(second, wg, wu)


def feed_kernel(own, last, mixer, second, chosen, wdt, gate_factor, up_factor, active, *rest):
    earlier, (gate, up, down, squares, mine, second_own) = rest[:-6], rest[-6:]

    @pl.when(pl.program_id(0) == 0)
    def pick():
        mine[...] = dot_last(chosen[...], mixer[...]).astype(BF)
        second_own[...] = dot_last(chosen[...], second[...]).astype(BF)
        squares[...] = jnp.zeros_like(squares)

    slope = dot(mixer[...], wdt[...])
    gate_slope = (slope * gate_factor[...].astype(F32)).astype(BF)
    up_slope = (slope * up_factor[...].astype(F32)).astype(BF)
    parts = (dot(second_own[...], gate_slope), dot(second_own[...], up_slope), dot(mine[...], active[...]))
    for k, (ref, part) in enumerate(zip((gate, up, down), parts)):
        part = part[:own]
        if earlier:
            part = part + earlier[k][...]
        ref[...] = part
        if last:
            squares[...] += jnp.sum(part * part, axis=0, keepdims=True)


def feed(own, last, mixer, second, chosen, wdt, made, earlier):
    rows, width = mixer.shape
    hidden = wdt.shape[1]
    piece = 512
    whole = lambda i: (0, 0)
    column = lambda i: (0, i)
    once = pl.Buffered(1)
    result = pl.BlockSpec((own, piece), column)
    return pl.pallas_call(
        functools.partial(feed_kernel, own, last),
        grid=(hidden // piece,),
        out_shape=[jax.ShapeDtypeStruct((own, hidden), F32)] * 3 + [jax.ShapeDtypeStruct((1, piece), F32)],
        in_specs=[pl.BlockSpec((rows, width), whole, pipeline_mode=once)] * 2
        + [pl.BlockSpec(chosen.shape, whole, pipeline_mode=once), pl.BlockSpec((width, piece), column)]
        + [pl.BlockSpec((rows, piece), column)] * 3
        + [result] * len(earlier),
        out_specs=[result] * 3 + [pl.BlockSpec((1, piece), whole)],
        scratch_shapes=[pltpu.VMEM((chosen.shape[0], rows), BF)] * 2,
        compiler_params=pltpu.CompilerParams(vmem_limit_bytes=16 * MEGA),
        cost_estimate=pl.CostEstimate(
            flops=2 * (rows + 3 * own) * wdt.size, bytes_accessed=8 * rows * hidden, transcendentals=0
        ),
        name="feed_gradient",
    )(mixer, second, chosen, wdt, *made, *earlier)


def finish_kernel(terms, squares, query, key, value, output, gains, total):
    edge = QUERY + 2 * PAIR
    whole = terms[...].astype(F32)
    query[...] = whole[:, :QUERY]
    key[...] = whole[:, QUERY : QUERY + PAIR].T
    value[...] = whole[:, QUERY + PAIR : edge].T
    output[...] = whole[:, JOINED : JOINED + QUERY]
    gains[...] = whole[:, edge : edge + 2]
    sums = jnp.sum(whole * whole, axis=0, keepdims=True)
    total[...] = jnp.sum(sums, axis=1, keepdims=True) + jnp.sum(squares[...], axis=1, keepdims=True)


def finish(terms, squares):
    own = terms.shape[0]
    shapes = ((own, QUERY), (PAIR, own), (PAIR, own), (own, QUERY), (own, 2), (1, 1))
    return pl.pallas_call(
        finish_kernel,
        out_shape=[jax.ShapeDtypeStruct(shape, F32) for shape in shapes],
        in_specs=[vmem()] * 2,
        out_specs=[vmem()] * len(shapes),
        compiler_params=pltpu.CompilerParams(vmem_limit_bytes=16 * MEGA),
        name="finish",
    )(terms, squares)


def after(value, *tokens):
    return lax.optimization_barrier((value,) + tokens)[0]


def gathered_at(block, axis, target):
    count = lax.axis_size(axis)
    pieces = [block if s == target else lax.ppermute(block, axis, [(s, target)]) for s in range(count)]
    return pieces


def spread_from(whole, axis, source):
    count = lax.axis_size(axis)
    width = whole.shape[1] // count
    columns = [whole[:, s * width : (s + 1) * width] for s in range(count)]
    mine = jnp.where(lax.axis_index(axis) == source, columns[source], jnp.zeros_like(columns[source]))
    for s in range(count):
        if s != source:
            mine = mine + lax.ppermute(columns[s], axis, [(source, s)])
    return mine


class LineGather:
    def __init__(self, block, axis):
        self.axis, self.count = axis, lax.axis_size(axis)
        self.line, self.step = self.count // 2, 0
        self.held = [block] + [None] * (self.line - 1)
        self.moving = (block, block)

    def advance(self, *tokens):
        ahead = [(i, i + 2) for i in range(self.count - 2)]
        self.step += 1
        below, above = self.moving
        if tokens:
            below, above, *_ = lax.optimization_barrier((below, above, *tokens))
        below = lax.ppermute(below, self.axis, ahead)
        above = lax.ppermute(above, self.axis, [(b, a) for a, b in ahead])
        self.moving = (below, above)
        for k, item in ((self.step, below), (self.line - self.step, above)):
            self.held[k] = item if self.held[k] is None else self.held[k] + item

    def finish(self):
        while self.step < self.line - 1:
            self.advance()
        mine = jnp.concatenate(self.held)
        other = lax.ppermute(mine, self.axis, [(i, i ^ 1) for i in range(self.count)])
        bands = [slice(start, start + BAND) for start in range(0, mine.shape[0], BAND)]
        return [half[band] for half in (mine, other) for band in bands]


def summed(value, axis, distances):
    count = lax.axis_size(axis)
    values = [value] + [lax.ppermute(value, axis, [(i, i ^ d) for i in range(count)]) for d in distances]
    while len(values) > 1:
        values = [a + b for a, b in zip(values[::2], values[1::2])]
    return values[0]


def per_device(
    inputs, cotangent, first_gain, w_query, w_key, w_value, w_output, second_gain, w_gate, w_up, w_down
):
    sections = lax.axis_size("section")
    replicas = lax.axis_size("dp")
    section = lax.axis_index("section")
    micro, length, part = inputs.shape
    rows, width = micro * length, part * sections
    hidden = w_gate.shape[2]
    own = width // replicas
    w_query, w_key, w_value, w_output = w_query[0], w_key[0], w_value[0], w_output[0]
    w_gate, w_up, w_down = w_gate[0], w_up[0], w_down[0]
    gains = (first_gain, second_gain)
    tables = tuple(jnp.asarray(table) for table in rotary_tables(length, rows))
    place = section.astype(jnp.int32).reshape(1)
    w_query, place = lax.optimization_barrier((w_query, place))
    own_rows = -(-own // 16) * 16
    at = lax.broadcasted_iota(jnp.int32, (own_rows, width), 0)
    chosen = jnp.logical_and(
        lax.broadcasted_iota(jnp.int32, (own_rows, width), 1) == at + own * lax.axis_index("dp"), at < own
    ).astype(BF)

    x = gathered_at(inputs.reshape(rows, part), "section", 0)
    w_down = w_down.T
    weights, joined_back = load(w_query, w_key.T, w_value.T, w_output, w_gate, w_up, w_down)
    last_slope = gathered_at(cotangent.reshape(rows, part), "section", sections - 1)

    stash = lefts = ()
    for t in range(sections):
        final, leaving, weights, stash, lefts = forward_pass(
            t, place, x, gains, tables, weights, stash, lefts, length, hidden
        )
        if t < sections - 1:
            x = [lax.ppermute(leaving, "section", [(t, t + 1)])]
        if t == 0:
            *changed, output_back, back_far = turned(*weights[:2])
            weights = [*changed, *weights[2:]]
    normed, context, second = lefts
    streamed = (output_back, joined_back)
    weights = weights[:2]

    slope = last_slope
    made = mixers = ()
    for t in reversed(range(sections)):
        entering, leaving, weights, stash, made, mixers, far = backward_pass(
            t, place, slope, gains, tables, stash, streamed, weights, made, mixers, length, hidden, t == sections - 1
        )
        if t > 0:
            slope = [lax.ppermute(leaving, "section", [(t, t - 1)])]
        if t == sections - 1:
            outputs = spread_from(after(final, leaving).astype(BF), "section", sections - 1)
        if t > 0:
            if t == sections - 1:
                second_all = lax.all_gather(after(second.reshape(2 * rows, width), far[0]), "dp", axis=0, tiled=True)
                near = moved((w_down, back_far, *far), True)
                weights, stash, made = near[:2], near[2:4], near[4:]
    slopes = made
    bands = [slice(start, start + BAND) for start in range(0, 2 * rows * replicas, BAND)]
    second_all = [second_all[band] for band in bands]
    mixer_all = lax.all_gather(mixers[0].reshape(2 * rows, width), "dp", axis=0, tiled=True)
    mixer_all = [mixer_all[band] for band in bands]
    delta_inputs = spread_from(leaving, "section", 0)
    terms = parts(normed, context, slopes[0])
    reduced = lax.psum_scatter(terms, "dp", scatter_dimension=0, tiled=True)
    made = [factors(second, w_gate, w_up) for second in second_all]
    feed_parts = ()
    for i, (mixer, second, item) in enumerate(zip(mixer_all, second_all, made)):
        last = i == len(made) - 1
        *feed_parts, squares = feed(own, last, mixer, second, chosen, w_down, item, feed_parts)
    gate, up, down = feed_parts
    query, key, value, output, gain_terms, total = finish(reduced, squares)
    total = summed(total, "dp", [1])
    total = summed(total, "dp", range(2, replicas, 2))
    total = summed(total, "section", range(1, sections))
    return (
        outputs.astype(F32).reshape(micro, length, part),
        delta_inputs.astype(F32).reshape(micro, length, part),
        gain_terms[:, 0][None],
        query[None],
        key.T[None],
        value.T[None],
        output[None],
        gain_terms[:, 1][None],
        gate[None],
        up[None],
        down.T[None],
        jnp.sqrt(total).reshape(()),
    )


def solution(mesh):
    stacked = P("section", None, None)
    rows = P("section", "dp", None)
    return jax.shard_map(
        per_device,
        mesh=mesh,
        in_specs=(P("dp", None, "section"),) * 2
        + (P("section", None),)
        + (stacked,) * 4
        + (P("section", None),)
        + (stacked,) * 3,
        out_specs=(P("dp", None, "section"),) * 2
        + (P("section", "dp"),)
        + (rows,) * 4
        + (P("section", "dp"),)
        + (rows,) * 2
        + (P("section", None, "dp"), P()),
        check_vma=False,
    )
```

```python
import functools

import jax
import jax.numpy as jnp
import numpy as np
from jax import lax
from jax.experimental import pallas as pl
from jax.experimental.pallas import tpu as pltpu
from jax.sharding import PartitionSpec as P

HEADS = 15
KV_HEADS = 5
HEAD = 64
EPSILON = 1e-05
THETA = 10000.0
LANES = 128
PIECES = 2
BAND = 1024
BF = jnp.bfloat16
F32 = jnp.float32
QUERY = HEADS * HEAD
PAIR = KV_HEADS * HEAD
JOINED = QUERY + 2 * PAIR + HEAD
CHUNKS = (HEADS + 1) // 2
MEGA = 2**20


def dot(left, right):
    return jnp.dot(left, right, preferred_element_type=F32)


def dot_last(left, right):
    return lax.dot_general(left, right, (((1,), (1,)), ((), ())), preferred_element_type=F32)


def dot_first(left, right):
    return lax.dot_general(left, right, (((0,), (0,)), ((), ())), preferred_element_type=F32)


def rotary_tables(length, rows):
    half = HEAD // 2
    frequency = THETA ** (-(np.arange(half, dtype=np.float64) * 2.0 / HEAD))
    angles = np.arange(length, dtype=np.float64)[:, None] * frequency[None, :]
    angles = np.concatenate([angles] * (LANES // half), axis=-1)
    sign = np.where(np.arange(LANES) % HEAD < half, -1.0, 1.0)
    copies = (rows // length, 1)
    return (
        np.tile(np.cos(angles), copies).astype(np.float32),
        np.tile(np.sin(angles) * sign, copies).astype(np.float32),
    )


def lane_index(rows):
    return lax.broadcasted_iota(jnp.int32, (rows, LANES), 1)


def half_turned(chunk, first_half):
    return jnp.where(first_half, pltpu.roll(chunk, LANES - HEAD // 2, 1), pltpu.roll(chunk, HEAD // 2, 1))


def mean_scale(residual):
    return lax.rsqrt(jnp.mean(residual * residual, axis=-1, keepdims=True) + EPSILON)


def group_of(head):
    return head // (HEADS // KV_HEADS)


def chunk_heads(chunk):
    return [head for head in (2 * chunk, 2 * chunk + 1) if head < HEADS]


def spread_groups(chunks, first_lane, lower):
    low, high = {}, {}
    for group in range(KV_HEADS):
        column = first_lane + group * HEAD
        chunk = chunks[column // LANES]
        swapped = pltpu.roll(chunk, HEAD, 1)
        here, there = (chunk, swapped) if column % LANES == 0 else (swapped, chunk)
        low[group] = jnp.where(lower, here, 0.0).astype(BF)
        high[group] = jnp.where(lower, 0.0, there).astype(BF)
    return low, high


def chunk_operand(spread, chunk):
    return [spread[head % 2][group_of(head)] for head in chunk_heads(chunk)]


LEFTS = ("normed", "context", "second")


def halves(ref, *sizes):
    starts = [sum(sizes[:i]) for i in range(len(sizes))]
    return [ref.at[pl.ds(start, size)] for start, size in zip(starts, sizes)]


def stash_widths(hidden):
    return {
        "query": CHUNKS * LANES,
        "keys": KV_HEADS * 2 * LANES,
        "values": KV_HEADS * 2 * LANES,
        "chances": CHUNKS * 2 * LANES,
        "gate_factor": hidden,
        "up_factor": hidden,
    }


def stash_shape(rows, hidden):
    return (2, rows, sum(stash_widths(hidden).values()))


def views(ref, widths, app):
    starts, start = {}, 0
    for name, width in widths.items():
        starts[name] = start
        start += -(-width // LANES) * LANES

    def get(name, low=0, high=None):
        high = widths[name] if high is None else high
        return ref[app, :, starts[name] + low : starts[name] + high]

    def put(name, value, low=0):
        ref[app, :, starts[name] + low : starts[name] + low + value.shape[1]] = value

    return get, put


def assembled(pieces):
    return jnp.concatenate([piece[...] for piece in pieces], axis=1)


def forward_kernel(tick, rows, length, hidden, old, count, section, gain_one, gain_two, cosine, sine, *rest):
    x, rest = rest[:count], rest[count:]
    (wide, tall, vqkv), (result, leaving) = rest[:3], rest[old : old + 2]
    stash, sums, *left_out, left, left_sems = rest[-7:]
    width = result.shape[1]
    vg, vu, _ = halves(wide, width, width, width)
    vd, _, _, vo = halves(tall, hidden, hidden, hidden, width)
    piece = hidden // PIECES

    @pl.when(section[0] == tick)
    def run():
        lanes = lane_index(rows)
        lower = lanes < HEAD
        first_half = lax.rem(lanes, HEAD) < HEAD // 2
        token = lax.broadcasted_iota(jnp.int32, (rows, rows), 0)
        other = lax.broadcasted_iota(jnp.int32, (rows, rows), 1)
        seen = jnp.logical_and(token <= other, lax.div(other, length) == lax.div(token, length))
        cos, sin = cosine[...], sine[...]
        residual = assembled(x).astype(F32)
        writes = []
        for app in range(2):
            def give(name, value, app=app):
                i = LEFTS.index(name)
                left[i, app] = value
                write = pltpu.make_async_copy(left.at[i, app], left_out[i].at[app], left_sems.at[i, app])
                write.start()
                writes.append(write)

            get, put = views(stash, stash_widths(hidden), app)
            sums[0, app] = residual
            normed = (residual * mean_scale(residual) * gain_one[...]).astype(BF)
            give("normed", normed)
            joined = dot(normed, vqkv[...])
            chunks = [joined[:, i * LANES : (i + 1) * LANES] for i in range(JOINED // LANES)]
            turned = (QUERY + PAIR) // LANES
            for i in range(turned):
                chunks[i] = chunks[i] * cos + half_turned(chunks[i], first_half) * sin
            queries = [chunk.astype(BF) for chunk in chunks[:CHUNKS]]
            keys = spread_groups(chunks, QUERY, lower)
            values = spread_groups(chunks, QUERY + PAIR, lower)
            for name, (low, high) in (("keys", keys), ("values", values)):
                for group in range(KV_HEADS):
                    at = 2 * group * LANES
                    put(name, low[group], at)
                    put(name, high[group], at + LANES)
            key_sides = [jnp.concatenate(chunk_operand(keys, c), axis=0) for c in range(CHUNKS)]
            value_sides = [jnp.concatenate(chunk_operand(values, c), axis=0) for c in range(CHUNKS)]
            all_scores = [dot_last(key_sides[c], queries[c]) for c in range(CHUNKS)]
            all_chances = []
            for c in range(CHUNKS):
                put("query", queries[c], c * LANES)
                parts = []
                for side in range(len(chunk_heads(c))):
                    at = (2 * c + side) * LANES
                    scores = all_scores[c][side * rows : (side + 1) * rows] * HEAD ** (-0.5)
                    scores = jnp.where(seen, scores, -1e30)
                    highest = jnp.max(scores, axis=0, keepdims=True)
                    powers = jnp.exp(scores - highest)
                    total = jnp.sum(powers, axis=0, keepdims=True)
                    parts.append((powers * (1.0 / total)).astype(BF))
                    put("chances", parts[side], at)
                all_chances.append(jnp.concatenate(parts, axis=0))
            contexts = [dot_first(all_chances[c], value_sides[c]).astype(BF) for c in range(CHUNKS)]
            context = jnp.concatenate(contexts, axis=1)[:, :QUERY]
            give("context", context)
            middle = residual + dot(context, vo[...])
            sums[1, app] = middle
            second = (middle * mean_scale(middle) * gain_two[...]).astype(BF)
            give("second", second)
            total = middle
            for i in range(PIECES):
                cols = slice(i * piece, (i + 1) * piece)
                gate = dot(second, vg[:, cols])
                up = dot(second, vu[:, cols])
                sigma = jax.nn.sigmoid(gate)
                linear = gate * sigma
                put("gate_factor", (up * (sigma + linear * (1.0 - sigma))).astype(BF), i * piece)
                put("up_factor", linear.astype(BF), i * piece)
                total = total + dot((linear * up).astype(BF), vd[cols])
            residual = total
        result[...] = residual
        leaving[...] = residual.astype(BF)
        for write in writes:
            write.wait()


def vmem():
    return pl.BlockSpec(memory_space=pltpu.VMEM)


def anywhere():
    return pl.BlockSpec(memory_space=pl.ANY)


def pinned(arrays):
    return [pltpu.with_memory_space_constraint(array, pltpu.HBM) for array in arrays]


def resident(arrays):
    return [pltpu.with_memory_space_constraint(array, pltpu.VMEM) for array in arrays]


def vmem_like(arrays):
    return [pltpu.VMEM(array.shape, array.dtype) for array in arrays]


def forward_pass(tick, section, x, gains, tables, weights, stash, lefts, length, hidden):
    rows, width = x[0].shape[0], weights[1].shape[1]
    held = [*weights, *stash]
    count = len(x)
    outs = pl.pallas_call(
        functools.partial(forward_kernel, tick, rows, length, hidden, len(held) + len(lefts), count),
        out_shape=[
            jax.ShapeDtypeStruct((rows, width), F32),
            jax.ShapeDtypeStruct((rows, width), BF),
        ]
        + vmem_like(weights)
        + [pltpu.VMEM(stash_shape(rows, hidden), BF), pltpu.VMEM((2, 2, rows, width), F32)]
        + [pltpu.HBM((2, rows, width), BF)] * len(LEFTS),
        in_specs=[pl.BlockSpec(memory_space=pltpu.SMEM)]
        + [vmem()] * (4 + count + len(held))
        + [pl.BlockSpec(memory_space=pltpu.HBM)] * len(lefts),
        out_specs=[vmem()] * (4 + len(weights)) + [pl.BlockSpec(memory_space=pltpu.HBM)] * len(LEFTS),
        scratch_shapes=[
            pltpu.VMEM((len(LEFTS), 2, rows, width), BF),
            pltpu.SemaphoreType.DMA((len(LEFTS), 2)),
        ],
        input_output_aliases={5 + count + i: 2 + i for i in range(len(held) + len(lefts))},
        compiler_params=pltpu.CompilerParams(vmem_limit_bytes=16 * MEGA),
        name="forward_pass",
    )(section, *resident((*gains, *tables, *x, *held)), *pinned(lefts))
    first = 2 + len(weights)
    return outs[0], outs[1], outs[2:first], outs[first : first + 2], outs[first + 2 :]


SLOPES = {"branch": QUERY, "attend": JOINED, "first": QUERY, "second": QUERY}
SLOPES_WIDTH = sum(-(-width // LANES) * LANES for width in SLOPES.values())


def backward_kernel(tick, rows, length, hidden, old, count, saves, section, gain_one, gain_two, cosine, sine, *rest):
    slope_in, rest = rest[:count], rest[count:]
    (wot, wqkvt, wide, tall, stash, sums), rest = rest[:6], rest[6 + old :]
    entering, leaving, _, _, _, _, made, mixer_out, *far, vot, vqkvt, mixers, sems, mixer_sems, far_sems = rest
    near = (stash, sums, made)
    saving = [pltpu.make_async_copy(near[i], far[i], far_sems.at[i]) for i in range(2)] if saves else []
    sending = [
        pltpu.make_async_copy(made.at[app], far[2].at[app], far_sems.at[2 + app]) for app in range(2) if saves
    ]
    width = entering.shape[1]
    if saves:
        _, _, vdt = halves(wide, width, width, width)
        _, vgt, vut, _ = halves(tall, hidden, hidden, hidden, width)
    else:
        vdt, (vgt, vut) = wide, halves(tall, hidden, hidden)
    piece = hidden // PIECES

    @pl.when(section[0] == tick)
    def run():
        lanes = lane_index(rows)
        lower = lanes < HEAD
        first_half = lax.rem(lanes, HEAD) < HEAD // 2
        cos, sin = cosine[...], sine[...]
        copies = [
            pltpu.make_async_copy(wot, vot, sems.at[0]),
            pltpu.make_async_copy(wqkvt, vqkvt, sems.at[1]),
        ]
        for copy in copies:
            copy.start()
        slope = assembled(slope_in).astype(F32)
        writes = []
        for app in (1, 0):
            if app == 0:
                for copy in saving + sending[1:]:
                    copy.start()
            get, _ = views(stash, stash_widths(hidden), app)
            _, put = views(made, SLOPES, app)
            mixer = slope.astype(BF)
            mixers[app] = mixer
            writes.append(pltpu.make_async_copy(mixers.at[app], mixer_out.at[app], mixer_sems.at[app]))
            writes[-1].start()
            back = None
            for i in range(PIECES):
                cols = slice(i * piece, (i + 1) * piece)
                active = dot(mixer, vdt[:, cols])
                gate = (active * get("gate_factor", i * piece, (i + 1) * piece).astype(F32)).astype(BF)
                up = (active * get("up_factor", i * piece, (i + 1) * piece).astype(F32)).astype(BF)
                part = dot(gate, vgt[cols]) + dot(up, vut[cols])
                back = part if back is None else back + part
            middle = sums[1, app]
            scale = mean_scale(middle)
            shaped = back * gain_two[...]
            inner = jnp.mean(shaped * middle, axis=-1, keepdims=True)
            put("second", (back * middle * scale).astype(BF))
            middle_slope = slope + scale * shaped - middle * (scale * scale * scale * inner)
            branch = middle_slope.astype(BF)
            put("branch", branch)
            if app == 1:
                copies[0].wait()
            context_slope = dot(branch, vot[...])
            query_back, key_back, value_back = [], {}, {}

            def operand(name, c):
                sides = range(len(chunk_heads(c)))
                places = [2 * c + side if name == "chances" else 2 * group_of(2 * c + side) + side for side in sides]
                return jnp.concatenate([get(name, place * LANES, (place + 1) * LANES) for place in places], axis=0)

            rounded = [context_slope[:, c * LANES : (c + 1) * LANES].astype(BF) for c in range(CHUNKS)]
            all_slopes = [dot_last(operand("values", c), rounded[c]) for c in range(CHUNKS)]
            all_chances = [operand("chances", c) for c in range(CHUNKS)]
            value_parts = [dot(all_chances[c], rounded[c]) for c in range(CHUNKS)]
            all_scores = []
            for c in range(CHUNKS):
                scores = []
                for side in range(len(chunk_heads(c))):
                    band = slice(side * rows, (side + 1) * rows)
                    chance, chance_slope = all_chances[c][band].astype(F32), all_slopes[c][band]
                    inner = jnp.sum(chance * chance_slope, axis=0, keepdims=True)
                    scores.append((chance * (chance_slope - inner)).astype(BF))
                all_scores.append(jnp.concatenate(scores, axis=0))
            key_parts = [dot(all_scores[c], get("query", c * LANES, (c + 1) * LANES)) for c in range(CHUNKS)]
            query_back = [dot_first(all_scores[c], operand("keys", c)) for c in range(CHUNKS)]
            for c in range(CHUNKS):
                key_part, value_part = key_parts[c], value_parts[c]
                for head in chunk_heads(c):
                    side, group = head % 2, group_of(head)
                    band = slice(side * rows, (side + 1) * rows)
                    for store, part in ((key_back, key_part), (value_back, value_part)):
                        item = part[band]
                        store[group, side] = store[group, side] + item if (group, side) in store else item

            def gathered(store, group, up_half):
                low, high = store[group, 0], store[group, 1]
                if up_half:
                    return pltpu.roll(low, HEAD, 1) + high
                return low + pltpu.roll(high, HEAD, 1)

            chunks = query_back + [None] * (JOINED // LANES - CHUNKS)
            for store, start in ((key_back, QUERY), (value_back, QUERY + PAIR)):
                for group in range(KV_HEADS):
                    at, offset = divmod(start + group * HEAD, LANES)
                    item = gathered(store, group, offset > 0)
                    if offset == 0:
                        chunks[at] = jnp.where(lower, item, 0.0)
                    else:
                        chunks[at] = jnp.where(lower, chunks[at], item)
            for i in range((QUERY + PAIR) // LANES):
                chunks[i] = (chunks[i] * cos - half_turned(chunks[i], first_half) * sin) * HEAD ** (-0.5)
            attend = jnp.concatenate([chunk.astype(BF) for chunk in chunks], axis=1)
            put("attend", attend)
            if app == 1:
                copies[1].wait()
            back = dot(attend, vqkvt[...])
            residual = sums[0, app]
            scale = mean_scale(residual)
            shaped = back * gain_one[...]
            inner = jnp.mean(shaped * residual, axis=-1, keepdims=True)
            put("first", (back * residual * scale).astype(BF))
            slope = middle_slope + scale * shaped - residual * (scale * scale * scale * inner)
        entering[...] = slope
        leaving[...] = slope.astype(BF)
        for write in writes:
            write.wait()

    @pl.when(section[0] != tick)
    def save():
        for copy in saving + sending[1:]:
            copy.start()

    for copy in sending[:1]:
        copy.start()
    for copy in saving + sending:
        copy.wait()


def backward_pass(tick, section, slope, gains, tables, stash, streamed, weights, made, mixers, length, hidden, saves):
    rows, width = slope[0].shape[0], weights[1].shape[1]
    held = [*weights, *stash, *made]
    count = len(slope)
    outs = pl.pallas_call(
        functools.partial(backward_kernel, tick, rows, length, hidden, len(made) + len(mixers), count, saves),
        out_shape=[
            jax.ShapeDtypeStruct((rows, width), F32),
            jax.ShapeDtypeStruct((rows, width), BF),
        ]
        + vmem_like([*weights, *stash])
        + [pltpu.VMEM((2, rows, SLOPES_WIDTH), BF), pltpu.HBM((2, rows, width), BF)]
        + (
            [pltpu.HBM(array.shape, array.dtype) for array in stash] + [pltpu.HBM((2, rows, SLOPES_WIDTH), BF)]
            if saves
            else []
        ),
        in_specs=[pl.BlockSpec(memory_space=pltpu.SMEM)]
        + [vmem()] * (4 + count)
        + [pl.BlockSpec(memory_space=pltpu.HBM)] * 2
        + [vmem()] * len(held)
        + [pl.BlockSpec(memory_space=pltpu.HBM)] * len(mixers),
        out_specs=[vmem()] * 7 + [pl.BlockSpec(memory_space=pltpu.HBM)] * (4 if saves else 1),
        scratch_shapes=[pltpu.VMEM(w.shape, BF) for w in streamed]
        + [pltpu.VMEM((2, rows, width), BF)]
        + [pltpu.SemaphoreType.DMA((2,))] * 2
        + [pltpu.SemaphoreType.DMA((4,))],
        input_output_aliases={7 + count + i: 2 + i for i in range(len(held) + len(mixers))},
        compiler_params=pltpu.CompilerParams(vmem_limit_bytes=16 * MEGA),
        name="backward_pass",
    )(section, *resident((*gains, *tables, *slope)), *pinned(streamed), *resident(held), *pinned(mixers))
    return outs[0], outs[1], outs[2:4], outs[4:6], outs[6:7], outs[7:8], outs[8:]


def turn(source, target, row=0, column=0):
    depth, width = source.shape
    for start in range(0, width, LANES):
        stop = min(start + LANES, width)
        target[row + start : row + stop, column : column + depth] = source[:, start:stop].T


def load_kernel(wq, wkt, wvt, wo, wg, wu, wdt, wide, tall, vqkv, wqkvt, sq, vqkvt, sems, out_sem):
    width, pair = wq.shape[0], wkt.shape[0]
    vg, vu, vdt = halves(wide, width, width, width)
    vd, _, _, vo = halves(tall, *[wg.shape[1]] * 3, width)
    copies = [
        pltpu.make_async_copy(source, target, sems.at[i])
        for i, (source, target) in enumerate(
            (
                (wq, sq),
                (wkt, vqkvt.at[pl.ds(width, pair)]),
                (wvt, vqkvt.at[pl.ds(width + pair, pair)]),
                (wdt, vdt),
                (wo, vo),
                (wg, vg),
                (wu, vu),
            )
        )
    ]
    for copy in copies:
        copy.start()
    vqkvt[width + 2 * pair :] = jnp.zeros((HEAD, width), BF)
    for copy in copies[:3]:
        copy.wait()
    vqkv[:, :width] = sq[...]
    vqkv[:, width:] = vqkvt[width:, :].T
    turn(sq, vqkvt)
    out = pltpu.make_async_copy(vqkvt, wqkvt, out_sem)
    out.start()
    copies[3].wait()
    turn(vdt, vd)
    for copy in copies[4:]:
        copy.wait()
    out.wait()


def load(wq, wkt, wvt, wo, wg, wu, wdt):
    width, hidden = wg.shape
    *weights, joined_back = pl.pallas_call(
        load_kernel,
        out_shape=[
            pltpu.VMEM((3 * width, hidden), BF),
            pltpu.VMEM((3 * hidden + width, width), BF),
            pltpu.VMEM((width, JOINED), BF),
            pltpu.HBM((JOINED, width), BF),
        ],
        in_specs=[pl.BlockSpec(memory_space=pltpu.HBM)] * 7,
        out_specs=[vmem()] * 3 + [pl.BlockSpec(memory_space=pltpu.HBM)],
        scratch_shapes=[
            pltpu.VMEM(wq.shape, BF),
            pltpu.VMEM((JOINED, width), BF),
            pltpu.SemaphoreType.DMA((7,)),
            pltpu.SemaphoreType.DMA,
        ],
        compiler_params=pltpu.CompilerParams(vmem_limit_bytes=16 * MEGA),
        name="load_weights",
    )(*pinned((wq, wkt, wvt, wo, wg, wu, wdt)))
    return weights, joined_back


def turn_kernel(wide, tall, wide_out, tall_out, wot, wback, vot, sems):
    hidden, width = wide.shape[1], tall.shape[1]
    vg, vu, _ = halves(wide, width, width, width)
    _, vgt, vut, vo = halves(tall, hidden, hidden, hidden, width)
    copies = [
        pltpu.make_async_copy(source, target, sems.at[i])
        for i, (source, target) in enumerate(zip((vot, vgt, vut), [wot] + halves(wback, hidden, hidden)))
    ]
    vot[:, :width] = vo[...].T
    vot[:, width:] = jnp.zeros((width, HEAD), BF)
    copies[0].start()
    for source, target, copy in zip((vg, vu), (vgt, vut), copies[1:]):
        turn(source, target)
        copy.start()
    for copy in copies:
        copy.wait()


def turned(wide, tall):
    hidden, width = wide.shape[1], tall.shape[1]
    back = (2 * hidden, width)
    return pl.pallas_call(
        turn_kernel,
        out_shape=vmem_like((wide, tall))
        + [pltpu.HBM((width, CHUNKS * LANES), BF), pltpu.HBM(back, BF)],
        in_specs=[vmem()] * 2,
        out_specs=[vmem()] * 2 + [pl.BlockSpec(memory_space=pltpu.HBM)] * 2,
        scratch_shapes=[
            pltpu.VMEM((width, CHUNKS * LANES), BF),
            pltpu.SemaphoreType.DMA((3,)),
        ],
        input_output_aliases={0: 0, 1: 1},
        compiler_params=pltpu.CompilerParams(vmem_limit_bytes=16 * MEGA),
        name="turn_weights",
    )(*resident((wide, tall)))


def moved_kernel(count, *refs):
    copies = [
        pltpu.make_async_copy(refs[i], refs[count + i], refs[-1].at[i]) for i in range(count)
    ]
    for copy in copies:
        copy.start()
    for copy in copies:
        copy.wait()


def moved(arrays, inward):
    count = len(arrays)
    near, far = (vmem(), pltpu.VMEM), (pl.BlockSpec(memory_space=pltpu.HBM), pltpu.HBM)
    (source, _), (target, place) = (far, near) if inward else (near, far)
    return pl.pallas_call(
        functools.partial(moved_kernel, count),
        out_shape=[place(array.shape, array.dtype) for array in arrays],
        in_specs=[source] * count,
        out_specs=[target] * count,
        scratch_shapes=[pltpu.SemaphoreType.DMA((count,))],
        compiler_params=pltpu.CompilerParams(vmem_limit_bytes=16 * MEGA),
        cost_estimate=pl.CostEstimate(
            flops=0, bytes_accessed=2 * sum(array.size * array.dtype.itemsize for array in arrays), transcendentals=0
        ),
        name="restored" if inward else "saved",
    )(*(pinned if inward else resident)(arrays))


def parts_kernel(normed, context, made, out, stage, sems):
    rows = normed.shape[0] * normed.shape[1]
    edge = QUERY + 2 * PAIR
    gets = [views(made, SLOPES, app)[0] for app in range(2)]
    attend, branch, first, second = (
        jnp.concatenate([get(name) for get in gets], axis=0) for name in ("attend", "branch", "first", "second")
    )

    def flat(ref):
        return ref[...].reshape(rows, ref.shape[2])

    half = 6 * LANES
    bounds = (0, half, JOINED, stage.shape[1])
    copies = [
        pltpu.make_async_copy(stage.at[:, pl.ds(low, high - low)], out.at[:, pl.ds(low, high - low)], sems.at[i])
        for i, (low, high) in enumerate(zip(bounds[:-1], bounds[1:]))
    ]
    left, right = flat(normed), attend
    stage[:, :half] = dot_first(left, right[:, :half]).astype(BF)
    copies[0].start()
    stage[:, half:JOINED] = dot_first(left, right[:, half:]).astype(BF)
    lanes = lax.broadcasted_iota(jnp.int32, (rows, HEAD), 1)
    gains = dot_first(first, (lanes == 0).astype(BF)) + dot_first(second, (lanes == 1).astype(BF))
    stage[:, edge:JOINED] = gains.astype(BF)
    copies[1].start()
    stage[:, JOINED : JOINED + QUERY] = dot_first(flat(context), branch).astype(BF)
    stage[:, JOINED + QUERY :] = jnp.zeros((QUERY, HEAD), BF)
    copies[2].start()
    for copy in copies:
        copy.wait()


def parts(normed, context, made):
    shape = (QUERY, JOINED + QUERY + HEAD)
    return pl.pallas_call(
        parts_kernel,
        out_shape=pltpu.HBM(shape, BF),
        in_specs=[vmem()] * 3,
        out_specs=pl.BlockSpec(memory_space=pltpu.HBM),
        scratch_shapes=[pltpu.VMEM(shape, BF), pltpu.SemaphoreType.DMA((3,))],
        compiler_params=pltpu.CompilerParams(vmem_limit_bytes=16 * MEGA),
        cost_estimate=pl.CostEstimate(flops=4 * shape[0] * shape[1] * normed.shape[0] * normed.shape[1], bytes_accessed=4 * shape[0] * shape[1], transcendentals=0),
        name="attention_parts",
    )(*resident((normed, context, made)))


def factors_kernel(second, wg, wu, gate_factor, up_factor, active):
    step = 256
    for i in range(second.shape[0] // step):
        band = slice(i * step, (i + 1) * step)
        block = second[band]
        gate = dot(block, wg[...])
        up = dot(block, wu[...])
        sigma = jax.nn.sigmoid(gate)
        linear = gate * sigma
        gate_factor[band] = (up * (sigma + linear * (1.0 - sigma))).astype(BF)
        up_factor[band] = linear.astype(BF)
        active[band] = (linear * up).astype(BF)


def factors(second, wg, wu):
    rows, width = second.shape
    hidden = wg.shape[1]
    block, piece = 512, 512
    wide = pl.BlockSpec((block, piece), lambda i, j: (j, i))
    weight = pl.BlockSpec((width, piece), lambda i, j: (0, i))
    return pl.pallas_call(
        factors_kernel,
        grid=(hidden // piece, rows // block),
        out_shape=[pltpu.HBM((rows, hidden), BF)] * 3,
        in_specs=[
            pl.BlockSpec((block, width), lambda i, j: (j, 0)),
            weight,
            weight,
        ],
        out_specs=[wide] * 3,
        compiler_params=pltpu.CompilerParams(vmem_limit_bytes=16 * MEGA),
        cost_estimate=pl.CostEstimate(flops=4 * rows * width * hidden, bytes_accessed=8 * rows * hidden, transcendentals=rows * hidden),
        name="feed_factors",
    )(second, wg, wu)


def feed_kernel(own, last, mixer, second, chosen, wdt, gate_factor, up_factor, active, *rest):
    earlier, (gate, up, down, squares, mine, second_own) = rest[:-6], rest[-6:]

    @pl.when(pl.program_id(0) == 0)
    def pick():
        mine[...] = dot_last(chosen[...], mixer[...]).astype(BF)
        second_own[...] = dot_last(chosen[...], second[...]).astype(BF)
        squares[...] = jnp.zeros_like(squares)

    slope = dot(mixer[...], wdt[...])
    gate_slope = (slope * gate_factor[...].astype(F32)).astype(BF)
    up_slope = (slope * up_factor[...].astype(F32)).astype(BF)
    parts = (dot(second_own[...], gate_slope), dot(second_own[...], up_slope), dot(mine[...], active[...]))
    for k, (ref, part) in enumerate(zip((gate, up, down), parts)):
        part = part[:own]
        if earlier:
            part = part + earlier[k][...]
        ref[...] = part
        if last:
            squares[...] += jnp.sum(part * part, axis=0, keepdims=True)


def feed(own, last, mixer, second, chosen, wdt, made, earlier):
    rows, width = mixer.shape
    hidden = wdt.shape[1]
    piece = 512
    whole = lambda i: (0, 0)
    column = lambda i: (0, i)
    once = pl.Buffered(1)
    result = pl.BlockSpec((own, piece), column)
    return pl.pallas_call(
        functools.partial(feed_kernel, own, last),
        grid=(hidden // piece,),
        out_shape=[jax.ShapeDtypeStruct((own, hidden), F32)] * 3 + [jax.ShapeDtypeStruct((1, piece), F32)],
        in_specs=[pl.BlockSpec((rows, width), whole, pipeline_mode=once)] * 2
        + [pl.BlockSpec(chosen.shape, whole, pipeline_mode=once), pl.BlockSpec((width, piece), column)]
        + [pl.BlockSpec((rows, piece), column)] * 3
        + [result] * len(earlier),
        out_specs=[result] * 3 + [pl.BlockSpec((1, piece), whole)],
        scratch_shapes=[pltpu.VMEM((chosen.shape[0], rows), BF)] * 2,
        compiler_params=pltpu.CompilerParams(vmem_limit_bytes=16 * MEGA),
        cost_estimate=pl.CostEstimate(
            flops=2 * (rows + 3 * own) * wdt.size, bytes_accessed=8 * rows * hidden, transcendentals=0
        ),
        name="feed_gradient",
    )(mixer, second, chosen, wdt, *made, *earlier)


def finish_kernel(terms, squares, query, key, value, output, gains, total):
    edge = QUERY + 2 * PAIR
    whole = terms[...].astype(F32)
    query[...] = whole[:, :QUERY]
    key[...] = whole[:, QUERY : QUERY + PAIR].T
    value[...] = whole[:, QUERY + PAIR : edge].T
    output[...] = whole[:, JOINED : JOINED + QUERY]
    gains[...] = whole[:, edge : edge + 2]
    sums = jnp.sum(whole * whole, axis=0, keepdims=True)
    total[...] = jnp.sum(sums, axis=1, keepdims=True) + jnp.sum(squares[...], axis=1, keepdims=True)


def finish(terms, squares):
    own = terms.shape[0]
    shapes = ((own, QUERY), (PAIR, own), (PAIR, own), (own, QUERY), (own, 2), (1, 1))
    return pl.pallas_call(
        finish_kernel,
        out_shape=[jax.ShapeDtypeStruct(shape, F32) for shape in shapes],
        in_specs=[vmem()] * 2,
        out_specs=[vmem()] * len(shapes),
        compiler_params=pltpu.CompilerParams(vmem_limit_bytes=16 * MEGA),
        name="finish",
    )(terms, squares)


def after(value, *tokens):
    return lax.optimization_barrier((value,) + tokens)[0]


def gathered_at(block, axis, target):
    count = lax.axis_size(axis)
    pieces = [block if s == target else lax.ppermute(block, axis, [(s, target)]) for s in range(count)]
    return pieces


def spread_from(whole, axis, source):
    count = lax.axis_size(axis)
    width = whole.shape[1] // count
    columns = [whole[:, s * width : (s + 1) * width] for s in range(count)]
    mine = jnp.where(lax.axis_index(axis) == source, columns[source], jnp.zeros_like(columns[source]))
    for s in range(count):
        if s != source:
            mine = mine + lax.ppermute(columns[s], axis, [(source, s)])
    return mine


class LineGather:
    def __init__(self, block, axis):
        self.axis, self.count = axis, lax.axis_size(axis)
        self.line, self.step = self.count // 2, 0
        self.held = [block] + [None] * (self.line - 1)
        self.moving = (block, block)

    def advance(self, *tokens):
        ahead = [(i, i + 2) for i in range(self.count - 2)]
        self.step += 1
        below, above = self.moving
        if tokens:
            below, above, *_ = lax.optimization_barrier((below, above, *tokens))
        below = lax.ppermute(below, self.axis, ahead)
        above = lax.ppermute(above, self.axis, [(b, a) for a, b in ahead])
        self.moving = (below, above)
        for k, item in ((self.step, below), (self.line - self.step, above)):
            self.held[k] = item if self.held[k] is None else self.held[k] + item

    def finish(self):
        while self.step < self.line - 1:
            self.advance()
        mine = jnp.concatenate(self.held)
        other = lax.ppermute(mine, self.axis, [(i, i ^ 1) for i in range(self.count)])
        bands = [slice(start, start + BAND) for start in range(0, mine.shape[0], BAND)]
        return [half[band] for half in (mine, other) for band in bands]


def summed(value, axis):
    count, distance = lax.axis_size(axis), 1
    while distance < count:
        value = value + lax.ppermute(value, axis, [(i, i ^ distance) for i in range(count)])
        distance *= 2
    return value


def per_device(
    inputs, cotangent, first_gain, w_query, w_key, w_value, w_output, second_gain, w_gate, w_up, w_down
):
    sections = lax.axis_size("section")
    replicas = lax.axis_size("dp")
    section = lax.axis_index("section")
    micro, length, part = inputs.shape
    rows, width = micro * length, part * sections
    hidden = w_gate.shape[2]
    own = width // replicas
    w_query, w_key, w_value, w_output = w_query[0], w_key[0], w_value[0], w_output[0]
    w_gate, w_up, w_down = w_gate[0], w_up[0], w_down[0]
    gains = (first_gain, second_gain)
    tables = tuple(jnp.asarray(table) for table in rotary_tables(length, rows))
    place = section.astype(jnp.int32).reshape(1)
    w_query, place = lax.optimization_barrier((w_query, place))
    own_rows = -(-own // 16) * 16
    at = lax.broadcasted_iota(jnp.int32, (own_rows, width), 0)
    chosen = jnp.logical_and(
        lax.broadcasted_iota(jnp.int32, (own_rows, width), 1) == at + own * lax.axis_index("dp"), at < own
    ).astype(BF)

    x = gathered_at(inputs.reshape(rows, part), "section", 0)
    w_down = w_down.T
    weights, joined_back = load(w_query, w_key.T, w_value.T, w_output, w_gate, w_up, w_down)
    last_slope = gathered_at(cotangent.reshape(rows, part), "section", sections - 1)

    stash = lefts = ()
    for t in range(sections):
        final, leaving, weights, stash, lefts = forward_pass(
            t, place, x, gains, tables, weights, stash, lefts, length, hidden
        )
        if t < sections - 1:
            x = [lax.ppermute(leaving, "section", [(t, t + 1)])]
        if t == 0:
            *changed, output_back, back_far = turned(*weights[:2])
            weights = [*changed, *weights[2:]]
    normed, context, second = lefts
    streamed = (output_back, joined_back)
    weights = weights[:2]

    slope = last_slope
    made = mixers = ()
    for t in reversed(range(sections)):
        entering, leaving, weights, stash, made, mixers, far = backward_pass(
            t, place, slope, gains, tables, stash, streamed, weights, made, mixers, length, hidden, t == sections - 1
        )
        if t > 0:
            slope = [lax.ppermute(leaving, "section", [(t, t - 1)])]
        if t == sections - 1:
            outputs = spread_from(after(final, leaving).astype(BF), "section", sections - 1)
        if t > 0:
            if t == sections - 1:
                second_all = lax.all_gather(after(second.reshape(2 * rows, width), far[0]), "dp", axis=0, tiled=True)
                near = moved((w_down, back_far, *far), True)
                weights, stash, made = near[:2], near[2:4], near[4:]
    slopes = made
    bands = [slice(start, start + BAND) for start in range(0, 2 * rows * replicas, BAND)]
    second_all = [second_all[band] for band in bands]
    mixer_all = lax.all_gather(mixers[0].reshape(2 * rows, width), "dp", axis=0, tiled=True)
    mixer_all = [mixer_all[band] for band in bands]
    delta_inputs = spread_from(leaving, "section", 0)
    terms = parts(normed, context, slopes[0])
    reduced = lax.psum_scatter(terms, "dp", scatter_dimension=0, tiled=True)
    made = [factors(second, w_gate, w_up) for second in second_all]
    feed_parts = ()
    for i, (mixer, second, item) in enumerate(zip(mixer_all, second_all, made)):
        last = i == len(made) - 1
        *feed_parts, squares = feed(own, last, mixer, second, chosen, w_down, item, feed_parts)
    gate, up, down = feed_parts
    query, key, value, output, gain_terms, total = finish(reduced, squares)
    total = summed(summed(total, "dp"), "section")
    return (
        outputs.astype(F32).reshape(micro, length, part),
        delta_inputs.astype(F32).reshape(micro, length, part),
        gain_terms[:, 0][None],
        query[None],
        key.T[None],
        value.T[None],
        output[None],
        gain_terms[:, 1][None],
        gate[None],
        up[None],
        down.T[None],
        jnp.sqrt(total).reshape(()),
    )


def solution(mesh):
    stacked = P("section", None, None)
    rows = P("section", "dp", None)
    return jax.shard_map(
        per_device,
        mesh=mesh,
        in_specs=(P("dp", None, "section"),) * 2
        + (P("section", None),)
        + (stacked,) * 4
        + (P("section", None),)
        + (stacked,) * 3,
        out_specs=(P("dp", None, "section"),) * 2
        + (P("section", "dp"),)
        + (rows,) * 4
        + (P("section", "dp"),)
        + (rows,) * 2
        + (P("section", None, "dp"), P()),
        check_vma=False,
    )
```

```python
import functools

import jax
import jax.numpy as jnp
import numpy as np
from jax import lax
from jax.experimental import pallas as pl
from jax.experimental.pallas import tpu as pltpu
from jax.sharding import PartitionSpec as P

HEADS = 15
KV_HEADS = 5
HEAD = 64
EPSILON = 1e-05
THETA = 10000.0
LANES = 128
PIECES = 2
BAND = 1024
BF = jnp.bfloat16
F32 = jnp.float32
QUERY = HEADS * HEAD
PAIR = KV_HEADS * HEAD
JOINED = QUERY + 2 * PAIR + HEAD
CHUNKS = (HEADS + 1) // 2
MEGA = 2**20


def dot(left, right):
    return jnp.dot(left, right, preferred_element_type=F32)


def dot_last(left, right):
    return lax.dot_general(left, right, (((1,), (1,)), ((), ())), preferred_element_type=F32)


def dot_first(left, right):
    return lax.dot_general(left, right, (((0,), (0,)), ((), ())), preferred_element_type=F32)


def rotary_tables(length, rows):
    half = HEAD // 2
    frequency = THETA ** (-(np.arange(half, dtype=np.float64) * 2.0 / HEAD))
    angles = np.arange(length, dtype=np.float64)[:, None] * frequency[None, :]
    angles = np.concatenate([angles] * (LANES // half), axis=-1)
    sign = np.where(np.arange(LANES) % HEAD < half, -1.0, 1.0)
    copies = (rows // length, 1)
    return (
        np.tile(np.cos(angles), copies).astype(np.float32),
        np.tile(np.sin(angles) * sign, copies).astype(np.float32),
    )


def lane_index(rows):
    return lax.broadcasted_iota(jnp.int32, (rows, LANES), 1)


def half_turned(chunk, first_half):
    return jnp.where(first_half, pltpu.roll(chunk, LANES - HEAD // 2, 1), pltpu.roll(chunk, HEAD // 2, 1))


def mean_scale(residual):
    return lax.rsqrt(jnp.mean(residual * residual, axis=-1, keepdims=True) + EPSILON)


def group_of(head):
    return head // (HEADS // KV_HEADS)


def chunk_heads(chunk):
    return [head for head in (2 * chunk, 2 * chunk + 1) if head < HEADS]


def spread_groups(chunks, first_lane, lower):
    low, high = {}, {}
    for group in range(KV_HEADS):
        column = first_lane + group * HEAD
        chunk = chunks[column // LANES]
        swapped = pltpu.roll(chunk, HEAD, 1)
        here, there = (chunk, swapped) if column % LANES == 0 else (swapped, chunk)
        low[group] = jnp.where(lower, here, 0.0).astype(BF)
        high[group] = jnp.where(lower, 0.0, there).astype(BF)
    return low, high


def chunk_operand(spread, chunk):
    return [spread[head % 2][group_of(head)] for head in chunk_heads(chunk)]


LEFTS = ("normed", "context", "second")


def halves(ref, *sizes):
    starts = [sum(sizes[:i]) for i in range(len(sizes))]
    return [ref.at[pl.ds(start, size)] for start, size in zip(starts, sizes)]


def stash_widths(hidden):
    return {
        "query": CHUNKS * LANES,
        "keys": KV_HEADS * 2 * LANES,
        "values": KV_HEADS * 2 * LANES,
        "chances": CHUNKS * 2 * LANES,
        "gate_factor": hidden,
        "up_factor": hidden,
    }


def stash_shape(rows, hidden):
    return (2, rows, sum(stash_widths(hidden).values()))


def views(ref, widths, app):
    starts, start = {}, 0
    for name, width in widths.items():
        starts[name] = start
        start += -(-width // LANES) * LANES

    def get(name, low=0, high=None):
        high = widths[name] if high is None else high
        return ref[app, :, starts[name] + low : starts[name] + high]

    def put(name, value, low=0):
        ref[app, :, starts[name] + low : starts[name] + low + value.shape[1]] = value

    return get, put


def assembled(pieces):
    return jnp.concatenate([piece[...] for piece in pieces], axis=1)


def forward_kernel(tick, rows, length, hidden, old, count, section, gain_one, gain_two, cosine, sine, *rest):
    x, rest = rest[:count], rest[count:]
    (wide, tall, vqkv), leaving = rest[:3], rest[old]
    stash, sums, *left_out, left, left_sems = rest[-7:]
    width = leaving.shape[1]
    vg, vu, _ = halves(wide, width, width, width)
    vd, _, _, vo = halves(tall, hidden, hidden, hidden, width)
    piece = hidden // PIECES

    @pl.when(section[0] == tick)
    def run():
        lanes = lane_index(rows)
        lower = lanes < HEAD
        first_half = lax.rem(lanes, HEAD) < HEAD // 2
        token = lax.broadcasted_iota(jnp.int32, (rows, rows), 0)
        other = lax.broadcasted_iota(jnp.int32, (rows, rows), 1)
        seen = jnp.logical_and(token <= other, lax.div(other, length) == lax.div(token, length))
        cos, sin = cosine[...], sine[...]
        residual = assembled(x).astype(F32)
        writes = []
        for app in range(2):
            def give(name, value, app=app):
                i = LEFTS.index(name)
                left[i, app] = value
                write = pltpu.make_async_copy(left.at[i, app], left_out[i].at[app], left_sems.at[i, app])
                write.start()
                writes.append(write)

            get, put = views(stash, stash_widths(hidden), app)
            sums[0, app] = residual
            normed = (residual * mean_scale(residual) * gain_one[...]).astype(BF)
            give("normed", normed)
            joined = dot(normed, vqkv[...])
            chunks = [joined[:, i * LANES : (i + 1) * LANES] for i in range(JOINED // LANES)]
            turned = (QUERY + PAIR) // LANES
            for i in range(turned):
                chunks[i] = chunks[i] * cos + half_turned(chunks[i], first_half) * sin
            queries = [chunk.astype(BF) for chunk in chunks[:CHUNKS]]
            keys = spread_groups(chunks, QUERY, lower)
            values = spread_groups(chunks, QUERY + PAIR, lower)
            for name, (low, high) in (("keys", keys), ("values", values)):
                for group in range(KV_HEADS):
                    at = 2 * group * LANES
                    put(name, low[group], at)
                    put(name, high[group], at + LANES)
            key_sides = [jnp.concatenate(chunk_operand(keys, c), axis=0) for c in range(CHUNKS)]
            value_sides = [jnp.concatenate(chunk_operand(values, c), axis=0) for c in range(CHUNKS)]
            all_scores = [dot_last(key_sides[c], queries[c]) for c in range(CHUNKS)]
            all_chances = []
            for c in range(CHUNKS):
                put("query", queries[c], c * LANES)
                parts = []
                for side in range(len(chunk_heads(c))):
                    at = (2 * c + side) * LANES
                    scores = all_scores[c][side * rows : (side + 1) * rows] * HEAD ** (-0.5)
                    scores = jnp.where(seen, scores, -1e30)
                    highest = jnp.max(scores, axis=0, keepdims=True)
                    powers = jnp.exp(scores - highest)
                    total = jnp.sum(powers, axis=0, keepdims=True)
                    parts.append((powers * (1.0 / total)).astype(BF))
                    put("chances", parts[side], at)
                all_chances.append(jnp.concatenate(parts, axis=0))
            contexts = [dot_first(all_chances[c], value_sides[c]).astype(BF) for c in range(CHUNKS)]
            context = jnp.concatenate(contexts, axis=1)[:, :QUERY]
            give("context", context)
            middle = residual + dot(context, vo[...])
            sums[1, app] = middle
            second = (middle * mean_scale(middle) * gain_two[...]).astype(BF)
            give("second", second)
            total = middle
            for i in range(PIECES):
                cols = slice(i * piece, (i + 1) * piece)
                gate = dot(second, vg[:, cols])
                up = dot(second, vu[:, cols])
                sigma = jax.nn.sigmoid(gate)
                linear = gate * sigma
                put("gate_factor", (up * (sigma + linear * (1.0 - sigma))).astype(BF), i * piece)
                put("up_factor", linear.astype(BF), i * piece)
                total = total + dot((linear * up).astype(BF), vd[cols])
            residual = total
        leaving[...] = residual.astype(BF)
        for write in writes:
            write.wait()


def vmem():
    return pl.BlockSpec(memory_space=pltpu.VMEM)


def anywhere():
    return pl.BlockSpec(memory_space=pl.ANY)


def pinned(arrays):
    return [pltpu.with_memory_space_constraint(array, pltpu.HBM) for array in arrays]


def resident(arrays):
    return [pltpu.with_memory_space_constraint(array, pltpu.VMEM) for array in arrays]


def vmem_like(arrays):
    return [pltpu.VMEM(array.shape, array.dtype) for array in arrays]


def forward_pass(tick, section, x, gains, tables, weights, stash, lefts, length, hidden):
    rows, width = x[0].shape[0], weights[1].shape[1]
    held = [*weights, *stash]
    count = len(x)
    outs = pl.pallas_call(
        functools.partial(forward_kernel, tick, rows, length, hidden, len(held) + len(lefts), count),
        out_shape=[pltpu.VMEM((rows, width), BF)]
        + vmem_like(weights)
        + [pltpu.VMEM(stash_shape(rows, hidden), BF), pltpu.VMEM((2, 2, rows, width), F32)]
        + [pltpu.HBM((2, rows, width), BF)] * len(LEFTS),
        in_specs=[pl.BlockSpec(memory_space=pltpu.SMEM)]
        + [vmem()] * (4 + count + len(held))
        + [pl.BlockSpec(memory_space=pltpu.HBM)] * len(lefts),
        out_specs=[vmem()] * (3 + len(weights)) + [pl.BlockSpec(memory_space=pltpu.HBM)] * len(LEFTS),
        scratch_shapes=[
            pltpu.VMEM((len(LEFTS), 2, rows, width), BF),
            pltpu.SemaphoreType.DMA((len(LEFTS), 2)),
        ],
        input_output_aliases={5 + count + i: 1 + i for i in range(len(held) + len(lefts))},
        compiler_params=pltpu.CompilerParams(vmem_limit_bytes=16 * MEGA),
        name="forward_pass",
    )(section, *resident((*gains, *tables, *x, *held)), *pinned(lefts))
    first = 1 + len(weights)
    return outs[0], outs[1:first], outs[first : first + 2], outs[first + 2 :]


SLOPES = {"branch": QUERY, "attend": JOINED, "first": QUERY, "second": QUERY}
SLOPES_WIDTH = sum(-(-width // LANES) * LANES for width in SLOPES.values())


def backward_kernel(tick, rows, length, hidden, old, count, saves, section, gain_one, gain_two, cosine, sine, *rest):
    slope_in, rest = rest[:count], rest[count:]
    (wot, wqkvt, wide, tall, stash, sums), rest = rest[:6], rest[6 + old :]
    leaving, _, _, _, _, made, mixer_out, *far, vot, vqkvt, mixers, sems, mixer_sems, far_sems = rest
    near = (stash, sums, made)
    saving = [pltpu.make_async_copy(near[i], far[i], far_sems.at[i]) for i in range(2)] if saves else []
    sending = [
        pltpu.make_async_copy(made.at[app], far[2].at[app], far_sems.at[2 + app]) for app in range(2) if saves
    ]
    width = leaving.shape[1]
    if saves:
        _, _, vdt = halves(wide, width, width, width)
        _, vgt, vut, _ = halves(tall, hidden, hidden, hidden, width)
    else:
        vdt, (vgt, vut) = wide, halves(tall, hidden, hidden)
    piece = hidden // PIECES

    @pl.when(section[0] == tick)
    def run():
        lanes = lane_index(rows)
        lower = lanes < HEAD
        first_half = lax.rem(lanes, HEAD) < HEAD // 2
        cos, sin = cosine[...], sine[...]
        copies = [
            pltpu.make_async_copy(wot, vot, sems.at[0]),
            pltpu.make_async_copy(wqkvt, vqkvt, sems.at[1]),
        ]
        for copy in copies:
            copy.start()
        slope = assembled(slope_in).astype(F32)
        writes = []
        for app in (1, 0):
            if app == 0:
                for copy in saving + sending[1:]:
                    copy.start()
            get, _ = views(stash, stash_widths(hidden), app)
            _, put = views(made, SLOPES, app)
            mixer = slope.astype(BF)
            mixers[app] = mixer
            writes.append(pltpu.make_async_copy(mixers.at[app], mixer_out.at[app], mixer_sems.at[app]))
            writes[-1].start()
            back = None
            for i in range(PIECES):
                cols = slice(i * piece, (i + 1) * piece)
                active = dot(mixer, vdt[:, cols])
                gate = (active * get("gate_factor", i * piece, (i + 1) * piece).astype(F32)).astype(BF)
                up = (active * get("up_factor", i * piece, (i + 1) * piece).astype(F32)).astype(BF)
                part = dot(gate, vgt[cols]) + dot(up, vut[cols])
                back = part if back is None else back + part
            middle = sums[1, app]
            scale = mean_scale(middle)
            shaped = back * gain_two[...]
            inner = jnp.mean(shaped * middle, axis=-1, keepdims=True)
            put("second", (back * middle * scale).astype(BF))
            middle_slope = slope + scale * shaped - middle * (scale * scale * scale * inner)
            branch = middle_slope.astype(BF)
            put("branch", branch)
            if app == 1:
                copies[0].wait()
            context_slope = dot(branch, vot[...])
            query_back, key_back, value_back = [], {}, {}

            def operand(name, c):
                sides = range(len(chunk_heads(c)))
                places = [2 * c + side if name == "chances" else 2 * group_of(2 * c + side) + side for side in sides]
                return jnp.concatenate([get(name, place * LANES, (place + 1) * LANES) for place in places], axis=0)

            rounded = [context_slope[:, c * LANES : (c + 1) * LANES].astype(BF) for c in range(CHUNKS)]
            all_slopes = [dot_last(operand("values", c), rounded[c]) for c in range(CHUNKS)]
            all_chances = [operand("chances", c) for c in range(CHUNKS)]
            value_parts = [dot(all_chances[c], rounded[c]) for c in range(CHUNKS)]
            all_scores = []
            for c in range(CHUNKS):
                scores = []
                for side in range(len(chunk_heads(c))):
                    band = slice(side * rows, (side + 1) * rows)
                    chance, chance_slope = all_chances[c][band].astype(F32), all_slopes[c][band]
                    inner = jnp.sum(chance * chance_slope, axis=0, keepdims=True)
                    scores.append((chance * (chance_slope - inner)).astype(BF))
                all_scores.append(jnp.concatenate(scores, axis=0))
            key_parts = [dot(all_scores[c], get("query", c * LANES, (c + 1) * LANES)) for c in range(CHUNKS)]
            query_back = [dot_first(all_scores[c], operand("keys", c)) for c in range(CHUNKS)]
            for c in range(CHUNKS):
                key_part, value_part = key_parts[c], value_parts[c]
                for head in chunk_heads(c):
                    side, group = head % 2, group_of(head)
                    band = slice(side * rows, (side + 1) * rows)
                    for store, part in ((key_back, key_part), (value_back, value_part)):
                        item = part[band]
                        store[group, side] = store[group, side] + item if (group, side) in store else item

            def gathered(store, group, up_half):
                low, high = store[group, 0], store[group, 1]
                if up_half:
                    return pltpu.roll(low, HEAD, 1) + high
                return low + pltpu.roll(high, HEAD, 1)

            chunks = query_back + [None] * (JOINED // LANES - CHUNKS)
            for store, start in ((key_back, QUERY), (value_back, QUERY + PAIR)):
                for group in range(KV_HEADS):
                    at, offset = divmod(start + group * HEAD, LANES)
                    item = gathered(store, group, offset > 0)
                    if offset == 0:
                        chunks[at] = jnp.where(lower, item, 0.0)
                    else:
                        chunks[at] = jnp.where(lower, chunks[at], item)
            for i in range((QUERY + PAIR) // LANES):
                chunks[i] = (chunks[i] * cos - half_turned(chunks[i], first_half) * sin) * HEAD ** (-0.5)
            attend = jnp.concatenate([chunk.astype(BF) for chunk in chunks], axis=1)
            put("attend", attend)
            if app == 1:
                copies[1].wait()
            back = dot(attend, vqkvt[...])
            residual = sums[0, app]
            scale = mean_scale(residual)
            shaped = back * gain_one[...]
            inner = jnp.mean(shaped * residual, axis=-1, keepdims=True)
            put("first", (back * residual * scale).astype(BF))
            slope = middle_slope + scale * shaped - residual * (scale * scale * scale * inner)
        leaving[...] = slope.astype(BF)
        for write in writes:
            write.wait()

    @pl.when(section[0] != tick)
    def save():
        for copy in saving + sending[1:]:
            copy.start()

    for copy in sending[:1]:
        copy.start()
    for copy in saving + sending:
        copy.wait()


def backward_pass(tick, section, slope, gains, tables, stash, streamed, weights, made, mixers, length, hidden, saves):
    rows, width = slope[0].shape[0], weights[1].shape[1]
    held = [*weights, *stash, *made]
    count = len(slope)
    outs = pl.pallas_call(
        functools.partial(backward_kernel, tick, rows, length, hidden, len(made) + len(mixers), count, saves),
        out_shape=[pltpu.VMEM((rows, width), BF)]
        + vmem_like([*weights, *stash])
        + [pltpu.VMEM((2, rows, SLOPES_WIDTH), BF), pltpu.HBM((2, rows, width), BF)]
        + (
            [pltpu.HBM(array.shape, array.dtype) for array in stash] + [pltpu.HBM((2, rows, SLOPES_WIDTH), BF)]
            if saves
            else []
        ),
        in_specs=[pl.BlockSpec(memory_space=pltpu.SMEM)]
        + [vmem()] * (4 + count)
        + [pl.BlockSpec(memory_space=pltpu.HBM)] * 2
        + [vmem()] * len(held)
        + [pl.BlockSpec(memory_space=pltpu.HBM)] * len(mixers),
        out_specs=[vmem()] * 6 + [pl.BlockSpec(memory_space=pltpu.HBM)] * (4 if saves else 1),
        scratch_shapes=[pltpu.VMEM(w.shape, BF) for w in streamed]
        + [pltpu.VMEM((2, rows, width), BF)]
        + [pltpu.SemaphoreType.DMA((2,))] * 2
        + [pltpu.SemaphoreType.DMA((4,))],
        input_output_aliases={7 + count + i: 1 + i for i in range(len(held) + len(mixers))},
        compiler_params=pltpu.CompilerParams(vmem_limit_bytes=16 * MEGA),
        name="backward_pass",
    )(section, *resident((*gains, *tables, *slope)), *pinned(streamed), *resident(held), *pinned(mixers))
    return outs[0], outs[1:3], outs[3:5], outs[5:6], outs[6:7], outs[7:]


def turn(source, target, row=0, column=0):
    depth, width = source.shape
    for start in range(0, width, LANES):
        stop = min(start + LANES, width)
        target[row + start : row + stop, column : column + depth] = source[:, start:stop].T


def load_kernel(wq, wkt, wvt, wo, wg, wu, wdt, wide, tall, vqkv, sq, pairs, sems):
    width, pair = wq.shape[0], wkt.shape[0]
    vg, vu, vdt = halves(wide, width, width, width)
    vd, _, _, vo = halves(tall, *[wg.shape[1]] * 3, width)
    moves = [(wdt, vdt), (wkt, pairs.at[pl.ds(0, pair)]), (wvt, pairs.at[pl.ds(pair, pair)]), (wq, sq), (wo, vo)]
    step = width // 3
    for i in range(3):
        band = pl.ds(i * step, step)
        moves += [(wg.at[band], vg.at[band]), (wu.at[band], vu.at[band])]
    copies = [pltpu.make_async_copy(source, target, sems.at[i]) for i, (source, target) in enumerate(moves)]
    for copy in copies:
        copy.start()
    pairs[2 * pair :] = jnp.zeros((HEAD, width), BF)
    copies[0].wait()
    turn(vdt, vd)
    for copy in copies[1:4]:
        copy.wait()
    vqkv[:, :width] = sq[...]
    vqkv[:, width:] = pairs[...].T
    for copy in copies[4:]:
        copy.wait()


def load(wq, wkt, wvt, wo, wg, wu, wdt):
    width, hidden = wg.shape
    return pl.pallas_call(
        load_kernel,
        out_shape=[
            pltpu.VMEM((3 * width, hidden), BF),
            pltpu.VMEM((3 * hidden + width, width), BF),
            pltpu.VMEM((width, JOINED), BF),
        ],
        in_specs=[pl.BlockSpec(memory_space=pltpu.HBM)] * 7,
        out_specs=[vmem()] * 3,
        scratch_shapes=[
            pltpu.VMEM(wq.shape, BF),
            pltpu.VMEM((2 * PAIR + HEAD, width), BF),
            pltpu.SemaphoreType.DMA((11,)),
        ],
        compiler_params=pltpu.CompilerParams(vmem_limit_bytes=16 * MEGA),
        name="load_weights",
    )(*pinned((wq, wkt, wvt, wo, wg, wu, wdt)))


def turn_kernel(wide, tall, vqkv, wide_out, tall_out, vqkv_out, wot, wback, wqkvt, vot, vqkvt, sems):
    hidden, width = wide.shape[1], tall.shape[1]
    vg, vu, _ = halves(wide, width, width, width)
    _, vgt, vut, vo = halves(tall, hidden, hidden, hidden, width)
    copies = [
        pltpu.make_async_copy(source, target, sems.at[i])
        for i, (source, target) in enumerate(zip((vot, vgt, vut), [wot] + halves(wback, hidden, hidden)))
    ]
    vot[:, :width] = vo[...].T
    vot[:, width:] = jnp.zeros((width, HEAD), BF)
    copies[0].start()
    copies.append(pltpu.make_async_copy(vqkvt, wqkvt, sems.at[3]))
    for source, target, copy in zip((vg, vu, vqkv), (vgt, vut, vqkvt), copies[1:]):
        turn(source, target)
        copy.start()
    for copy in copies:
        copy.wait()


def turned(wide, tall, vqkv):
    hidden, width = wide.shape[1], tall.shape[1]
    back = (2 * hidden, width)
    return pl.pallas_call(
        turn_kernel,
        out_shape=vmem_like((wide, tall, vqkv))
        + [pltpu.HBM((width, CHUNKS * LANES), BF), pltpu.HBM(back, BF), pltpu.HBM((JOINED, width), BF)],
        in_specs=[vmem()] * 3,
        out_specs=[vmem()] * 3 + [pl.BlockSpec(memory_space=pltpu.HBM)] * 3,
        scratch_shapes=[
            pltpu.VMEM((width, CHUNKS * LANES), BF),
            pltpu.VMEM((JOINED, width), BF),
            pltpu.SemaphoreType.DMA((4,)),
        ],
        input_output_aliases={0: 0, 1: 1, 2: 2},
        compiler_params=pltpu.CompilerParams(vmem_limit_bytes=16 * MEGA),
        name="turn_weights",
    )(*resident((wide, tall, vqkv)))


def moved_kernel(count, *refs):
    copies = [
        pltpu.make_async_copy(refs[i], refs[count + i], refs[-1].at[i]) for i in range(count)
    ]
    for copy in copies:
        copy.start()
    for copy in copies:
        copy.wait()


def moved(arrays, inward):
    count = len(arrays)
    near, far = (vmem(), pltpu.VMEM), (pl.BlockSpec(memory_space=pltpu.HBM), pltpu.HBM)
    (source, _), (target, place) = (far, near) if inward else (near, far)
    return pl.pallas_call(
        functools.partial(moved_kernel, count),
        out_shape=[place(array.shape, array.dtype) for array in arrays],
        in_specs=[source] * count,
        out_specs=[target] * count,
        scratch_shapes=[pltpu.SemaphoreType.DMA((count,))],
        compiler_params=pltpu.CompilerParams(vmem_limit_bytes=16 * MEGA),
        cost_estimate=pl.CostEstimate(
            flops=0, bytes_accessed=2 * sum(array.size * array.dtype.itemsize for array in arrays), transcendentals=0
        ),
        name="restored" if inward else "saved",
    )(*(pinned if inward else resident)(arrays))


def parts_kernel(normed, context, made, out, stage, sems):
    rows = normed.shape[0] * normed.shape[1]
    edge = QUERY + 2 * PAIR
    gets = [views(made, SLOPES, app)[0] for app in range(2)]
    attend, branch, first, second = (
        jnp.concatenate([get(name) for get in gets], axis=0) for name in ("attend", "branch", "first", "second")
    )

    def flat(ref):
        return ref[...].reshape(rows, ref.shape[2])

    half = 6 * LANES
    bounds = (0, half, JOINED, stage.shape[1])
    copies = [
        pltpu.make_async_copy(stage.at[:, pl.ds(low, high - low)], out.at[:, pl.ds(low, high - low)], sems.at[i])
        for i, (low, high) in enumerate(zip(bounds[:-1], bounds[1:]))
    ]
    left, right = flat(normed), attend
    stage[:, :half] = dot_first(left, right[:, :half]).astype(BF)
    copies[0].start()
    stage[:, half:JOINED] = dot_first(left, right[:, half:]).astype(BF)
    lanes = lax.broadcasted_iota(jnp.int32, (rows, HEAD), 1)
    gains = dot_first(first, (lanes == 0).astype(BF)) + dot_first(second, (lanes == 1).astype(BF))
    stage[:, edge:JOINED] = gains.astype(BF)
    copies[1].start()
    stage[:, JOINED : JOINED + QUERY] = dot_first(flat(context), branch).astype(BF)
    stage[:, JOINED + QUERY :] = jnp.zeros((QUERY, HEAD), BF)
    copies[2].start()
    for copy in copies:
        copy.wait()


def parts(normed, context, made):
    shape = (QUERY, JOINED + QUERY + HEAD)
    return pl.pallas_call(
        parts_kernel,
        out_shape=pltpu.HBM(shape, BF),
        in_specs=[vmem()] * 3,
        out_specs=pl.BlockSpec(memory_space=pltpu.HBM),
        scratch_shapes=[pltpu.VMEM(shape, BF), pltpu.SemaphoreType.DMA((3,))],
        compiler_params=pltpu.CompilerParams(vmem_limit_bytes=16 * MEGA),
        cost_estimate=pl.CostEstimate(flops=4 * shape[0] * shape[1] * normed.shape[0] * normed.shape[1], bytes_accessed=4 * shape[0] * shape[1], transcendentals=0),
        name="attention_parts",
    )(*resident((normed, context, made)))


def factors_kernel(second, wg, wu, gate_factor, up_factor, active):
    step = 256
    for i in range(second.shape[0] // step):
        band = slice(i * step, (i + 1) * step)
        block = second[band]
        gate = dot(block, wg[...])
        up = dot(block, wu[...])
        sigma = jax.nn.sigmoid(gate)
        linear = gate * sigma
        gate_factor[band] = (up * (sigma + linear * (1.0 - sigma))).astype(BF)
        up_factor[band] = linear.astype(BF)
        active[band] = (linear * up).astype(BF)


def factors(second, wg, wu):
    rows, width = second.shape
    hidden = wg.shape[1]
    block, piece = 512, 512
    wide = pl.BlockSpec((block, piece), lambda i, j: (j, i))
    weight = pl.BlockSpec((width, piece), lambda i, j: (0, i))
    return pl.pallas_call(
        factors_kernel,
        grid=(hidden // piece, rows // block),
        out_shape=[pltpu.HBM((rows, hidden), BF)] * 3,
        in_specs=[
            pl.BlockSpec((block, width), lambda i, j: (j, 0)),
            weight,
            weight,
        ],
        out_specs=[wide] * 3,
        compiler_params=pltpu.CompilerParams(vmem_limit_bytes=16 * MEGA),
        cost_estimate=pl.CostEstimate(flops=4 * rows * width * hidden, bytes_accessed=8 * rows * hidden, transcendentals=rows * hidden),
        name="feed_factors",
    )(second, wg, wu)


def feed_kernel(own, last, mixer, second, chosen, wdt, gate_factor, up_factor, active, *rest):
    earlier, (gate, up, down, squares, mine, second_own) = rest[:-6], rest[-6:]

    @pl.when(pl.program_id(0) == 0)
    def pick():
        mine[...] = dot_last(chosen[...], mixer[...]).astype(BF)
        second_own[...] = dot_last(chosen[...], second[...]).astype(BF)
        squares[...] = jnp.zeros_like(squares)

    slope = dot(mixer[...], wdt[...])
    gate_slope = (slope * gate_factor[...].astype(F32)).astype(BF)
    up_slope = (slope * up_factor[...].astype(F32)).astype(BF)
    parts = (dot(second_own[...], gate_slope), dot(second_own[...], up_slope), dot(mine[...], active[...]))
    for k, (ref, part) in enumerate(zip((gate, up, down), parts)):
        part = part[:own]
        if earlier:
            part = part + earlier[k][...]
        ref[...] = part
        if last:
            squares[...] += jnp.sum(part * part, axis=0, keepdims=True)


def feed(own, last, mixer, second, chosen, wdt, made, earlier):
    rows, width = mixer.shape
    hidden = wdt.shape[1]
    piece = 512
    whole = lambda i: (0, 0)
    column = lambda i: (0, i)
    once = pl.Buffered(1)
    result = pl.BlockSpec((own, piece), column)
    return pl.pallas_call(
        functools.partial(feed_kernel, own, last),
        grid=(hidden // piece,),
        out_shape=[jax.ShapeDtypeStruct((own, hidden), F32)] * 3 + [jax.ShapeDtypeStruct((1, piece), F32)],
        in_specs=[pl.BlockSpec((rows, width), whole, pipeline_mode=once)] * 2
        + [pl.BlockSpec(chosen.shape, whole, pipeline_mode=once), pl.BlockSpec((width, piece), column)]
        + [pl.BlockSpec((rows, piece), column)] * 3
        + [result] * len(earlier),
        out_specs=[result] * 3 + [pl.BlockSpec((1, piece), whole)],
        scratch_shapes=[pltpu.VMEM((chosen.shape[0], rows), BF)] * 2,
        compiler_params=pltpu.CompilerParams(vmem_limit_bytes=16 * MEGA),
        cost_estimate=pl.CostEstimate(
            flops=2 * (rows + 3 * own) * wdt.size, bytes_accessed=8 * rows * hidden, transcendentals=0
        ),
        name="feed_gradient",
    )(mixer, second, chosen, wdt, *made, *earlier)


def finish_kernel(terms, squares, query, key, value, output, gains, total):
    edge = QUERY + 2 * PAIR
    whole = terms[...].astype(F32)
    query[...] = whole[:, :QUERY]
    key[...] = whole[:, QUERY : QUERY + PAIR].T
    value[...] = whole[:, QUERY + PAIR : edge].T
    output[...] = whole[:, JOINED : JOINED + QUERY]
    gains[...] = whole[:, edge : edge + 2]
    sums = jnp.sum(whole * whole, axis=0, keepdims=True)
    total[...] = jnp.sum(sums, axis=1, keepdims=True) + jnp.sum(squares[...], axis=1, keepdims=True)


def finish(terms, squares):
    own = terms.shape[0]
    shapes = ((own, QUERY), (PAIR, own), (PAIR, own), (own, QUERY), (own, 2), (1, 1))
    return pl.pallas_call(
        finish_kernel,
        out_shape=[jax.ShapeDtypeStruct(shape, F32) for shape in shapes],
        in_specs=[vmem()] * 2,
        out_specs=[vmem()] * len(shapes),
        compiler_params=pltpu.CompilerParams(vmem_limit_bytes=16 * MEGA),
        name="finish",
    )(terms, squares)


def after(value, *tokens):
    return lax.optimization_barrier((value,) + tokens)[0]


def gathered_at(block, axis, target):
    count = lax.axis_size(axis)
    pieces = [block if s == target else lax.ppermute(block, axis, [(s, target)]) for s in range(count)]
    return pieces


def spread_from(whole, axis, source):
    count = lax.axis_size(axis)
    width = whole.shape[1] // count
    columns = [whole[:, s * width : (s + 1) * width] for s in range(count)]
    mine = jnp.where(lax.axis_index(axis) == source, columns[source], jnp.zeros_like(columns[source]))
    for s in range(count):
        if s != source:
            mine = mine + lax.ppermute(columns[s], axis, [(source, s)])
    return mine


class LineGather:
    def __init__(self, block, axis):
        self.axis, self.count = axis, lax.axis_size(axis)
        self.line, self.step = self.count // 2, 0
        self.held = [block] + [None] * (self.line - 1)
        self.moving = (block, block)

    def advance(self, *tokens):
        ahead = [(i, i + 2) for i in range(self.count - 2)]
        self.step += 1
        below, above = self.moving
        if tokens:
            below, above, *_ = lax.optimization_barrier((below, above, *tokens))
        below = lax.ppermute(below, self.axis, ahead)
        above = lax.ppermute(above, self.axis, [(b, a) for a, b in ahead])
        self.moving = (below, above)
        for k, item in ((self.step, below), (self.line - self.step, above)):
            self.held[k] = item if self.held[k] is None else self.held[k] + item

    def finish(self):
        while self.step < self.line - 1:
            self.advance()
        mine = jnp.concatenate(self.held)
        other = lax.ppermute(mine, self.axis, [(i, i ^ 1) for i in range(self.count)])
        bands = [slice(start, start + BAND) for start in range(0, mine.shape[0], BAND)]
        return [half[band] for half in (mine, other) for band in bands]


def summed(value, axis):
    count, distance = lax.axis_size(axis), 1
    while distance < count:
        value = value + lax.ppermute(value, axis, [(i, i ^ distance) for i in range(count)])
        distance *= 2
    return value


def per_device(
    inputs, cotangent, first_gain, w_query, w_key, w_value, w_output, second_gain, w_gate, w_up, w_down
):
    sections = lax.axis_size("section")
    replicas = lax.axis_size("dp")
    section = lax.axis_index("section")
    micro, length, part = inputs.shape
    rows, width = micro * length, part * sections
    hidden = w_gate.shape[2]
    own = width // replicas
    w_query, w_key, w_value, w_output = w_query[0], w_key[0], w_value[0], w_output[0]
    w_gate, w_up, w_down = w_gate[0], w_up[0], w_down[0]
    gains = (first_gain, second_gain)
    tables = tuple(jnp.asarray(table) for table in rotary_tables(length, rows))
    place = section.astype(jnp.int32).reshape(1)
    w_query, place = lax.optimization_barrier((w_query, place))
    own_rows = -(-own // 16) * 16
    at = lax.broadcasted_iota(jnp.int32, (own_rows, width), 0)
    chosen = jnp.logical_and(
        lax.broadcasted_iota(jnp.int32, (own_rows, width), 1) == at + own * lax.axis_index("dp"), at < own
    ).astype(BF)

    x = gathered_at(inputs.reshape(rows, part), "section", 0)
    w_down = w_down.T
    weights = load(w_query, w_key.T, w_value.T, w_output, w_gate, w_up, w_down)
    last_slope = gathered_at(cotangent.reshape(rows, part), "section", sections - 1)

    stash = lefts = ()
    for t in range(sections):
        leaving, weights, stash, lefts = forward_pass(
            t, place, x, gains, tables, weights, stash, lefts, length, hidden
        )
        if t < sections - 1:
            x = [lax.ppermute(leaving, "section", [(t, t + 1)])]
        if t == 0:
            *weights, output_back, back_far, joined_back = turned(*weights)
    normed, context, second = lefts
    streamed = (output_back, joined_back)
    weights = weights[:2]

    final = leaving
    slope = last_slope
    made = mixers = ()
    for t in reversed(range(sections)):
        leaving, weights, stash, made, mixers, far = backward_pass(
            t, place, slope, gains, tables, stash, streamed, weights, made, mixers, length, hidden, t == sections - 1
        )
        if t > 0:
            slope = [lax.ppermute(leaving, "section", [(t, t - 1)])]
        if t == sections - 1:
            outputs = spread_from(after(final, leaving), "section", sections - 1)
        if t > 0:
            if t == sections - 1:
                second_all = lax.all_gather(after(second.reshape(2 * rows, width), far[0]), "dp", axis=0, tiled=True)
                near = moved((w_down, back_far, *far), True)
                weights, stash, made = near[:2], near[2:4], near[4:]
    slopes = made
    bands = [slice(start, start + BAND) for start in range(0, 2 * rows * replicas, BAND)]
    second_all = [second_all[band] for band in bands]
    mixer_all = lax.all_gather(mixers[0].reshape(2 * rows, width), "dp", axis=0, tiled=True)
    mixer_all = [mixer_all[band] for band in bands]
    delta_inputs = spread_from(leaving, "section", 0)
    terms = parts(normed, context, slopes[0])
    reduced = lax.psum_scatter(terms, "dp", scatter_dimension=0, tiled=True)
    made = [factors(second, w_gate, w_up) for second in second_all]
    feed_parts = ()
    for i, (mixer, second, item) in enumerate(zip(mixer_all, second_all, made)):
        last = i == len(made) - 1
        *feed_parts, squares = feed(own, last, mixer, second, chosen, w_down, item, feed_parts)
    gate, up, down = feed_parts
    query, key, value, output, gain_terms, total = finish(reduced, squares)
    total = summed(summed(total, "dp"), "section")
    return (
        outputs.astype(F32).reshape(micro, length, part),
        delta_inputs.astype(F32).reshape(micro, length, part),
        gain_terms[:, 0][None],
        query[None],
        key.T[None],
        value.T[None],
        output[None],
        gain_terms[:, 1][None],
        gate[None],
        up[None],
        down.T[None],
        jnp.sqrt(total).reshape(()),
    )


def solution(mesh):
    stacked = P("section", None, None)
    rows = P("section", "dp", None)
    return jax.shard_map(
        per_device,
        mesh=mesh,
        in_specs=(P("dp", None, "section"),) * 2
        + (P("section", None),)
        + (stacked,) * 4
        + (P("section", None),)
        + (stacked,) * 3,
        out_specs=(P("dp", None, "section"),) * 2
        + (P("section", "dp"),)
        + (rows,) * 4
        + (P("section", "dp"),)
        + (rows,) * 2
        + (P("section", None, "dp"), P()),
        check_vma=False,
    )
```

```python
import functools

import jax
import jax.numpy as jnp
import numpy as np
from jax import lax
from jax.experimental import pallas as pl
from jax.experimental.pallas import tpu as pltpu
from jax.sharding import PartitionSpec as P

HEADS = 15
KV_HEADS = 5
HEAD = 64
EPSILON = 1e-05
THETA = 10000.0
LANES = 128
PIECES = 2
BAND = 1024
BF = jnp.bfloat16
F32 = jnp.float32
QUERY = HEADS * HEAD
PAIR = KV_HEADS * HEAD
JOINED = QUERY + 2 * PAIR + HEAD
CHUNKS = (HEADS + 1) // 2
MEGA = 2**20


def dot(left, right):
    return jnp.dot(left, right, preferred_element_type=F32)


def dot_last(left, right):
    return lax.dot_general(left, right, (((1,), (1,)), ((), ())), preferred_element_type=F32)


def dot_first(left, right):
    return lax.dot_general(left, right, (((0,), (0,)), ((), ())), preferred_element_type=F32)


def rotary_tables(length, rows):
    half = HEAD // 2
    frequency = THETA ** (-(np.arange(half, dtype=np.float64) * 2.0 / HEAD))
    angles = np.arange(length, dtype=np.float64)[:, None] * frequency[None, :]
    angles = np.concatenate([angles] * (LANES // half), axis=-1)
    sign = np.where(np.arange(LANES) % HEAD < half, -1.0, 1.0)
    copies = (rows // length, 1)
    return (
        np.tile(np.cos(angles), copies).astype(np.float32),
        np.tile(np.sin(angles) * sign, copies).astype(np.float32),
    )


def lane_index(rows):
    return lax.broadcasted_iota(jnp.int32, (rows, LANES), 1)


def half_turned(chunk, first_half):
    return jnp.where(first_half, pltpu.roll(chunk, LANES - HEAD // 2, 1), pltpu.roll(chunk, HEAD // 2, 1))


def mean_scale(residual):
    return lax.rsqrt(jnp.mean(residual * residual, axis=-1, keepdims=True) + EPSILON)


def group_of(head):
    return head // (HEADS // KV_HEADS)


def chunk_heads(chunk):
    return [head for head in (2 * chunk, 2 * chunk + 1) if head < HEADS]


def spread_groups(chunks, first_lane, lower):
    low, high = {}, {}
    for group in range(KV_HEADS):
        column = first_lane + group * HEAD
        chunk = chunks[column // LANES]
        swapped = pltpu.roll(chunk, HEAD, 1)
        here, there = (chunk, swapped) if column % LANES == 0 else (swapped, chunk)
        low[group] = jnp.where(lower, here, 0.0).astype(BF)
        high[group] = jnp.where(lower, 0.0, there).astype(BF)
    return low, high


def chunk_operand(spread, chunk):
    return [spread[head % 2][group_of(head)] for head in chunk_heads(chunk)]


LEFTS = ("normed", "context", "second")


def halves(ref, *sizes):
    starts = [sum(sizes[:i]) for i in range(len(sizes))]
    return [ref.at[pl.ds(start, size)] for start, size in zip(starts, sizes)]


def stash_widths(hidden):
    return {
        "query": CHUNKS * LANES,
        "keys": KV_HEADS * 2 * LANES,
        "values": KV_HEADS * 2 * LANES,
        "chances": CHUNKS * 2 * LANES,
        "gate_factor": hidden,
        "up_factor": hidden,
    }


def stash_shape(rows, hidden):
    return (2, rows, sum(stash_widths(hidden).values()))


def views(ref, widths, app):
    starts, start = {}, 0
    for name, width in widths.items():
        starts[name] = start
        start += -(-width // LANES) * LANES

    def get(name, low=0, high=None):
        high = widths[name] if high is None else high
        return ref[app, :, starts[name] + low : starts[name] + high]

    def put(name, value, low=0):
        ref[app, :, starts[name] + low : starts[name] + low + value.shape[1]] = value

    return get, put


def assembled(pieces):
    return jnp.concatenate([piece[...] for piece in pieces], axis=1)


def forward_kernel(tick, rows, length, hidden, old, count, section, gain_one, gain_two, cosine, sine, *rest):
    x, rest = rest[:count], rest[count:]
    (wide, tall, vqkv), leaving = rest[:3], rest[old]
    stash, sums, *left_out, left, left_sems = rest[-7:]
    width = leaving.shape[1]
    vg, vu, _ = halves(wide, width, width, width)
    vd, _, _, vo = halves(tall, hidden, hidden, hidden, width)
    piece = hidden // PIECES

    @pl.when(section[0] == tick)
    def run():
        lanes = lane_index(rows)
        lower = lanes < HEAD
        first_half = lax.rem(lanes, HEAD) < HEAD // 2
        token = lax.broadcasted_iota(jnp.int32, (rows, rows), 0)
        other = lax.broadcasted_iota(jnp.int32, (rows, rows), 1)
        seen = jnp.logical_and(token <= other, lax.div(other, length) == lax.div(token, length))
        cos, sin = cosine[...], sine[...]
        residual = assembled(x).astype(F32)
        writes = []
        for app in range(2):
            def give(name, value, app=app):
                i = LEFTS.index(name)
                left[i, app] = value
                write = pltpu.make_async_copy(left.at[i, app], left_out[i].at[app], left_sems.at[i, app])
                write.start()
                writes.append(write)

            get, put = views(stash, stash_widths(hidden), app)
            sums[0, app] = residual
            normed = (residual * mean_scale(residual) * gain_one[...]).astype(BF)
            give("normed", normed)
            joined = dot(normed, vqkv[...])
            chunks = [joined[:, i * LANES : (i + 1) * LANES] for i in range(JOINED // LANES)]
            turned = (QUERY + PAIR) // LANES
            for i in range(turned):
                chunks[i] = chunks[i] * cos + half_turned(chunks[i], first_half) * sin
            queries = [chunk.astype(BF) for chunk in chunks[:CHUNKS]]
            keys = spread_groups(chunks, QUERY, lower)
            values = spread_groups(chunks, QUERY + PAIR, lower)
            for name, (low, high) in (("keys", keys), ("values", values)):
                for group in range(KV_HEADS):
                    at = 2 * group * LANES
                    put(name, low[group], at)
                    put(name, high[group], at + LANES)
            key_sides = [jnp.concatenate(chunk_operand(keys, c), axis=0) for c in range(CHUNKS)]
            value_sides = [jnp.concatenate(chunk_operand(values, c), axis=0) for c in range(CHUNKS)]
            all_scores = [dot_last(key_sides[c], queries[c]) for c in range(CHUNKS)]
            all_chances = []
            for c in range(CHUNKS):
                put("query", queries[c], c * LANES)
                parts = []
                for side in range(len(chunk_heads(c))):
                    at = (2 * c + side) * LANES
                    scores = all_scores[c][side * rows : (side + 1) * rows] * HEAD ** (-0.5)
                    scores = jnp.where(seen, scores, -1e30)
                    highest = jnp.max(scores, axis=0, keepdims=True)
                    powers = jnp.exp(scores - highest)
                    total = jnp.sum(powers, axis=0, keepdims=True)
                    parts.append((powers * (1.0 / total)).astype(BF))
                    put("chances", parts[side], at)
                all_chances.append(jnp.concatenate(parts, axis=0))
            contexts = [dot_first(all_chances[c], value_sides[c]).astype(BF) for c in range(CHUNKS)]
            context = jnp.concatenate(contexts, axis=1)[:, :QUERY]
            give("context", context)
            middle = residual + dot(context, vo[...])
            sums[1, app] = middle
            second = (middle * mean_scale(middle) * gain_two[...]).astype(BF)
            give("second", second)
            total = middle
            for i in range(PIECES):
                cols = slice(i * piece, (i + 1) * piece)
                gate = dot(second, vg[:, cols])
                up = dot(second, vu[:, cols])
                sigma = jax.nn.sigmoid(gate)
                linear = gate * sigma
                put("gate_factor", (up * (sigma + linear * (1.0 - sigma))).astype(BF), i * piece)
                put("up_factor", linear.astype(BF), i * piece)
                total = total + dot((linear * up).astype(BF), vd[cols])
            residual = total
        leaving[...] = residual.astype(BF)
        for write in writes:
            write.wait()


def vmem():
    return pl.BlockSpec(memory_space=pltpu.VMEM)


def anywhere():
    return pl.BlockSpec(memory_space=pl.ANY)


def pinned(arrays):
    return [pltpu.with_memory_space_constraint(array, pltpu.HBM) for array in arrays]


def resident(arrays):
    return [pltpu.with_memory_space_constraint(array, pltpu.VMEM) for array in arrays]


def vmem_like(arrays):
    return [pltpu.VMEM(array.shape, array.dtype) for array in arrays]


def forward_pass(tick, section, x, gains, tables, weights, stash, lefts, length, hidden):
    rows, width = x[0].shape[0], weights[1].shape[1]
    held = [*weights, *stash]
    count = len(x)
    outs = pl.pallas_call(
        functools.partial(forward_kernel, tick, rows, length, hidden, len(held) + len(lefts), count),
        out_shape=[pltpu.VMEM((rows, width), BF)]
        + vmem_like(weights)
        + [pltpu.VMEM(stash_shape(rows, hidden), BF), pltpu.VMEM((2, 2, rows, width), F32)]
        + [pltpu.HBM((2, rows, width), BF)] * len(LEFTS),
        in_specs=[pl.BlockSpec(memory_space=pltpu.SMEM)]
        + [vmem()] * (4 + count + len(held))
        + [pl.BlockSpec(memory_space=pltpu.HBM)] * len(lefts),
        out_specs=[vmem()] * (3 + len(weights)) + [pl.BlockSpec(memory_space=pltpu.HBM)] * len(LEFTS),
        scratch_shapes=[
            pltpu.VMEM((len(LEFTS), 2, rows, width), BF),
            pltpu.SemaphoreType.DMA((len(LEFTS), 2)),
        ],
        input_output_aliases={5 + count + i: 1 + i for i in range(len(held) + len(lefts))},
        compiler_params=pltpu.CompilerParams(vmem_limit_bytes=16 * MEGA),
        name="forward_pass",
    )(section, *resident((*gains, *tables, *x, *held)), *pinned(lefts))
    first = 1 + len(weights)
    return outs[0], outs[1:first], outs[first : first + 2], outs[first + 2 :]


SLOPES = {"branch": QUERY, "attend": JOINED, "first": QUERY, "second": QUERY}
SLOPES_WIDTH = sum(-(-width // LANES) * LANES for width in SLOPES.values())


def backward_kernel(tick, rows, length, hidden, old, count, saves, section, gain_one, gain_two, cosine, sine, *rest):
    slope_in, rest = rest[:count], rest[count:]
    (wot, wqkvt, wide, tall, stash, sums), rest = rest[:6], rest[6 + old :]
    leaving, _, _, _, _, made, mixer_out, *far, vot, vqkvt, mixers, sems, mixer_sems, far_sems = rest
    near = (stash, sums, made)
    saving = [pltpu.make_async_copy(near[i], far[i], far_sems.at[i]) for i in range(2)] if saves else []
    sending = [
        pltpu.make_async_copy(made.at[app], far[2].at[app], far_sems.at[2 + app]) for app in range(2) if saves
    ]
    width = leaving.shape[1]
    if saves:
        _, _, vdt = halves(wide, width, width, width)
        _, vgt, vut, _ = halves(tall, hidden, hidden, hidden, width)
    else:
        vdt, (vgt, vut) = wide, halves(tall, hidden, hidden)
    piece = hidden // PIECES

    @pl.when(section[0] == tick)
    def run():
        lanes = lane_index(rows)
        lower = lanes < HEAD
        first_half = lax.rem(lanes, HEAD) < HEAD // 2
        cos, sin = cosine[...], sine[...]
        copies = [
            pltpu.make_async_copy(wot, vot, sems.at[0]),
            pltpu.make_async_copy(wqkvt, vqkvt, sems.at[1]),
        ]
        for copy in copies:
            copy.start()
        slope = assembled(slope_in).astype(F32)
        writes = []
        for app in (1, 0):
            if app == 0:
                for copy in saving + sending[1:]:
                    copy.start()
            get, _ = views(stash, stash_widths(hidden), app)
            _, put = views(made, SLOPES, app)
            mixer = slope.astype(BF)
            mixers[app] = mixer
            writes.append(pltpu.make_async_copy(mixers.at[app], mixer_out.at[app], mixer_sems.at[app]))
            writes[-1].start()
            back = None
            for i in range(PIECES):
                cols = slice(i * piece, (i + 1) * piece)
                active = dot(mixer, vdt[:, cols])
                gate = (active * get("gate_factor", i * piece, (i + 1) * piece).astype(F32)).astype(BF)
                up = (active * get("up_factor", i * piece, (i + 1) * piece).astype(F32)).astype(BF)
                part = dot(gate, vgt[cols]) + dot(up, vut[cols])
                back = part if back is None else back + part
            middle = sums[1, app]
            scale = mean_scale(middle)
            shaped = back * gain_two[...]
            inner = jnp.mean(shaped * middle, axis=-1, keepdims=True)
            put("second", (back * middle * scale).astype(BF))
            middle_slope = slope + scale * shaped - middle * (scale * scale * scale * inner)
            branch = middle_slope.astype(BF)
            put("branch", branch)
            if app == 1:
                copies[0].wait()
            context_slope = dot(branch, vot[...])
            query_back, key_back, value_back = [], {}, {}

            def operand(name, c):
                sides = range(len(chunk_heads(c)))
                places = [2 * c + side if name == "chances" else 2 * group_of(2 * c + side) + side for side in sides]
                return jnp.concatenate([get(name, place * LANES, (place + 1) * LANES) for place in places], axis=0)

            rounded = [context_slope[:, c * LANES : (c + 1) * LANES].astype(BF) for c in range(CHUNKS)]
            all_slopes = [dot_last(operand("values", c), rounded[c]) for c in range(CHUNKS)]
            all_chances = [operand("chances", c) for c in range(CHUNKS)]
            value_parts = [dot(all_chances[c], rounded[c]) for c in range(CHUNKS)]
            all_scores = []
            for c in range(CHUNKS):
                scores = []
                for side in range(len(chunk_heads(c))):
                    band = slice(side * rows, (side + 1) * rows)
                    chance, chance_slope = all_chances[c][band].astype(F32), all_slopes[c][band]
                    inner = jnp.sum(chance * chance_slope, axis=0, keepdims=True)
                    scores.append((chance * (chance_slope - inner)).astype(BF))
                all_scores.append(jnp.concatenate(scores, axis=0))
            key_parts = [dot(all_scores[c], get("query", c * LANES, (c + 1) * LANES)) for c in range(CHUNKS)]
            query_back = [dot_first(all_scores[c], operand("keys", c)) for c in range(CHUNKS)]
            for c in range(CHUNKS):
                key_part, value_part = key_parts[c], value_parts[c]
                for head in chunk_heads(c):
                    side, group = head % 2, group_of(head)
                    band = slice(side * rows, (side + 1) * rows)
                    for store, part in ((key_back, key_part), (value_back, value_part)):
                        item = part[band]
                        store[group, side] = store[group, side] + item if (group, side) in store else item

            def gathered(store, group, up_half):
                low, high = store[group, 0], store[group, 1]
                if up_half:
                    return pltpu.roll(low, HEAD, 1) + high
                return low + pltpu.roll(high, HEAD, 1)

            chunks = query_back + [None] * (JOINED // LANES - CHUNKS)
            for store, start in ((key_back, QUERY), (value_back, QUERY + PAIR)):
                for group in range(KV_HEADS):
                    at, offset = divmod(start + group * HEAD, LANES)
                    item = gathered(store, group, offset > 0)
                    if offset == 0:
                        chunks[at] = jnp.where(lower, item, 0.0)
                    else:
                        chunks[at] = jnp.where(lower, chunks[at], item)
            for i in range((QUERY + PAIR) // LANES):
                chunks[i] = (chunks[i] * cos - half_turned(chunks[i], first_half) * sin) * HEAD ** (-0.5)
            attend = jnp.concatenate([chunk.astype(BF) for chunk in chunks], axis=1)
            put("attend", attend)
            if app == 1:
                copies[1].wait()
            back = dot(attend, vqkvt[...])
            residual = sums[0, app]
            scale = mean_scale(residual)
            shaped = back * gain_one[...]
            inner = jnp.mean(shaped * residual, axis=-1, keepdims=True)
            put("first", (back * residual * scale).astype(BF))
            slope = middle_slope + scale * shaped - residual * (scale * scale * scale * inner)
        leaving[...] = slope.astype(BF)
        for write in writes:
            write.wait()

    @pl.when(section[0] != tick)
    def save():
        for copy in saving + sending[1:]:
            copy.start()

    for copy in sending[:1]:
        copy.start()
    for copy in saving + sending:
        copy.wait()


def backward_pass(tick, section, slope, gains, tables, stash, streamed, weights, made, mixers, length, hidden, saves):
    rows, width = slope[0].shape[0], weights[1].shape[1]
    held = [*weights, *stash, *made]
    count = len(slope)
    outs = pl.pallas_call(
        functools.partial(backward_kernel, tick, rows, length, hidden, len(made) + len(mixers), count, saves),
        out_shape=[pltpu.VMEM((rows, width), BF)]
        + vmem_like([*weights, *stash])
        + [pltpu.VMEM((2, rows, SLOPES_WIDTH), BF), pltpu.HBM((2, rows, width), BF)]
        + (
            [pltpu.HBM(array.shape, array.dtype) for array in stash] + [pltpu.HBM((2, rows, SLOPES_WIDTH), BF)]
            if saves
            else []
        ),
        in_specs=[pl.BlockSpec(memory_space=pltpu.SMEM)]
        + [vmem()] * (4 + count)
        + [pl.BlockSpec(memory_space=pltpu.HBM)] * 2
        + [vmem()] * len(held)
        + [pl.BlockSpec(memory_space=pltpu.HBM)] * len(mixers),
        out_specs=[vmem()] * 6 + [pl.BlockSpec(memory_space=pltpu.HBM)] * (4 if saves else 1),
        scratch_shapes=[pltpu.VMEM(w.shape, BF) for w in streamed]
        + [pltpu.VMEM((2, rows, width), BF)]
        + [pltpu.SemaphoreType.DMA((2,))] * 2
        + [pltpu.SemaphoreType.DMA((4,))],
        input_output_aliases={7 + count + i: 1 + i for i in range(len(held) + len(mixers))},
        compiler_params=pltpu.CompilerParams(vmem_limit_bytes=16 * MEGA),
        name="backward_pass",
    )(section, *resident((*gains, *tables, *slope)), *pinned(streamed), *resident(held), *pinned(mixers))
    return outs[0], outs[1:3], outs[3:5], outs[5:6], outs[6:7], outs[7:]


def turn(source, target, row=0, column=0):
    depth, width = source.shape
    for start in range(0, width, LANES):
        stop = min(start + LANES, width)
        target[row + start : row + stop, column : column + depth] = source[:, start:stop].T


def load_kernel(wq, wkt, wvt, wo, wg, wu, wdt, wide, tall, vqkv, sq, pairs, sems):
    width, pair = wq.shape[0], wkt.shape[0]
    vg, vu, vdt = halves(wide, width, width, width)
    vd, _, _, vo = halves(tall, *[wg.shape[1]] * 3, width)
    moves = [(wdt, vdt), (wkt, pairs.at[pl.ds(0, pair)]), (wvt, pairs.at[pl.ds(pair, pair)]), (wq, sq), (wo, vo)]
    step = width // 3
    for i in range(3):
        band = pl.ds(i * step, step)
        moves += [(wg.at[band], vg.at[band]), (wu.at[band], vu.at[band])]
    copies = [pltpu.make_async_copy(source, target, sems.at[i]) for i, (source, target) in enumerate(moves)]
    for copy in copies:
        copy.start()
    pairs[2 * pair :] = jnp.zeros((HEAD, width), BF)
    copies[0].wait()
    turn(vdt, vd)
    for copy in copies[1:4]:
        copy.wait()
    vqkv[:, :width] = sq[...]
    vqkv[:, width:] = pairs[...].T
    for copy in copies[4:]:
        copy.wait()


def load(wq, wkt, wvt, wo, wg, wu, wdt):
    width, hidden = wg.shape
    return pl.pallas_call(
        load_kernel,
        out_shape=[
            pltpu.VMEM((3 * width, hidden), BF),
            pltpu.VMEM((3 * hidden + width, width), BF),
            pltpu.VMEM((width, JOINED), BF),
        ],
        in_specs=[pl.BlockSpec(memory_space=pltpu.HBM)] * 7,
        out_specs=[vmem()] * 3,
        scratch_shapes=[
            pltpu.VMEM(wq.shape, BF),
            pltpu.VMEM((2 * PAIR + HEAD, width), BF),
            pltpu.SemaphoreType.DMA((11,)),
        ],
        compiler_params=pltpu.CompilerParams(vmem_limit_bytes=16 * MEGA),
        name="load_weights",
    )(*pinned((wq, wkt, wvt, wo, wg, wu, wdt)))


def turn_kernel(wide, tall, vqkv, wide_out, tall_out, vqkv_out, wot, wback, wqkvt, vot, vqkvt, sems):
    hidden, width = wide.shape[1], tall.shape[1]
    vg, vu, _ = halves(wide, width, width, width)
    _, vgt, vut, vo = halves(tall, hidden, hidden, hidden, width)
    copies = [
        pltpu.make_async_copy(source, target, sems.at[i])
        for i, (source, target) in enumerate(zip((vot, vgt, vut), [wot] + halves(wback, hidden, hidden)))
    ]
    vot[:, :width] = vo[...].T
    vot[:, width:] = jnp.zeros((width, HEAD), BF)
    copies[0].start()
    copies.append(pltpu.make_async_copy(vqkvt, wqkvt, sems.at[3]))
    for source, target, copy in zip((vg, vu, vqkv), (vgt, vut, vqkvt), copies[1:]):
        turn(source, target)
        copy.start()
    for copy in copies:
        copy.wait()


def turned(wide, tall, vqkv):
    hidden, width = wide.shape[1], tall.shape[1]
    back = (2 * hidden, width)
    return pl.pallas_call(
        turn_kernel,
        out_shape=vmem_like((wide, tall, vqkv))
        + [pltpu.HBM((width, CHUNKS * LANES), BF), pltpu.HBM(back, BF), pltpu.HBM((JOINED, width), BF)],
        in_specs=[vmem()] * 3,
        out_specs=[vmem()] * 3 + [pl.BlockSpec(memory_space=pltpu.HBM)] * 3,
        scratch_shapes=[
            pltpu.VMEM((width, CHUNKS * LANES), BF),
            pltpu.VMEM((JOINED, width), BF),
            pltpu.SemaphoreType.DMA((4,)),
        ],
        input_output_aliases={0: 0, 1: 1, 2: 2},
        compiler_params=pltpu.CompilerParams(vmem_limit_bytes=16 * MEGA),
        name="turn_weights",
    )(*resident((wide, tall, vqkv)))


def moved_kernel(count, *refs):
    copies = [
        pltpu.make_async_copy(refs[i], refs[count + i], refs[-1].at[i]) for i in range(count)
    ]
    for copy in copies:
        copy.start()
    for copy in copies:
        copy.wait()


def moved(arrays, inward):
    count = len(arrays)
    near, far = (vmem(), pltpu.VMEM), (pl.BlockSpec(memory_space=pltpu.HBM), pltpu.HBM)
    (source, _), (target, place) = (far, near) if inward else (near, far)
    return pl.pallas_call(
        functools.partial(moved_kernel, count),
        out_shape=[place(array.shape, array.dtype) for array in arrays],
        in_specs=[source] * count,
        out_specs=[target] * count,
        scratch_shapes=[pltpu.SemaphoreType.DMA((count,))],
        compiler_params=pltpu.CompilerParams(vmem_limit_bytes=16 * MEGA),
        cost_estimate=pl.CostEstimate(
            flops=0, bytes_accessed=2 * sum(array.size * array.dtype.itemsize for array in arrays), transcendentals=0
        ),
        name="restored" if inward else "saved",
    )(*(pinned if inward else resident)(arrays))


def parts_kernel(normed, context, made, out, stage, sems):
    rows = normed.shape[0] * normed.shape[1]
    edge = QUERY + 2 * PAIR
    gets = [views(made, SLOPES, app)[0] for app in range(2)]
    attend, branch, first, second = (
        jnp.concatenate([get(name) for get in gets], axis=0) for name in ("attend", "branch", "first", "second")
    )

    def flat(ref):
        return ref[...].reshape(rows, ref.shape[2])

    half = 6 * LANES
    bounds = (0, half, JOINED, stage.shape[1])
    copies = [
        pltpu.make_async_copy(stage.at[:, pl.ds(low, high - low)], out.at[:, pl.ds(low, high - low)], sems.at[i])
        for i, (low, high) in enumerate(zip(bounds[:-1], bounds[1:]))
    ]
    left, right = flat(normed), attend
    stage[:, :half] = dot_first(left, right[:, :half]).astype(BF)
    copies[0].start()
    stage[:, half:JOINED] = dot_first(left, right[:, half:]).astype(BF)
    lanes = lax.broadcasted_iota(jnp.int32, (rows, HEAD), 1)
    gains = dot_first(first, (lanes == 0).astype(BF)) + dot_first(second, (lanes == 1).astype(BF))
    stage[:, edge:JOINED] = gains.astype(BF)
    copies[1].start()
    stage[:, JOINED : JOINED + QUERY] = dot_first(flat(context), branch).astype(BF)
    stage[:, JOINED + QUERY :] = jnp.zeros((QUERY, HEAD), BF)
    copies[2].start()
    for copy in copies:
        copy.wait()


def parts(normed, context, made):
    shape = (QUERY, JOINED + QUERY + HEAD)
    return pl.pallas_call(
        parts_kernel,
        out_shape=pltpu.HBM(shape, BF),
        in_specs=[vmem()] * 3,
        out_specs=pl.BlockSpec(memory_space=pltpu.HBM),
        scratch_shapes=[pltpu.VMEM(shape, BF), pltpu.SemaphoreType.DMA((3,))],
        compiler_params=pltpu.CompilerParams(vmem_limit_bytes=16 * MEGA),
        cost_estimate=pl.CostEstimate(flops=4 * shape[0] * shape[1] * normed.shape[0] * normed.shape[1], bytes_accessed=4 * shape[0] * shape[1], transcendentals=0),
        name="attention_parts",
    )(*resident((normed, context, made)))


def factors_kernel(second, wg, wu, gate_factor, up_factor, active):
    step = 256
    for i in range(second.shape[0] // step):
        band = slice(i * step, (i + 1) * step)
        block = second[band]
        gate = dot(block, wg[...])
        up = dot(block, wu[...])
        sigma = jax.nn.sigmoid(gate)
        linear = gate * sigma
        gate_factor[band] = (up * (sigma + linear * (1.0 - sigma))).astype(BF)
        up_factor[band] = linear.astype(BF)
        active[band] = (linear * up).astype(BF)


def factors(second_all, band, wg, wu):
    rows, width = BAND, second_all.shape[1]
    hidden = wg.shape[1]
    block, piece = 512, 512
    first = band * (rows // block)
    wide = pl.BlockSpec((block, piece), lambda i, j: (j, i))
    weight = pl.BlockSpec((width, piece), lambda i, j: (0, i))
    return pl.pallas_call(
        factors_kernel,
        grid=(hidden // piece, rows // block),
        out_shape=[pltpu.HBM((rows, hidden), BF)] * 3,
        in_specs=[
            pl.BlockSpec((block, width), lambda i, j: (first + j, 0)),
            weight,
            weight,
        ],
        out_specs=[wide] * 3,
        compiler_params=pltpu.CompilerParams(vmem_limit_bytes=16 * MEGA),
        cost_estimate=pl.CostEstimate(flops=4 * rows * width * hidden, bytes_accessed=8 * rows * hidden, transcendentals=rows * hidden),
        name="feed_factors",
    )(second_all, *pinned((wg, wu)))


def feed_kernel(own, last, mixer, second, chosen, wdt, gate_factor, up_factor, active, *rest):
    earlier, (gate, up, down, squares, mine, second_own) = rest[:-6], rest[-6:]

    @pl.when(pl.program_id(0) == 0)
    def pick():
        mine[...] = dot(mixer[...], chosen[...]).T.astype(BF)
        second_own[...] = dot(second[...], chosen[...]).T.astype(BF)
        squares[...] = jnp.zeros_like(squares)

    parts = None
    step = mixer.shape[0] // 2
    for i in range(2):
        band = slice(i * step, (i + 1) * step)
        slope = dot(mixer[band], wdt[...])
        gate_slope = (slope * gate_factor[band].astype(F32)).astype(BF)
        up_slope = (slope * up_factor[band].astype(F32)).astype(BF)
        here = (
            dot(second_own[:, band], gate_slope),
            dot(second_own[:, band], up_slope),
            dot(mine[:, band], active[band]),
        )
        parts = here if parts is None else [a + b for a, b in zip(parts, here)]
    for k, (ref, part) in enumerate(zip((gate, up, down), parts)):
        part = part[:own]
        if earlier:
            part = part + earlier[k][...]
        ref[...] = part
        if last:
            squares[...] += jnp.sum(part * part, axis=0, keepdims=True)


def feed(own, last, band, mixer_all, second_all, chosen, wdt, made, earlier):
    rows, width = BAND, mixer_all.shape[1]
    hidden = wdt.shape[1]
    piece = 512
    whole = lambda i: (0, 0)
    column = lambda i: (0, i)
    once = pl.Buffered(1)
    result = pl.BlockSpec((own, piece), column)
    return pl.pallas_call(
        functools.partial(feed_kernel, own, last),
        grid=(hidden // piece,),
        out_shape=[(jax.ShapeDtypeStruct if last else pltpu.HBM)((own, hidden), F32)] * 3
        + [jax.ShapeDtypeStruct((1, piece), F32)],
        in_specs=[pl.BlockSpec((rows, width), lambda i: (band, 0), pipeline_mode=once)] * 2
        + [pl.BlockSpec(chosen.shape, whole, pipeline_mode=once), pl.BlockSpec((width, piece), column)]
        + [pl.BlockSpec((rows, piece), column)] * 3
        + [result] * len(earlier),
        out_specs=[result] * 3 + [pl.BlockSpec((1, piece), whole)],
        scratch_shapes=[pltpu.VMEM((chosen.shape[1], rows), BF)] * 2,
        compiler_params=pltpu.CompilerParams(vmem_limit_bytes=16 * MEGA),
        cost_estimate=pl.CostEstimate(
            flops=2 * (rows + 3 * own) * wdt.size, bytes_accessed=8 * rows * hidden, transcendentals=0
        ),
        name="feed_gradient",
    )(mixer_all, second_all, chosen, *pinned((wdt, *made, *earlier)))


def finish_kernel(terms, squares, query, key, value, output, gains, total):
    edge = QUERY + 2 * PAIR
    whole = terms[...].astype(F32)
    query[...] = whole[:, :QUERY]
    key[...] = whole[:, QUERY : QUERY + PAIR].T
    value[...] = whole[:, QUERY + PAIR : edge].T
    output[...] = whole[:, JOINED : JOINED + QUERY]
    gains[...] = whole[:, edge : edge + 2]
    sums = jnp.sum(whole * whole, axis=0, keepdims=True)
    total[...] = jnp.sum(sums, axis=1, keepdims=True) + jnp.sum(squares[...], axis=1, keepdims=True)


def finish(terms, squares):
    own = terms.shape[0]
    shapes = ((own, QUERY), (PAIR, own), (PAIR, own), (own, QUERY), (own, 2), (1, 1))
    return pl.pallas_call(
        finish_kernel,
        out_shape=[jax.ShapeDtypeStruct(shape, F32) for shape in shapes],
        in_specs=[vmem()] * 2,
        out_specs=[vmem()] * len(shapes),
        compiler_params=pltpu.CompilerParams(vmem_limit_bytes=16 * MEGA),
        name="finish",
    )(terms, squares)


def after(value, *tokens):
    return lax.optimization_barrier((value,) + tokens)[0]


def gathered_at(block, axis, target):
    count = lax.axis_size(axis)
    pieces = [block if s == target else lax.ppermute(block, axis, [(s, target)]) for s in range(count)]
    return pieces


def spread_from(whole, axis, source):
    count = lax.axis_size(axis)
    width = whole.shape[1] // count
    columns = [whole[:, s * width : (s + 1) * width] for s in range(count)]
    mine = jnp.where(lax.axis_index(axis) == source, columns[source], jnp.zeros_like(columns[source]))
    for s in range(count):
        if s != source:
            mine = mine + lax.ppermute(columns[s], axis, [(source, s)])
    return mine


class LineGather:
    def __init__(self, block, axis):
        self.axis, self.count = axis, lax.axis_size(axis)
        self.line, self.step = self.count // 2, 0
        self.held = [block] + [None] * (self.line - 1)
        self.moving = (block, block)

    def advance(self, *tokens):
        ahead = [(i, i + 2) for i in range(self.count - 2)]
        self.step += 1
        below, above = self.moving
        if tokens:
            below, above, *_ = lax.optimization_barrier((below, above, *tokens))
        below = lax.ppermute(below, self.axis, ahead)
        above = lax.ppermute(above, self.axis, [(b, a) for a, b in ahead])
        self.moving = (below, above)
        for k, item in ((self.step, below), (self.line - self.step, above)):
            self.held[k] = item if self.held[k] is None else self.held[k] + item

    def finish(self):
        while self.step < self.line - 1:
            self.advance()
        mine = jnp.concatenate(self.held)
        other = lax.ppermute(mine, self.axis, [(i, i ^ 1) for i in range(self.count)])
        bands = [slice(start, start + BAND) for start in range(0, mine.shape[0], BAND)]
        return [half[band] for half in (mine, other) for band in bands]


def summed(value, axis):
    count, distance = lax.axis_size(axis), 1
    while distance < count:
        value = value + lax.ppermute(value, axis, [(i, i ^ distance) for i in range(count)])
        distance *= 2
    return value


def per_device(
    inputs, cotangent, first_gain, w_query, w_key, w_value, w_output, second_gain, w_gate, w_up, w_down
):
    sections = lax.axis_size("section")
    replicas = lax.axis_size("dp")
    section = lax.axis_index("section")
    micro, length, part = inputs.shape
    rows, width = micro * length, part * sections
    hidden = w_gate.shape[2]
    own = width // replicas
    w_query, w_key, w_value, w_output = w_query[0], w_key[0], w_value[0], w_output[0]
    w_gate, w_up, w_down = w_gate[0], w_up[0], w_down[0]
    gains = (first_gain, second_gain)
    tables = tuple(jnp.asarray(table) for table in rotary_tables(length, rows))
    place = section.astype(jnp.int32).reshape(1)
    w_query, place = lax.optimization_barrier((w_query, place))
    own_rows = -(-own // 16) * 16
    at = lax.broadcasted_iota(jnp.int32, (width, own_rows), 1)
    chosen = jnp.logical_and(
        lax.broadcasted_iota(jnp.int32, (width, own_rows), 0) == at + own * lax.axis_index("dp"), at < own
    ).astype(BF)

    x = gathered_at(inputs.reshape(rows, part), "section", 0)
    w_down = w_down.T
    weights = load(w_query, w_key.T, w_value.T, w_output, w_gate, w_up, w_down)
    last_slope = gathered_at(cotangent.reshape(rows, part), "section", sections - 1)

    stash = lefts = ()
    for t in range(sections):
        leaving, weights, stash, lefts = forward_pass(
            t, place, x, gains, tables, weights, stash, lefts, length, hidden
        )
        if t < sections - 1:
            x = [lax.ppermute(leaving, "section", [(t, t + 1)])]
        if t == 0:
            *weights, output_back, back_far, joined_back = turned(*weights)
    normed, context, second = lefts
    streamed = (output_back, joined_back)
    weights = weights[:2]

    final = leaving
    slope = last_slope
    made = mixers = ()
    for t in reversed(range(sections)):
        leaving, weights, stash, made, mixers, far = backward_pass(
            t, place, slope, gains, tables, stash, streamed, weights, made, mixers, length, hidden, t == sections - 1
        )
        if t > 0:
            slope = [lax.ppermute(leaving, "section", [(t, t - 1)])]
        if t > 0:
            if t == sections - 1:
                second_all = lax.all_gather(after(second.reshape(2 * rows, width), far[0]), "dp", axis=0, tiled=True)
                near = moved((w_down, back_far, *far), True)
                weights, stash, made = near[:2], near[2:4], near[4:]
    mixer_all = lax.all_gather(mixers[0].reshape(2 * rows, width), "dp", axis=0, tiled=True)
    terms = parts(normed, context, made[0])
    index = after(lax.axis_index("dp"), leaving)
    pairs = terms.reshape(replicas // 2, 2, own, terms.shape[1])
    other = lax.dynamic_index_in_dim(pairs, 1 - lax.bitwise_and(index, 1), 1, keepdims=False)
    mine = lax.dynamic_index_in_dim(pairs, lax.bitwise_and(index, 1), 1, keepdims=False)
    swap = [(i, i ^ 1) for i in range(replicas)]
    other = lax.ppermute(other, "dp", swap)
    made = [factors(second_all, 0, w_gate, w_up)]
    other = after(other, made[0][0])
    terms = (mine + other).reshape(-1, terms.shape[1])
    groups = [list(range(core, replicas, 2)) for core in range(2)]
    reduced = lax.psum_scatter(terms, "dp", scatter_dimension=0, axis_index_groups=groups, tiled=True)
    made += [factors(second_all, band, w_gate, w_up) for band in range(1, 2 * rows * replicas // BAND)]
    outputs, delta_inputs = (
        spread_from(after(item, made[-1][0]), "section", source)
        for item, source in ((final, sections - 1), (leaving, 0))
    )
    feed_parts = ()
    for band, item in enumerate(made):
        last = band == len(made) - 1
        *feed_parts, squares = feed(own, last, band, mixer_all, second_all, chosen, w_down, item, feed_parts)
    gate, up, down = feed_parts
    query, key, value, output, gain_terms, total = finish(reduced, squares)
    total = summed(summed(total, "dp"), "section")
    return (
        outputs.astype(F32).reshape(micro, length, part),
        delta_inputs.astype(F32).reshape(micro, length, part),
        gain_terms[:, 0][None],
        query[None],
        key.T[None],
        value.T[None],
        output[None],
        gain_terms[:, 1][None],
        gate[None],
        up[None],
        down.T[None],
        jnp.sqrt(total).reshape(()),
    )


def solution(mesh):
    stacked = P("section", None, None)
    rows = P("section", "dp", None)
    return jax.shard_map(
        per_device,
        mesh=mesh,
        in_specs=(P("dp", None, "section"),) * 2
        + (P("section", None),)
        + (stacked,) * 4
        + (P("section", None),)
        + (stacked,) * 3,
        out_specs=(P("dp", None, "section"),) * 2
        + (P("section", "dp"),)
        + (rows,) * 4
        + (P("section", "dp"),)
        + (rows,) * 2
        + (P("section", None, "dp"), P()),
        check_vma=False,
    )
```

```python
import functools

import jax
import jax.numpy as jnp
import numpy as np
from jax import lax
from jax.experimental import pallas as pl
from jax.experimental.pallas import tpu as pltpu
from jax.sharding import PartitionSpec as P

HEADS = 15
KV_HEADS = 5
HEAD = 64
EPSILON = 1e-05
THETA = 10000.0
LANES = 128
PIECES = 2
BAND = 1024
BF = jnp.bfloat16
F32 = jnp.float32
QUERY = HEADS * HEAD
PAIR = KV_HEADS * HEAD
JOINED = QUERY + 2 * PAIR + HEAD
CHUNKS = (HEADS + 1) // 2
MEGA = 2**20


def dot(left, right):
    return jnp.dot(left, right, preferred_element_type=F32)


def dot_last(left, right):
    return lax.dot_general(left, right, (((1,), (1,)), ((), ())), preferred_element_type=F32)


def dot_first(left, right):
    return lax.dot_general(left, right, (((0,), (0,)), ((), ())), preferred_element_type=F32)


def rotary_tables(length, rows):
    half = HEAD // 2
    frequency = THETA ** (-(np.arange(half, dtype=np.float64) * 2.0 / HEAD))
    angles = np.arange(length, dtype=np.float64)[:, None] * frequency[None, :]
    angles = np.concatenate([angles] * (LANES // half), axis=-1)
    sign = np.where(np.arange(LANES) % HEAD < half, -1.0, 1.0)
    copies = (rows // length, 1)
    return (
        np.tile(np.cos(angles), copies).astype(np.float32),
        np.tile(np.sin(angles) * sign, copies).astype(np.float32),
    )


def lane_index(rows):
    return lax.broadcasted_iota(jnp.int32, (rows, LANES), 1)


def half_turned(chunk, first_half):
    return jnp.where(first_half, pltpu.roll(chunk, LANES - HEAD // 2, 1), pltpu.roll(chunk, HEAD // 2, 1))


def mean_scale(residual):
    return lax.rsqrt(jnp.mean(residual * residual, axis=-1, keepdims=True) + EPSILON)


def group_of(head):
    return head // (HEADS // KV_HEADS)


def chunk_heads(chunk):
    return [head for head in (2 * chunk, 2 * chunk + 1) if head < HEADS]


def spread_groups(chunks, first_lane, lower):
    low, high = {}, {}
    for group in range(KV_HEADS):
        column = first_lane + group * HEAD
        chunk = chunks[column // LANES]
        swapped = pltpu.roll(chunk, HEAD, 1)
        here, there = (chunk, swapped) if column % LANES == 0 else (swapped, chunk)
        low[group] = jnp.where(lower, here, 0.0).astype(BF)
        high[group] = jnp.where(lower, 0.0, there).astype(BF)
    return low, high


def chunk_operand(spread, chunk):
    return [spread[head % 2][group_of(head)] for head in chunk_heads(chunk)]


LEFTS = ("normed", "context", "second")


def halves(ref, *sizes):
    starts = [sum(sizes[:i]) for i in range(len(sizes))]
    return [ref.at[pl.ds(start, size)] for start, size in zip(starts, sizes)]


def stash_widths(hidden):
    return {
        "query": CHUNKS * LANES,
        "keys": KV_HEADS * 2 * LANES,
        "values": KV_HEADS * 2 * LANES,
        "chances": CHUNKS * 2 * LANES,
        "gate_factor": hidden,
        "up_factor": hidden,
    }


def stash_shape(rows, hidden):
    return (2, rows, sum(stash_widths(hidden).values()))


def views(ref, widths, app):
    starts, start = {}, 0
    for name, width in widths.items():
        starts[name] = start
        start += -(-width // LANES) * LANES

    def get(name, low=0, high=None):
        high = widths[name] if high is None else high
        return ref[app, :, starts[name] + low : starts[name] + high]

    def put(name, value, low=0):
        ref[app, :, starts[name] + low : starts[name] + low + value.shape[1]] = value

    return get, put


def assembled(pieces):
    return jnp.concatenate([piece[...] for piece in pieces], axis=1)


def forward_kernel(tick, rows, length, hidden, old, count, section, gain_one, gain_two, cosine, sine, *rest):
    x, rest = rest[:count], rest[count:]
    (wide, tall, vqkv), leaving = rest[:3], rest[old]
    stash, sums, *left_out, left, left_sems = rest[-7:]
    width = leaving.shape[1]
    vg, vu, _ = halves(wide, width, width, width)
    vd, _, _, vo = halves(tall, hidden, hidden, hidden, width)
    piece = hidden // PIECES

    @pl.when(section[0] == tick)
    def run():
        lanes = lane_index(rows)
        lower = lanes < HEAD
        first_half = lax.rem(lanes, HEAD) < HEAD // 2
        token = lax.broadcasted_iota(jnp.int32, (rows, rows), 0)
        other = lax.broadcasted_iota(jnp.int32, (rows, rows), 1)
        seen = jnp.logical_and(token <= other, lax.div(other, length) == lax.div(token, length))
        cos, sin = cosine[...], sine[...]
        residual = assembled(x).astype(F32)
        writes = []
        for app in range(2):
            def give(name, value, app=app):
                i = LEFTS.index(name)
                left[i, app] = value
                write = pltpu.make_async_copy(left.at[i, app], left_out[i].at[app], left_sems.at[i, app])
                write.start()
                writes.append(write)

            get, put = views(stash, stash_widths(hidden), app)
            sums[0, app] = residual
            normed = (residual * mean_scale(residual) * gain_one[...]).astype(BF)
            give("normed", normed)
            joined = dot(normed, vqkv[...])
            chunks = [joined[:, i * LANES : (i + 1) * LANES] for i in range(JOINED // LANES)]
            turned = (QUERY + PAIR) // LANES
            for i in range(turned):
                chunks[i] = chunks[i] * cos + half_turned(chunks[i], first_half) * sin
            queries = [chunk.astype(BF) for chunk in chunks[:CHUNKS]]
            keys = spread_groups(chunks, QUERY, lower)
            values = spread_groups(chunks, QUERY + PAIR, lower)
            for name, (low, high) in (("keys", keys), ("values", values)):
                for group in range(KV_HEADS):
                    at = 2 * group * LANES
                    put(name, low[group], at)
                    put(name, high[group], at + LANES)
            key_sides = [jnp.concatenate(chunk_operand(keys, c), axis=0) for c in range(CHUNKS)]
            value_sides = [jnp.concatenate(chunk_operand(values, c), axis=0) for c in range(CHUNKS)]
            all_scores = [dot_last(key_sides[c], queries[c]) for c in range(CHUNKS)]
            all_chances = []
            for c in range(CHUNKS):
                put("query", queries[c], c * LANES)
                parts = []
                for side in range(len(chunk_heads(c))):
                    at = (2 * c + side) * LANES
                    scores = all_scores[c][side * rows : (side + 1) * rows] * HEAD ** (-0.5)
                    scores = jnp.where(seen, scores, -1e30)
                    highest = jnp.max(scores, axis=0, keepdims=True)
                    powers = jnp.exp(scores - highest)
                    total = jnp.sum(powers, axis=0, keepdims=True)
                    parts.append((powers * (1.0 / total)).astype(BF))
                    put("chances", parts[side], at)
                all_chances.append(jnp.concatenate(parts, axis=0))
            contexts = [dot_first(all_chances[c], value_sides[c]).astype(BF) for c in range(CHUNKS)]
            context = jnp.concatenate(contexts, axis=1)[:, :QUERY]
            give("context", context)
            middle = residual + dot(context, vo[...])
            sums[1, app] = middle
            second = (middle * mean_scale(middle) * gain_two[...]).astype(BF)
            give("second", second)
            total = middle
            for i in range(PIECES):
                cols = slice(i * piece, (i + 1) * piece)
                gate = dot(second, vg[:, cols])
                up = dot(second, vu[:, cols])
                sigma = jax.nn.sigmoid(gate)
                linear = gate * sigma
                put("gate_factor", (up * (sigma + linear * (1.0 - sigma))).astype(BF), i * piece)
                put("up_factor", linear.astype(BF), i * piece)
                total = total + dot((linear * up).astype(BF), vd[cols])
            residual = total
        leaving[...] = residual.astype(BF)
        for write in writes:
            write.wait()


def vmem():
    return pl.BlockSpec(memory_space=pltpu.VMEM)


def anywhere():
    return pl.BlockSpec(memory_space=pl.ANY)


def pinned(arrays):
    return [pltpu.with_memory_space_constraint(array, pltpu.HBM) for array in arrays]


def resident(arrays):
    return [pltpu.with_memory_space_constraint(array, pltpu.VMEM) for array in arrays]


def vmem_like(arrays):
    return [pltpu.VMEM(array.shape, array.dtype) for array in arrays]


def forward_pass(tick, section, x, gains, tables, weights, stash, lefts, length, hidden):
    rows, width = x[0].shape[0], weights[1].shape[1]
    held = [*weights, *stash]
    count = len(x)
    outs = pl.pallas_call(
        functools.partial(forward_kernel, tick, rows, length, hidden, len(held) + len(lefts), count),
        out_shape=[pltpu.VMEM((rows, width), BF)]
        + vmem_like(weights)
        + [pltpu.VMEM(stash_shape(rows, hidden), BF), pltpu.VMEM((2, 2, rows, width), F32)]
        + [pltpu.HBM((2, rows, width), BF)] * len(LEFTS),
        in_specs=[pl.BlockSpec(memory_space=pltpu.SMEM)]
        + [vmem()] * (4 + count + len(held))
        + [pl.BlockSpec(memory_space=pltpu.HBM)] * len(lefts),
        out_specs=[vmem()] * (3 + len(weights)) + [pl.BlockSpec(memory_space=pltpu.HBM)] * len(LEFTS),
        scratch_shapes=[
            pltpu.VMEM((len(LEFTS), 2, rows, width), BF),
            pltpu.SemaphoreType.DMA((len(LEFTS), 2)),
        ],
        input_output_aliases={5 + count + i: 1 + i for i in range(len(held) + len(lefts))},
        compiler_params=pltpu.CompilerParams(vmem_limit_bytes=16 * MEGA),
        name="forward_pass",
    )(section, *resident((*gains, *tables, *x, *held)), *pinned(lefts))
    first = 1 + len(weights)
    return outs[0], outs[1:first], outs[first : first + 2], outs[first + 2 :]


SLOPES = {"branch": QUERY, "attend": JOINED, "first": QUERY, "second": QUERY}
SLOPES_WIDTH = sum(-(-width // LANES) * LANES for width in SLOPES.values())


def backward_kernel(tick, rows, length, hidden, old, count, saves, section, gain_one, gain_two, cosine, sine, *rest):
    slope_in, rest = rest[:count], rest[count:]
    (wot, wqkvt, wide, tall, stash, sums), rest = rest[:6], rest[6 + old :]
    leaving, _, _, _, _, made, mixer_out, *far, vot, vqkvt, mixers, sems, mixer_sems, far_sems = rest
    near = (stash, sums, made)
    saving = [pltpu.make_async_copy(near[i], far[i], far_sems.at[i]) for i in range(2)] if saves else []
    sending = [
        pltpu.make_async_copy(made.at[app], far[2].at[app], far_sems.at[2 + app]) for app in range(2) if saves
    ]
    width = leaving.shape[1]
    if saves:
        _, _, vdt = halves(wide, width, width, width)
        _, vgt, vut, _ = halves(tall, hidden, hidden, hidden, width)
    else:
        vdt, (vgt, vut) = wide, halves(tall, hidden, hidden)
    piece = hidden // PIECES

    @pl.when(section[0] == tick)
    def run():
        lanes = lane_index(rows)
        lower = lanes < HEAD
        first_half = lax.rem(lanes, HEAD) < HEAD // 2
        cos, sin = cosine[...], sine[...]
        copies = [
            pltpu.make_async_copy(wot, vot, sems.at[0]),
            pltpu.make_async_copy(wqkvt, vqkvt, sems.at[1]),
        ]
        for copy in copies:
            copy.start()
        slope = assembled(slope_in).astype(F32)
        writes = []
        for app in (1, 0):
            if app == 0:
                for copy in saving + sending[1:]:
                    copy.start()
            get, _ = views(stash, stash_widths(hidden), app)
            _, put = views(made, SLOPES, app)
            mixer = slope.astype(BF)
            mixers[app] = mixer
            writes.append(pltpu.make_async_copy(mixers.at[app], mixer_out.at[app], mixer_sems.at[app]))
            writes[-1].start()
            back = None
            for i in range(PIECES):
                cols = slice(i * piece, (i + 1) * piece)
                active = dot(mixer, vdt[:, cols])
                gate = (active * get("gate_factor", i * piece, (i + 1) * piece).astype(F32)).astype(BF)
                up = (active * get("up_factor", i * piece, (i + 1) * piece).astype(F32)).astype(BF)
                part = dot(gate, vgt[cols]) + dot(up, vut[cols])
                back = part if back is None else back + part
            middle = sums[1, app]
            scale = mean_scale(middle)
            shaped = back * gain_two[...]
            inner = jnp.mean(shaped * middle, axis=-1, keepdims=True)
            put("second", (back * middle * scale).astype(BF))
            middle_slope = slope + scale * shaped - middle * (scale * scale * scale * inner)
            branch = middle_slope.astype(BF)
            put("branch", branch)
            if app == 1:
                copies[0].wait()
            context_slope = dot(branch, vot[...])
            query_back, key_back, value_back = [], {}, {}

            def operand(name, c):
                sides = range(len(chunk_heads(c)))
                places = [2 * c + side if name == "chances" else 2 * group_of(2 * c + side) + side for side in sides]
                return jnp.concatenate([get(name, place * LANES, (place + 1) * LANES) for place in places], axis=0)

            rounded = [context_slope[:, c * LANES : (c + 1) * LANES].astype(BF) for c in range(CHUNKS)]
            all_slopes = [dot_last(operand("values", c), rounded[c]) for c in range(CHUNKS)]
            all_chances = [operand("chances", c) for c in range(CHUNKS)]
            value_parts = [dot(all_chances[c], rounded[c]) for c in range(CHUNKS)]
            all_scores = []
            for c in range(CHUNKS):
                scores = []
                for side in range(len(chunk_heads(c))):
                    band = slice(side * rows, (side + 1) * rows)
                    chance, chance_slope = all_chances[c][band].astype(F32), all_slopes[c][band]
                    inner = jnp.sum(chance * chance_slope, axis=0, keepdims=True)
                    scores.append((chance * (chance_slope - inner)).astype(BF))
                all_scores.append(jnp.concatenate(scores, axis=0))
            key_parts = [dot(all_scores[c], get("query", c * LANES, (c + 1) * LANES)) for c in range(CHUNKS)]
            query_back = [dot_first(all_scores[c], operand("keys", c)) for c in range(CHUNKS)]
            for c in range(CHUNKS):
                key_part, value_part = key_parts[c], value_parts[c]
                for head in chunk_heads(c):
                    side, group = head % 2, group_of(head)
                    band = slice(side * rows, (side + 1) * rows)
                    for store, part in ((key_back, key_part), (value_back, value_part)):
                        item = part[band]
                        store[group, side] = store[group, side] + item if (group, side) in store else item

            def gathered(store, group, up_half):
                low, high = store[group, 0], store[group, 1]
                if up_half:
                    return pltpu.roll(low, HEAD, 1) + high
                return low + pltpu.roll(high, HEAD, 1)

            chunks = query_back + [None] * (JOINED // LANES - CHUNKS)
            for store, start in ((key_back, QUERY), (value_back, QUERY + PAIR)):
                for group in range(KV_HEADS):
                    at, offset = divmod(start + group * HEAD, LANES)
                    item = gathered(store, group, offset > 0)
                    if offset == 0:
                        chunks[at] = jnp.where(lower, item, 0.0)
                    else:
                        chunks[at] = jnp.where(lower, chunks[at], item)
            for i in range((QUERY + PAIR) // LANES):
                chunks[i] = (chunks[i] * cos - half_turned(chunks[i], first_half) * sin) * HEAD ** (-0.5)
            attend = jnp.concatenate([chunk.astype(BF) for chunk in chunks], axis=1)
            put("attend", attend)
            if app == 1:
                copies[1].wait()
            back = dot(attend, vqkvt[...])
            residual = sums[0, app]
            scale = mean_scale(residual)
            shaped = back * gain_one[...]
            inner = jnp.mean(shaped * residual, axis=-1, keepdims=True)
            put("first", (back * residual * scale).astype(BF))
            slope = middle_slope + scale * shaped - residual * (scale * scale * scale * inner)
        leaving[...] = slope.astype(BF)
        for write in writes:
            write.wait()

    @pl.when(section[0] != tick)
    def save():
        for copy in saving + sending[1:]:
            copy.start()

    for copy in sending[:1]:
        copy.start()
    for copy in saving + sending:
        copy.wait()


def backward_pass(tick, section, slope, gains, tables, stash, streamed, weights, made, mixers, length, hidden, saves):
    rows, width = slope[0].shape[0], weights[1].shape[1]
    held = [*weights, *stash, *made]
    count = len(slope)
    outs = pl.pallas_call(
        functools.partial(backward_kernel, tick, rows, length, hidden, len(made) + len(mixers), count, saves),
        out_shape=[pltpu.VMEM((rows, width), BF)]
        + vmem_like([*weights, *stash])
        + [pltpu.VMEM((2, rows, SLOPES_WIDTH), BF), pltpu.HBM((2, rows, width), BF)]
        + (
            [pltpu.HBM(array.shape, array.dtype) for array in stash] + [pltpu.HBM((2, rows, SLOPES_WIDTH), BF)]
            if saves
            else []
        ),
        in_specs=[pl.BlockSpec(memory_space=pltpu.SMEM)]
        + [vmem()] * (4 + count)
        + [pl.BlockSpec(memory_space=pltpu.HBM)] * 2
        + [vmem()] * len(held)
        + [pl.BlockSpec(memory_space=pltpu.HBM)] * len(mixers),
        out_specs=[vmem()] * 6 + [pl.BlockSpec(memory_space=pltpu.HBM)] * (4 if saves else 1),
        scratch_shapes=[pltpu.VMEM(w.shape, BF) for w in streamed]
        + [pltpu.VMEM((2, rows, width), BF)]
        + [pltpu.SemaphoreType.DMA((2,))] * 2
        + [pltpu.SemaphoreType.DMA((4,))],
        input_output_aliases={7 + count + i: 1 + i for i in range(len(held) + len(mixers))},
        compiler_params=pltpu.CompilerParams(vmem_limit_bytes=16 * MEGA),
        name="backward_pass",
    )(section, *resident((*gains, *tables, *slope)), *pinned(streamed), *resident(held), *pinned(mixers))
    return outs[0], outs[1:3], outs[3:5], outs[5:6], outs[6:7], outs[7:]


def turn(source, target, row=0, column=0):
    depth, width = source.shape
    for start in range(0, width, LANES):
        stop = min(start + LANES, width)
        target[row + start : row + stop, column : column + depth] = source[:, start:stop].T


def load_kernel(wq, wkt, wvt, wo, wg, wu, wdt, wide, tall, vqkv, sq, pairs, sems):
    width, pair = wq.shape[0], wkt.shape[0]
    vg, vu, vdt = halves(wide, width, width, width)
    vd, _, _, vo = halves(tall, *[wg.shape[1]] * 3, width)
    moves = [(wdt, vdt), (wkt, pairs.at[pl.ds(0, pair)]), (wvt, pairs.at[pl.ds(pair, pair)]), (wq, sq), (wo, vo)]
    step = width // 3
    for i in range(3):
        band = pl.ds(i * step, step)
        moves += [(wg.at[band], vg.at[band]), (wu.at[band], vu.at[band])]
    copies = [pltpu.make_async_copy(source, target, sems.at[i]) for i, (source, target) in enumerate(moves)]
    for copy in copies:
        copy.start()
    pairs[2 * pair :] = jnp.zeros((HEAD, width), BF)
    copies[0].wait()
    turn(vdt, vd)
    for copy in copies[1:4]:
        copy.wait()
    vqkv[:, :width] = sq[...]
    vqkv[:, width:] = pairs[...].T
    for copy in copies[4:]:
        copy.wait()


def load(wq, wkt, wvt, wo, wg, wu, wdt):
    width, hidden = wg.shape
    return pl.pallas_call(
        load_kernel,
        out_shape=[
            pltpu.VMEM((3 * width, hidden), BF),
            pltpu.VMEM((3 * hidden + width, width), BF),
            pltpu.VMEM((width, JOINED), BF),
        ],
        in_specs=[pl.BlockSpec(memory_space=pltpu.HBM)] * 7,
        out_specs=[vmem()] * 3,
        scratch_shapes=[
            pltpu.VMEM(wq.shape, BF),
            pltpu.VMEM((2 * PAIR + HEAD, width), BF),
            pltpu.SemaphoreType.DMA((11,)),
        ],
        compiler_params=pltpu.CompilerParams(vmem_limit_bytes=16 * MEGA),
        name="load_weights",
    )(*pinned((wq, wkt, wvt, wo, wg, wu, wdt)))


def turn_kernel(wide, tall, vqkv, wide_out, tall_out, vqkv_out, wot, wback, wqkvt, vot, vqkvt, sems):
    hidden, width = wide.shape[1], tall.shape[1]
    vg, vu, _ = halves(wide, width, width, width)
    _, vgt, vut, vo = halves(tall, hidden, hidden, hidden, width)
    copies = [
        pltpu.make_async_copy(source, target, sems.at[i])
        for i, (source, target) in enumerate(zip((vot, vgt, vut), [wot] + halves(wback, hidden, hidden)))
    ]
    vot[:, :width] = vo[...].T
    vot[:, width:] = jnp.zeros((width, HEAD), BF)
    copies[0].start()
    copies.append(pltpu.make_async_copy(vqkvt, wqkvt, sems.at[3]))
    for source, target, copy in zip((vg, vu, vqkv), (vgt, vut, vqkvt), copies[1:]):
        turn(source, target)
        copy.start()
    for copy in copies:
        copy.wait()


def turned(wide, tall, vqkv):
    hidden, width = wide.shape[1], tall.shape[1]
    back = (2 * hidden, width)
    return pl.pallas_call(
        turn_kernel,
        out_shape=vmem_like((wide, tall, vqkv))
        + [pltpu.HBM((width, CHUNKS * LANES), BF), pltpu.HBM(back, BF), pltpu.HBM((JOINED, width), BF)],
        in_specs=[vmem()] * 3,
        out_specs=[vmem()] * 3 + [pl.BlockSpec(memory_space=pltpu.HBM)] * 3,
        scratch_shapes=[
            pltpu.VMEM((width, CHUNKS * LANES), BF),
            pltpu.VMEM((JOINED, width), BF),
            pltpu.SemaphoreType.DMA((4,)),
        ],
        input_output_aliases={0: 0, 1: 1, 2: 2},
        compiler_params=pltpu.CompilerParams(vmem_limit_bytes=16 * MEGA),
        name="turn_weights",
    )(*resident((wide, tall, vqkv)))


def moved_kernel(count, *refs):
    copies = [
        pltpu.make_async_copy(refs[i], refs[count + i], refs[-1].at[i]) for i in range(count)
    ]
    for copy in copies:
        copy.start()
    for copy in copies:
        copy.wait()


def moved(arrays, inward):
    count = len(arrays)
    near, far = (vmem(), pltpu.VMEM), (pl.BlockSpec(memory_space=pltpu.HBM), pltpu.HBM)
    (source, _), (target, place) = (far, near) if inward else (near, far)
    return pl.pallas_call(
        functools.partial(moved_kernel, count),
        out_shape=[place(array.shape, array.dtype) for array in arrays],
        in_specs=[source] * count,
        out_specs=[target] * count,
        scratch_shapes=[pltpu.SemaphoreType.DMA((count,))],
        compiler_params=pltpu.CompilerParams(vmem_limit_bytes=16 * MEGA),
        cost_estimate=pl.CostEstimate(
            flops=0, bytes_accessed=2 * sum(array.size * array.dtype.itemsize for array in arrays), transcendentals=0
        ),
        name="restored" if inward else "saved",
    )(*(pinned if inward else resident)(arrays))


def parts_kernel(normed, context, made, out, stage, sems):
    rows = normed.shape[0] * normed.shape[1]
    edge = QUERY + 2 * PAIR
    gets = [views(made, SLOPES, app)[0] for app in range(2)]
    attend, branch, first, second = (
        jnp.concatenate([get(name) for get in gets], axis=0) for name in ("attend", "branch", "first", "second")
    )

    def flat(ref):
        return ref[...].reshape(rows, ref.shape[2])

    half = 6 * LANES
    bounds = (0, half, JOINED, stage.shape[1])
    copies = [
        pltpu.make_async_copy(stage.at[:, pl.ds(low, high - low)], out.at[:, pl.ds(low, high - low)], sems.at[i])
        for i, (low, high) in enumerate(zip(bounds[:-1], bounds[1:]))
    ]
    left, right = flat(normed), attend
    stage[:, :half] = dot_first(left, right[:, :half]).astype(BF)
    copies[0].start()
    stage[:, half:JOINED] = dot_first(left, right[:, half:]).astype(BF)
    lanes = lax.broadcasted_iota(jnp.int32, (rows, HEAD), 1)
    gains = dot_first(first, (lanes == 0).astype(BF)) + dot_first(second, (lanes == 1).astype(BF))
    stage[:, edge:JOINED] = gains.astype(BF)
    copies[1].start()
    stage[:, JOINED : JOINED + QUERY] = dot_first(flat(context), branch).astype(BF)
    stage[:, JOINED + QUERY :] = jnp.zeros((QUERY, HEAD), BF)
    copies[2].start()
    for copy in copies:
        copy.wait()


def parts(normed, context, made):
    shape = (QUERY, JOINED + QUERY + HEAD)
    return pl.pallas_call(
        parts_kernel,
        out_shape=pltpu.HBM(shape, BF),
        in_specs=[vmem()] * 3,
        out_specs=pl.BlockSpec(memory_space=pltpu.HBM),
        scratch_shapes=[pltpu.VMEM(shape, BF), pltpu.SemaphoreType.DMA((3,))],
        compiler_params=pltpu.CompilerParams(vmem_limit_bytes=16 * MEGA),
        cost_estimate=pl.CostEstimate(flops=4 * shape[0] * shape[1] * normed.shape[0] * normed.shape[1], bytes_accessed=4 * shape[0] * shape[1], transcendentals=0),
        name="attention_parts",
    )(*resident((normed, context, made)))


def factors_kernel(second, wg, wu, gate_factor, up_factor, active):
    step = 256
    for i in range(second.shape[0] // step):
        band = slice(i * step, (i + 1) * step)
        block = second[band]
        gate = dot(block, wg[...])
        up = dot(block, wu[...])
        sigma = jax.nn.sigmoid(gate)
        linear = gate * sigma
        gate_factor[band] = (up * (sigma + linear * (1.0 - sigma))).astype(BF)
        up_factor[band] = linear.astype(BF)
        active[band] = (linear * up).astype(BF)


def factors(second_all, band, wg, wu):
    rows, width = BAND, second_all.shape[1]
    hidden = wg.shape[1]
    block, piece = 512, 512
    first = band * (rows // block)
    wide = pl.BlockSpec((block, piece), lambda i, j: (j, i))
    weight = pl.BlockSpec((width, piece), lambda i, j: (0, i))
    return pl.pallas_call(
        factors_kernel,
        grid=(hidden // piece, rows // block),
        out_shape=[pltpu.HBM((rows, hidden), BF)] * 3,
        in_specs=[
            pl.BlockSpec((block, width), lambda i, j: (first + j, 0)),
            weight,
            weight,
        ],
        out_specs=[wide] * 3,
        compiler_params=pltpu.CompilerParams(vmem_limit_bytes=16 * MEGA),
        cost_estimate=pl.CostEstimate(flops=4 * rows * width * hidden, bytes_accessed=8 * rows * hidden, transcendentals=rows * hidden),
        name="feed_factors",
    )(second_all, *pinned((wg, wu)))


def feed_kernel(own, last, mixer, second, chosen, wdt, gate_factor, up_factor, active, *rest):
    earlier, (gate, up, down, squares, mine, second_own) = rest[:-6], rest[-6:]

    @pl.when(pl.program_id(0) == 0)
    def pick():
        mine[...] = dot(mixer[...], chosen[...]).T.astype(BF)
        second_own[...] = dot(second[...], chosen[...]).T.astype(BF)
        squares[...] = jnp.zeros_like(squares)

    parts = None
    step = mixer.shape[0] // 2
    for i in range(2):
        band = slice(i * step, (i + 1) * step)
        slope = dot(mixer[band], wdt[...])
        gate_slope = (slope * gate_factor[band].astype(F32)).astype(BF)
        up_slope = (slope * up_factor[band].astype(F32)).astype(BF)
        here = (
            dot(second_own[:, band], gate_slope),
            dot(second_own[:, band], up_slope),
            dot(mine[:, band], active[band]),
        )
        parts = here if parts is None else [a + b for a, b in zip(parts, here)]
    for k, (ref, part) in enumerate(zip((gate, up, down), parts)):
        part = part[:own]
        if earlier:
            part = part + earlier[k][...]
        ref[...] = part
        if last:
            squares[...] += jnp.sum(part * part, axis=0, keepdims=True)


def feed(own, last, band, mixer_all, second_all, chosen, wdt, made, earlier):
    rows, width = BAND, mixer_all.shape[1]
    hidden = wdt.shape[1]
    piece = 512
    whole = lambda i: (0, 0)
    column = lambda i: (0, i)
    once = pl.Buffered(1)
    result = pl.BlockSpec((own, piece), column)
    return pl.pallas_call(
        functools.partial(feed_kernel, own, last),
        grid=(hidden // piece,),
        out_shape=[(jax.ShapeDtypeStruct if last else pltpu.HBM)((own, hidden), F32)] * 3
        + [jax.ShapeDtypeStruct((1, piece), F32)],
        in_specs=[pl.BlockSpec((rows, width), lambda i: (band, 0), pipeline_mode=once)] * 2
        + [pl.BlockSpec(chosen.shape, whole, pipeline_mode=once), pl.BlockSpec((width, piece), column)]
        + [pl.BlockSpec((rows, piece), column)] * 3
        + [result] * len(earlier),
        out_specs=[result] * 3 + [pl.BlockSpec((1, piece), whole)],
        scratch_shapes=[pltpu.VMEM((chosen.shape[1], rows), BF)] * 2,
        compiler_params=pltpu.CompilerParams(vmem_limit_bytes=16 * MEGA),
        cost_estimate=pl.CostEstimate(
            flops=2 * (rows + 3 * own) * wdt.size, bytes_accessed=8 * rows * hidden, transcendentals=0
        ),
        name="feed_gradient",
    )(mixer_all, second_all, chosen, *pinned((wdt, *made, *earlier)))


def finish_kernel(terms, squares, query, key, value, output, gains, total):
    edge = QUERY + 2 * PAIR
    whole = terms[...].astype(F32)
    query[...] = whole[:, :QUERY]
    key[...] = whole[:, QUERY : QUERY + PAIR].T
    value[...] = whole[:, QUERY + PAIR : edge].T
    output[...] = whole[:, JOINED : JOINED + QUERY]
    gains[...] = whole[:, edge : edge + 2]
    sums = jnp.sum(whole * whole, axis=0, keepdims=True)
    total[...] = jnp.sum(sums, axis=1, keepdims=True) + jnp.sum(squares[...], axis=1, keepdims=True)


def finish(terms, squares):
    own = terms.shape[0]
    shapes = ((own, QUERY), (PAIR, own), (PAIR, own), (own, QUERY), (own, 2), (1, 1))
    return pl.pallas_call(
        finish_kernel,
        out_shape=[jax.ShapeDtypeStruct(shape, F32) for shape in shapes],
        in_specs=[vmem()] * 2,
        out_specs=[vmem()] * len(shapes),
        compiler_params=pltpu.CompilerParams(vmem_limit_bytes=16 * MEGA),
        name="finish",
    )(terms, squares)


def after(value, *tokens):
    return lax.optimization_barrier((value,) + tokens)[0]


def gathered_at(block, axis, target):
    count = lax.axis_size(axis)
    pieces = [block if s == target else lax.ppermute(block, axis, [(s, target)]) for s in range(count)]
    return pieces


def spread_from(whole, axis, source):
    count = lax.axis_size(axis)
    width = whole.shape[1] // count
    columns = [whole[:, s * width : (s + 1) * width] for s in range(count)]
    mine = jnp.where(lax.axis_index(axis) == source, columns[source], jnp.zeros_like(columns[source]))
    for s in range(count):
        if s != source:
            mine = mine + lax.ppermute(columns[s], axis, [(source, s)])
    return mine


class LineGather:
    def __init__(self, block, axis):
        self.axis, self.count = axis, lax.axis_size(axis)
        self.line, self.step = self.count // 2, 0
        self.held = [block] + [None] * (self.line - 1)
        self.moving = (block, block)

    def advance(self, *tokens):
        ahead = [(i, i + 2) for i in range(self.count - 2)]
        self.step += 1
        below, above = self.moving
        if tokens:
            below, above, *_ = lax.optimization_barrier((below, above, *tokens))
        below = lax.ppermute(below, self.axis, ahead)
        above = lax.ppermute(above, self.axis, [(b, a) for a, b in ahead])
        self.moving = (below, above)
        for k, item in ((self.step, below), (self.line - self.step, above)):
            self.held[k] = item if self.held[k] is None else self.held[k] + item

    def finish(self):
        while self.step < self.line - 1:
            self.advance()
        mine = jnp.concatenate(self.held)
        other = lax.ppermute(mine, self.axis, [(i, i ^ 1) for i in range(self.count)])
        bands = [slice(start, start + BAND) for start in range(0, mine.shape[0], BAND)]
        return [half[band] for half in (mine, other) for band in bands]


def summed(value, axis, distances):
    count = lax.axis_size(axis)
    values = [value] + [lax.ppermute(value, axis, [(i, i ^ d) for i in range(count)]) for d in distances]
    while len(values) > 1:
        values = [a + b for a, b in zip(values[::2], values[1::2])]
    return values[0]


def per_device(
    inputs, cotangent, first_gain, w_query, w_key, w_value, w_output, second_gain, w_gate, w_up, w_down
):
    sections = lax.axis_size("section")
    replicas = lax.axis_size("dp")
    section = lax.axis_index("section")
    micro, length, part = inputs.shape
    rows, width = micro * length, part * sections
    hidden = w_gate.shape[2]
    own = width // replicas
    w_query, w_key, w_value, w_output = w_query[0], w_key[0], w_value[0], w_output[0]
    w_gate, w_up, w_down = w_gate[0], w_up[0], w_down[0]
    gains = (first_gain, second_gain)
    tables = tuple(jnp.asarray(table) for table in rotary_tables(length, rows))
    place = section.astype(jnp.int32).reshape(1)
    w_query, place = lax.optimization_barrier((w_query, place))
    own_rows = -(-own // 16) * 16
    at = lax.broadcasted_iota(jnp.int32, (width, own_rows), 1)
    chosen = jnp.logical_and(
        lax.broadcasted_iota(jnp.int32, (width, own_rows), 0) == at + own * lax.axis_index("dp"), at < own
    ).astype(BF)

    x = gathered_at(inputs.reshape(rows, part), "section", 0)
    w_down = w_down.T
    weights = load(w_query, w_key.T, w_value.T, w_output, w_gate, w_up, w_down)
    last_slope = gathered_at(cotangent.reshape(rows, part), "section", sections - 1)

    stash = lefts = ()
    for t in range(sections):
        leaving, weights, stash, lefts = forward_pass(
            t, place, x, gains, tables, weights, stash, lefts, length, hidden
        )
        if t < sections - 1:
            x = [lax.ppermute(leaving, "section", [(t, t + 1)])]
        if t == 0:
            *weights, output_back, back_far, joined_back = turned(*weights)
    normed, context, second = lefts
    streamed = (output_back, joined_back)
    weights = weights[:2]

    final = leaving
    slope = last_slope
    made = mixers = ()
    for t in reversed(range(sections)):
        leaving, weights, stash, made, mixers, far = backward_pass(
            t, place, slope, gains, tables, stash, streamed, weights, made, mixers, length, hidden, t == sections - 1
        )
        if t > 0:
            slope = [lax.ppermute(leaving, "section", [(t, t - 1)])]
        if t > 0:
            if t == sections - 1:
                second_all = lax.all_gather(after(second.reshape(2 * rows, width), far[0]), "dp", axis=0, tiled=True)
                near = moved((w_down, back_far, *far), True)
                weights, stash, made = near[:2], near[2:4], near[4:]
    mixer_all = lax.all_gather(mixers[0].reshape(2 * rows, width), "dp", axis=0, tiled=True)
    terms = parts(normed, context, made[0])
    index = after(lax.axis_index("dp"), leaving)
    pairs = terms.reshape(replicas // 2, 2, own, terms.shape[1])
    other = lax.dynamic_index_in_dim(pairs, 1 - lax.bitwise_and(index, 1), 1, keepdims=False)
    mine = lax.dynamic_index_in_dim(pairs, lax.bitwise_and(index, 1), 1, keepdims=False)
    swap = [(i, i ^ 1) for i in range(replicas)]
    other = lax.ppermute(other, "dp", swap)
    made = [factors(second_all, 0, w_gate, w_up)]
    other = after(other, made[0][0])
    terms = (mine + other).reshape(-1, terms.shape[1])
    groups = [list(range(core, replicas, 2)) for core in range(2)]
    reduced = lax.psum_scatter(terms, "dp", scatter_dimension=0, axis_index_groups=groups, tiled=True)
    made += [factors(second_all, band, w_gate, w_up) for band in range(1, 2 * rows * replicas // BAND)]
    outputs, delta_inputs = (
        spread_from(after(item, made[-1][0]), "section", source)
        for item, source in ((final, sections - 1), (leaving, 0))
    )
    feed_parts = ()
    for band, item in enumerate(made):
        last = band == len(made) - 1
        *feed_parts, squares = feed(own, last, band, mixer_all, second_all, chosen, w_down, item, feed_parts)
    gate, up, down = feed_parts
    query, key, value, output, gain_terms, total = finish(reduced, squares)
    total = summed(total, "dp", [1])
    total = summed(total, "dp", range(2, replicas, 2))
    total = summed(total, "section", range(1, sections))
    return (
        outputs.astype(F32).reshape(micro, length, part),
        delta_inputs.astype(F32).reshape(micro, length, part),
        gain_terms[:, 0][None],
        query[None],
        key.T[None],
        value.T[None],
        output[None],
        gain_terms[:, 1][None],
        gate[None],
        up[None],
        down.T[None],
        jnp.sqrt(total).reshape(()),
    )


def solution(mesh):
    stacked = P("section", None, None)
    rows = P("section", "dp", None)
    return jax.shard_map(
        per_device,
        mesh=mesh,
        in_specs=(P("dp", None, "section"),) * 2
        + (P("section", None),)
        + (stacked,) * 4
        + (P("section", None),)
        + (stacked,) * 3,
        out_specs=(P("dp", None, "section"),) * 2
        + (P("section", "dp"),)
        + (rows,) * 4
        + (P("section", "dp"),)
        + (rows,) * 2
        + (P("section", None, "dp"), P()),
        check_vma=False,
    )
```

```python
import functools

import jax
import jax.numpy as jnp
import numpy as np
from jax import lax
from jax.experimental import pallas as pl
from jax.experimental.pallas import tpu as pltpu
from jax.sharding import PartitionSpec as P

HEADS = 15
KV_HEADS = 5
HEAD = 64
EPSILON = 1e-05
THETA = 10000.0
LANES = 128
PIECES = 2
BAND = 1024
BF = jnp.bfloat16
F32 = jnp.float32
QUERY = HEADS * HEAD
PAIR = KV_HEADS * HEAD
JOINED = QUERY + 2 * PAIR + HEAD
CHUNKS = (HEADS + 1) // 2
MEGA = 2**20


def dot(left, right):
    return jnp.dot(left, right, preferred_element_type=F32)


def dot_last(left, right):
    return lax.dot_general(left, right, (((1,), (1,)), ((), ())), preferred_element_type=F32)


def dot_first(left, right):
    return lax.dot_general(left, right, (((0,), (0,)), ((), ())), preferred_element_type=F32)


def rotary_tables(length, rows):
    half = HEAD // 2
    frequency = THETA ** (-(np.arange(half, dtype=np.float64) * 2.0 / HEAD))
    angles = np.arange(length, dtype=np.float64)[:, None] * frequency[None, :]
    angles = np.concatenate([angles] * (LANES // half), axis=-1)
    sign = np.where(np.arange(LANES) % HEAD < half, -1.0, 1.0)
    copies = (rows // length, 1)
    return (
        np.tile(np.cos(angles), copies).astype(np.float32),
        np.tile(np.sin(angles) * sign, copies).astype(np.float32),
    )


def lane_index(rows):
    return lax.broadcasted_iota(jnp.int32, (rows, LANES), 1)


def half_turned(chunk, first_half):
    return jnp.where(first_half, pltpu.roll(chunk, LANES - HEAD // 2, 1), pltpu.roll(chunk, HEAD // 2, 1))


def mean_scale(residual):
    return lax.rsqrt(jnp.mean(residual * residual, axis=-1, keepdims=True) + EPSILON)


def group_of(head):
    return head // (HEADS // KV_HEADS)


def chunk_heads(chunk):
    return [head for head in (2 * chunk, 2 * chunk + 1) if head < HEADS]


def spread_groups(chunks, first_lane, lower):
    low, high = {}, {}
    for group in range(KV_HEADS):
        column = first_lane + group * HEAD
        chunk = chunks[column // LANES]
        swapped = pltpu.roll(chunk, HEAD, 1)
        here, there = (chunk, swapped) if column % LANES == 0 else (swapped, chunk)
        low[group] = jnp.where(lower, here, 0.0).astype(BF)
        high[group] = jnp.where(lower, 0.0, there).astype(BF)
    return low, high


def chunk_operand(spread, chunk):
    return [spread[head % 2][group_of(head)] for head in chunk_heads(chunk)]


LEFTS = ("normed", "context", "second")


def halves(ref, *sizes):
    starts = [sum(sizes[:i]) for i in range(len(sizes))]
    return [ref.at[pl.ds(start, size)] for start, size in zip(starts, sizes)]


def stash_widths(hidden):
    return {
        "query": CHUNKS * LANES,
        "keys": KV_HEADS * 2 * LANES,
        "values": KV_HEADS * 2 * LANES,
        "chances": CHUNKS * 2 * LANES,
        "gate_factor": hidden,
        "up_factor": hidden,
    }


def stash_shape(rows, hidden):
    return (2, rows, sum(stash_widths(hidden).values()))


def views(ref, widths, app):
    starts, start = {}, 0
    for name, width in widths.items():
        starts[name] = start
        start += -(-width // LANES) * LANES

    def get(name, low=0, high=None):
        high = widths[name] if high is None else high
        return ref[app, :, starts[name] + low : starts[name] + high]

    def put(name, value, low=0):
        ref[app, :, starts[name] + low : starts[name] + low + value.shape[1]] = value

    return get, put


def assembled(pieces):
    return jnp.concatenate([piece[...] for piece in pieces], axis=1)


def forward_kernel(tick, rows, length, hidden, old, count, section, gain_one, gain_two, cosine, sine, *rest):
    x, rest = rest[:count], rest[count:]
    (wide, tall, vqkv), leaving = rest[:3], rest[old]
    stash, sums, *left_out, left, left_sems = rest[-7:]
    width = leaving.shape[1]
    vg, vu, _ = halves(wide, width, width, width)
    vd, _, _, vo = halves(tall, hidden, hidden, hidden, width)
    piece = hidden // PIECES

    @pl.when(section[0] == tick)
    def run():
        lanes = lane_index(rows)
        lower = lanes < HEAD
        first_half = lax.rem(lanes, HEAD) < HEAD // 2
        token = lax.broadcasted_iota(jnp.int32, (rows, rows), 0)
        other = lax.broadcasted_iota(jnp.int32, (rows, rows), 1)
        seen = jnp.logical_and(token <= other, lax.div(other, length) == lax.div(token, length))
        cos, sin = cosine[...], sine[...]
        residual = assembled(x).astype(F32)
        writes = []
        for app in range(2):
            def give(name, value, app=app):
                i = LEFTS.index(name)
                left[i, app] = value
                write = pltpu.make_async_copy(left.at[i, app], left_out[i].at[app], left_sems.at[i, app])
                write.start()
                writes.append(write)

            get, put = views(stash, stash_widths(hidden), app)
            sums[0, app] = residual
            normed = (residual * mean_scale(residual) * gain_one[...]).astype(BF)
            give("normed", normed)
            joined = dot(normed, vqkv[...])
            chunks = [joined[:, i * LANES : (i + 1) * LANES] for i in range(JOINED // LANES)]
            turned = (QUERY + PAIR) // LANES
            for i in range(turned):
                chunks[i] = chunks[i] * cos + half_turned(chunks[i], first_half) * sin
            queries = [chunk.astype(BF) for chunk in chunks[:CHUNKS]]
            keys = spread_groups(chunks, QUERY, lower)
            values = spread_groups(chunks, QUERY + PAIR, lower)
            for name, (low, high) in (("keys", keys), ("values", values)):
                for group in range(KV_HEADS):
                    at = 2 * group * LANES
                    put(name, low[group], at)
                    put(name, high[group], at + LANES)
            key_sides = [jnp.concatenate(chunk_operand(keys, c), axis=0) for c in range(CHUNKS)]
            value_sides = [jnp.concatenate(chunk_operand(values, c), axis=0) for c in range(CHUNKS)]
            all_scores = [dot_last(key_sides[c], queries[c]) for c in range(CHUNKS)]
            all_chances = []
            for c in range(CHUNKS):
                put("query", queries[c], c * LANES)
                parts = []
                for side in range(len(chunk_heads(c))):
                    at = (2 * c + side) * LANES
                    scores = all_scores[c][side * rows : (side + 1) * rows] * HEAD ** (-0.5)
                    scores = jnp.where(seen, scores, -1e30)
                    highest = jnp.max(scores, axis=0, keepdims=True)
                    powers = jnp.exp(scores - highest)
                    total = jnp.sum(powers, axis=0, keepdims=True)
                    parts.append((powers * (1.0 / total)).astype(BF))
                    put("chances", parts[side], at)
                all_chances.append(jnp.concatenate(parts, axis=0))
            contexts = [dot_first(all_chances[c], value_sides[c]).astype(BF) for c in range(CHUNKS)]
            context = jnp.concatenate(contexts, axis=1)[:, :QUERY]
            give("context", context)
            middle = residual + dot(context, vo[...])
            sums[1, app] = middle
            second = (middle * mean_scale(middle) * gain_two[...]).astype(BF)
            give("second", second)
            total = middle
            for i in range(PIECES):
                cols = slice(i * piece, (i + 1) * piece)
                gate = dot(second, vg[:, cols])
                up = dot(second, vu[:, cols])
                sigma = jax.nn.sigmoid(gate)
                linear = gate * sigma
                put("gate_factor", (up * (sigma + linear * (1.0 - sigma))).astype(BF), i * piece)
                put("up_factor", linear.astype(BF), i * piece)
                total = total + dot((linear * up).astype(BF), vd[cols])
            residual = total
        leaving[...] = residual.astype(BF)
        for write in writes:
            write.wait()


def vmem():
    return pl.BlockSpec(memory_space=pltpu.VMEM)


def anywhere():
    return pl.BlockSpec(memory_space=pl.ANY)


def pinned(arrays):
    return [pltpu.with_memory_space_constraint(array, pltpu.HBM) for array in arrays]


def resident(arrays):
    return [pltpu.with_memory_space_constraint(array, pltpu.VMEM) for array in arrays]


def vmem_like(arrays):
    return [pltpu.VMEM(array.shape, array.dtype) for array in arrays]


def forward_pass(tick, section, x, gains, tables, weights, stash, lefts, length, hidden):
    rows, width = x[0].shape[0], weights[1].shape[1]
    held = [*weights, *stash]
    count = len(x)
    outs = pl.pallas_call(
        functools.partial(forward_kernel, tick, rows, length, hidden, len(held) + len(lefts), count),
        out_shape=[pltpu.VMEM((rows, width), BF)]
        + vmem_like(weights)
        + [pltpu.VMEM(stash_shape(rows, hidden), BF), pltpu.VMEM((2, 2, rows, width), F32)]
        + [pltpu.HBM((2, rows, width), BF)] * len(LEFTS),
        in_specs=[pl.BlockSpec(memory_space=pltpu.SMEM)]
        + [vmem()] * (4 + count + len(held))
        + [pl.BlockSpec(memory_space=pltpu.HBM)] * len(lefts),
        out_specs=[vmem()] * (3 + len(weights)) + [pl.BlockSpec(memory_space=pltpu.HBM)] * len(LEFTS),
        scratch_shapes=[
            pltpu.VMEM((len(LEFTS), 2, rows, width), BF),
            pltpu.SemaphoreType.DMA((len(LEFTS), 2)),
        ],
        input_output_aliases={5 + count + i: 1 + i for i in range(len(held) + len(lefts))},
        compiler_params=pltpu.CompilerParams(vmem_limit_bytes=16 * MEGA),
        name="forward_pass",
    )(section, *resident((*gains, *tables, *x, *held)), *pinned(lefts))
    first = 1 + len(weights)
    return outs[0], outs[1:first], outs[first : first + 2], outs[first + 2 :]


SLOPES = {"branch": QUERY, "attend": JOINED, "first": QUERY, "second": QUERY}
SLOPES_WIDTH = sum(-(-width // LANES) * LANES for width in SLOPES.values())


def backward_kernel(tick, rows, length, hidden, old, count, saves, section, gain_one, gain_two, cosine, sine, *rest):
    slope_in, rest = rest[:count], rest[count:]
    (wot, wqkvt, wide, tall, stash, sums), rest = rest[:6], rest[6 + old :]
    leaving, _, _, _, _, made, mixer_out, *far, vot, vqkvt, mixers, sems, mixer_sems, far_sems = rest
    near = (stash, sums, made)
    saving = [pltpu.make_async_copy(near[i], far[i], far_sems.at[i]) for i in range(2)] if saves else []
    sending = [
        pltpu.make_async_copy(made.at[app], far[2].at[app], far_sems.at[2 + app]) for app in range(2) if saves
    ]
    width = leaving.shape[1]
    if saves:
        _, _, vdt = halves(wide, width, width, width)
        _, vgt, vut, _ = halves(tall, hidden, hidden, hidden, width)
    else:
        vdt, (vgt, vut) = wide, halves(tall, hidden, hidden)
    piece = hidden // PIECES

    @pl.when(section[0] == tick)
    def run():
        lanes = lane_index(rows)
        lower = lanes < HEAD
        first_half = lax.rem(lanes, HEAD) < HEAD // 2
        cos, sin = cosine[...], sine[...]
        copies = [
            pltpu.make_async_copy(wot, vot, sems.at[0]),
            pltpu.make_async_copy(wqkvt, vqkvt, sems.at[1]),
        ]
        for copy in copies:
            copy.start()
        slope = assembled(slope_in).astype(F32)
        writes = []
        for app in (1, 0):
            if app == 0:
                for copy in saving + sending[1:]:
                    copy.start()
            get, _ = views(stash, stash_widths(hidden), app)
            _, put = views(made, SLOPES, app)
            mixer = slope.astype(BF)
            mixers[app] = mixer
            writes.append(pltpu.make_async_copy(mixers.at[app], mixer_out.at[app], mixer_sems.at[app]))
            writes[-1].start()
            back = None
            for i in range(PIECES):
                cols = slice(i * piece, (i + 1) * piece)
                active = dot(mixer, vdt[:, cols])
                gate = (active * get("gate_factor", i * piece, (i + 1) * piece).astype(F32)).astype(BF)
                up = (active * get("up_factor", i * piece, (i + 1) * piece).astype(F32)).astype(BF)
                part = dot(gate, vgt[cols]) + dot(up, vut[cols])
                back = part if back is None else back + part
            middle = sums[1, app]
            scale = mean_scale(middle)
            shaped = back * gain_two[...]
            inner = jnp.mean(shaped * middle, axis=-1, keepdims=True)
            put("second", (back * middle * scale).astype(BF))
            middle_slope = slope + scale * shaped - middle * (scale * scale * scale * inner)
            branch = middle_slope.astype(BF)
            put("branch", branch)
            if app == 1:
                copies[0].wait()
            context_slope = dot(branch, vot[...])
            query_back, key_back, value_back = [], {}, {}

            def operand(name, c):
                sides = range(len(chunk_heads(c)))
                places = [2 * c + side if name == "chances" else 2 * group_of(2 * c + side) + side for side in sides]
                return jnp.concatenate([get(name, place * LANES, (place + 1) * LANES) for place in places], axis=0)

            rounded = [context_slope[:, c * LANES : (c + 1) * LANES].astype(BF) for c in range(CHUNKS)]
            all_slopes = [dot_last(operand("values", c), rounded[c]) for c in range(CHUNKS)]
            all_chances = [operand("chances", c) for c in range(CHUNKS)]
            value_parts = [dot(all_chances[c], rounded[c]) for c in range(CHUNKS)]
            all_scores = []
            for c in range(CHUNKS):
                scores = []
                for side in range(len(chunk_heads(c))):
                    band = slice(side * rows, (side + 1) * rows)
                    chance, chance_slope = all_chances[c][band].astype(F32), all_slopes[c][band]
                    inner = jnp.sum(chance * chance_slope, axis=0, keepdims=True)
                    scores.append((chance * (chance_slope - inner)).astype(BF))
                all_scores.append(jnp.concatenate(scores, axis=0))
            key_parts = [dot(all_scores[c], get("query", c * LANES, (c + 1) * LANES)) for c in range(CHUNKS)]
            query_back = [dot_first(all_scores[c], operand("keys", c)) for c in range(CHUNKS)]
            for c in range(CHUNKS):
                key_part, value_part = key_parts[c], value_parts[c]
                for head in chunk_heads(c):
                    side, group = head % 2, group_of(head)
                    band = slice(side * rows, (side + 1) * rows)
                    for store, part in ((key_back, key_part), (value_back, value_part)):
                        item = part[band]
                        store[group, side] = store[group, side] + item if (group, side) in store else item

            def gathered(store, group, up_half):
                low, high = store[group, 0], store[group, 1]
                if up_half:
                    return pltpu.roll(low, HEAD, 1) + high
                return low + pltpu.roll(high, HEAD, 1)

            chunks = query_back + [None] * (JOINED // LANES - CHUNKS)
            for store, start in ((key_back, QUERY), (value_back, QUERY + PAIR)):
                for group in range(KV_HEADS):
                    at, offset = divmod(start + group * HEAD, LANES)
                    item = gathered(store, group, offset > 0)
                    if offset == 0:
                        chunks[at] = jnp.where(lower, item, 0.0)
                    else:
                        chunks[at] = jnp.where(lower, chunks[at], item)
            for i in range((QUERY + PAIR) // LANES):
                chunks[i] = (chunks[i] * cos - half_turned(chunks[i], first_half) * sin) * HEAD ** (-0.5)
            attend = jnp.concatenate([chunk.astype(BF) for chunk in chunks], axis=1)
            put("attend", attend)
            if app == 1:
                copies[1].wait()
            back = dot(attend, vqkvt[...])
            residual = sums[0, app]
            scale = mean_scale(residual)
            shaped = back * gain_one[...]
            inner = jnp.mean(shaped * residual, axis=-1, keepdims=True)
            put("first", (back * residual * scale).astype(BF))
            slope = middle_slope + scale * shaped - residual * (scale * scale * scale * inner)
        leaving[...] = slope.astype(BF)
        for write in writes:
            write.wait()

    @pl.when(section[0] != tick)
    def save():
        for copy in saving + sending[1:]:
            copy.start()

    for copy in sending[:1]:
        copy.start()
    for copy in saving + sending:
        copy.wait()


def backward_pass(tick, section, slope, gains, tables, stash, streamed, weights, made, mixers, length, hidden, saves):
    rows, width = slope[0].shape[0], weights[1].shape[1]
    held = [*weights, *stash, *made]
    count = len(slope)
    outs = pl.pallas_call(
        functools.partial(backward_kernel, tick, rows, length, hidden, len(made) + len(mixers), count, saves),
        out_shape=[pltpu.VMEM((rows, width), BF)]
        + vmem_like([*weights, *stash])
        + [pltpu.VMEM((2, rows, SLOPES_WIDTH), BF), pltpu.HBM((2, rows, width), BF)]
        + (
            [pltpu.HBM(array.shape, array.dtype) for array in stash] + [pltpu.HBM((2, rows, SLOPES_WIDTH), BF)]
            if saves
            else []
        ),
        in_specs=[pl.BlockSpec(memory_space=pltpu.SMEM)]
        + [vmem()] * (4 + count)
        + [pl.BlockSpec(memory_space=pltpu.HBM)] * 2
        + [vmem()] * len(held)
        + [pl.BlockSpec(memory_space=pltpu.HBM)] * len(mixers),
        out_specs=[vmem()] * 6 + [pl.BlockSpec(memory_space=pltpu.HBM)] * (4 if saves else 1),
        scratch_shapes=[pltpu.VMEM(w.shape, BF) for w in streamed]
        + [pltpu.VMEM((2, rows, width), BF)]
        + [pltpu.SemaphoreType.DMA((2,))] * 2
        + [pltpu.SemaphoreType.DMA((4,))],
        input_output_aliases={7 + count + i: 1 + i for i in range(len(held) + len(mixers))},
        compiler_params=pltpu.CompilerParams(vmem_limit_bytes=16 * MEGA),
        name="backward_pass",
    )(section, *resident((*gains, *tables, *slope)), *pinned(streamed), *resident(held), *pinned(mixers))
    return outs[0], outs[1:3], outs[3:5], outs[5:6], outs[6:7], outs[7:]


def turn(source, target, row=0, column=0):
    depth, width = source.shape
    for start in range(0, width, LANES):
        stop = min(start + LANES, width)
        target[row + start : row + stop, column : column + depth] = source[:, start:stop].T


def load_kernel(wq, wkt, wvt, wo, wg, wu, wdt, wide, tall, vqkv, sq, pairs, sems):
    width, pair = wq.shape[0], wkt.shape[0]
    vg, vu, vdt = halves(wide, width, width, width)
    vd, _, _, vo = halves(tall, *[wg.shape[1]] * 3, width)
    moves = [(wdt, vdt), (wkt, pairs.at[pl.ds(0, pair)]), (wvt, pairs.at[pl.ds(pair, pair)]), (wq, sq), (wo, vo)]
    step = width // 3
    for i in range(3):
        band = pl.ds(i * step, step)
        moves += [(wg.at[band], vg.at[band]), (wu.at[band], vu.at[band])]
    copies = [pltpu.make_async_copy(source, target, sems.at[i]) for i, (source, target) in enumerate(moves)]
    for copy in copies:
        copy.start()
    pairs[2 * pair :] = jnp.zeros((HEAD, width), BF)
    copies[0].wait()
    turn(vdt, vd)
    for copy in copies[1:4]:
        copy.wait()
    vqkv[:, :width] = sq[...]
    vqkv[:, width:] = pairs[...].T
    for copy in copies[4:]:
        copy.wait()


def load(wq, wkt, wvt, wo, wg, wu, wdt):
    width, hidden = wg.shape
    return pl.pallas_call(
        load_kernel,
        out_shape=[
            pltpu.VMEM((3 * width, hidden), BF),
            pltpu.VMEM((3 * hidden + width, width), BF),
            pltpu.VMEM((width, JOINED), BF),
        ],
        in_specs=[pl.BlockSpec(memory_space=pltpu.HBM)] * 7,
        out_specs=[vmem()] * 3,
        scratch_shapes=[
            pltpu.VMEM(wq.shape, BF),
            pltpu.VMEM((2 * PAIR + HEAD, width), BF),
            pltpu.SemaphoreType.DMA((11,)),
        ],
        compiler_params=pltpu.CompilerParams(vmem_limit_bytes=16 * MEGA),
        name="load_weights",
    )(*pinned((wq, wkt, wvt, wo, wg, wu, wdt)))


def turn_kernel(wide, tall, vqkv, wide_out, tall_out, vqkv_out, wot, wback, wqkvt, vot, vqkvt, sems):
    hidden, width = wide.shape[1], tall.shape[1]
    vg, vu, _ = halves(wide, width, width, width)
    _, vgt, vut, vo = halves(tall, hidden, hidden, hidden, width)
    copies = [
        pltpu.make_async_copy(source, target, sems.at[i])
        for i, (source, target) in enumerate(zip((vot, vgt, vut), [wot] + halves(wback, hidden, hidden)))
    ]
    vot[:, :width] = vo[...].T
    vot[:, width:] = jnp.zeros((width, HEAD), BF)
    copies[0].start()
    copies.append(pltpu.make_async_copy(vqkvt, wqkvt, sems.at[3]))
    for source, target, copy in zip((vg, vu, vqkv), (vgt, vut, vqkvt), copies[1:]):
        turn(source, target)
        copy.start()
    for copy in copies:
        copy.wait()


def turned(wide, tall, vqkv):
    hidden, width = wide.shape[1], tall.shape[1]
    back = (2 * hidden, width)
    return pl.pallas_call(
        turn_kernel,
        out_shape=vmem_like((wide, tall, vqkv))
        + [pltpu.HBM((width, CHUNKS * LANES), BF), pltpu.HBM(back, BF), pltpu.HBM((JOINED, width), BF)],
        in_specs=[vmem()] * 3,
        out_specs=[vmem()] * 3 + [pl.BlockSpec(memory_space=pltpu.HBM)] * 3,
        scratch_shapes=[
            pltpu.VMEM((width, CHUNKS * LANES), BF),
            pltpu.VMEM((JOINED, width), BF),
            pltpu.SemaphoreType.DMA((4,)),
        ],
        input_output_aliases={0: 0, 1: 1, 2: 2},
        compiler_params=pltpu.CompilerParams(vmem_limit_bytes=16 * MEGA),
        name="turn_weights",
    )(*resident((wide, tall, vqkv)))


def moved_kernel(count, *refs):
    copies = [
        pltpu.make_async_copy(refs[i], refs[count + i], refs[-1].at[i]) for i in range(count)
    ]
    for copy in copies:
        copy.start()
    for copy in copies:
        copy.wait()


def moved(arrays, inward):
    count = len(arrays)
    near, far = (vmem(), pltpu.VMEM), (pl.BlockSpec(memory_space=pltpu.HBM), pltpu.HBM)
    (source, _), (target, place) = (far, near) if inward else (near, far)
    return pl.pallas_call(
        functools.partial(moved_kernel, count),
        out_shape=[place(array.shape, array.dtype) for array in arrays],
        in_specs=[source] * count,
        out_specs=[target] * count,
        scratch_shapes=[pltpu.SemaphoreType.DMA((count,))],
        compiler_params=pltpu.CompilerParams(vmem_limit_bytes=16 * MEGA),
        cost_estimate=pl.CostEstimate(
            flops=0, bytes_accessed=2 * sum(array.size * array.dtype.itemsize for array in arrays), transcendentals=0
        ),
        name="restored" if inward else "saved",
    )(*(pinned if inward else resident)(arrays))


def parts_kernel(normed, context, made, out, stage, sems):
    rows = normed.shape[0] * normed.shape[1]
    edge = QUERY + 2 * PAIR
    gets = [views(made, SLOPES, app)[0] for app in range(2)]
    attend, branch, first, second = (
        jnp.concatenate([get(name) for get in gets], axis=0) for name in ("attend", "branch", "first", "second")
    )

    def flat(ref):
        return ref[...].reshape(rows, ref.shape[2])

    half = 6 * LANES
    bounds = (0, half, JOINED, stage.shape[1])
    copies = [
        pltpu.make_async_copy(stage.at[:, pl.ds(low, high - low)], out.at[:, pl.ds(low, high - low)], sems.at[i])
        for i, (low, high) in enumerate(zip(bounds[:-1], bounds[1:]))
    ]
    left, right = flat(normed), attend
    stage[:, :half] = dot_first(left, right[:, :half]).astype(BF)
    copies[0].start()
    stage[:, half:JOINED] = dot_first(left, right[:, half:]).astype(BF)
    lanes = lax.broadcasted_iota(jnp.int32, (rows, HEAD), 1)
    gains = dot_first(first, (lanes == 0).astype(BF)) + dot_first(second, (lanes == 1).astype(BF))
    stage[:, edge:JOINED] = gains.astype(BF)
    copies[1].start()
    stage[:, JOINED : JOINED + QUERY] = dot_first(flat(context), branch).astype(BF)
    stage[:, JOINED + QUERY :] = jnp.zeros((QUERY, HEAD), BF)
    copies[2].start()
    for copy in copies:
        copy.wait()


def parts(normed, context, made):
    shape = (QUERY, JOINED + QUERY + HEAD)
    return pl.pallas_call(
        parts_kernel,
        out_shape=pltpu.HBM(shape, BF),
        in_specs=[vmem()] * 3,
        out_specs=pl.BlockSpec(memory_space=pltpu.HBM),
        scratch_shapes=[pltpu.VMEM(shape, BF), pltpu.SemaphoreType.DMA((3,))],
        compiler_params=pltpu.CompilerParams(vmem_limit_bytes=16 * MEGA),
        cost_estimate=pl.CostEstimate(flops=4 * shape[0] * shape[1] * normed.shape[0] * normed.shape[1], bytes_accessed=4 * shape[0] * shape[1], transcendentals=0),
        name="attention_parts",
    )(*resident((normed, context, made)))


def factors_kernel(second, wg, wu, gate_factor, up_factor, active):
    step = 256
    for i in range(second.shape[0] // step):
        band = slice(i * step, (i + 1) * step)
        block = second[band]
        gate = dot(block, wg[...])
        up = dot(block, wu[...])
        sigma = jax.nn.sigmoid(gate)
        linear = gate * sigma
        gate_factor[band] = (up * (sigma + linear * (1.0 - sigma))).astype(BF)
        up_factor[band] = linear.astype(BF)
        active[band] = (linear * up).astype(BF)


def factors(second_all, band, wg, wu):
    rows, width = BAND, second_all.shape[1]
    hidden = wg.shape[1]
    block, piece = 512, 512
    first = band * (rows // block)
    wide = pl.BlockSpec((block, piece), lambda i, j: (j, i))
    weight = pl.BlockSpec((width, piece), lambda i, j: (0, i))
    return pl.pallas_call(
        factors_kernel,
        grid=(hidden // piece, rows // block),
        out_shape=[pltpu.HBM((rows, hidden), BF)] * 3,
        in_specs=[
            pl.BlockSpec((block, width), lambda i, j: (first + j, 0)),
            weight,
            weight,
        ],
        out_specs=[wide] * 3,
        compiler_params=pltpu.CompilerParams(vmem_limit_bytes=16 * MEGA),
        cost_estimate=pl.CostEstimate(flops=4 * rows * width * hidden, bytes_accessed=8 * rows * hidden, transcendentals=rows * hidden),
        name="feed_factors",
    )(second_all, *pinned((wg, wu)))


def feed_kernel(own, last, mixer, second, chosen, wdt, gate_factor, up_factor, active, *rest):
    earlier, (gate, up, down, squares, mine, second_own) = rest[:-6], rest[-6:]

    @pl.when(pl.program_id(0) == 0)
    def pick():
        mine[...] = dot(mixer[...], chosen[...]).T.astype(BF)
        second_own[...] = dot(second[...], chosen[...]).T.astype(BF)
        squares[...] = jnp.zeros_like(squares)

    parts = None
    step = mixer.shape[0] // 2
    for i in range(2):
        band = slice(i * step, (i + 1) * step)
        slope = dot(mixer[band], wdt[...])
        gate_slope = (slope * gate_factor[band].astype(F32)).astype(BF)
        up_slope = (slope * up_factor[band].astype(F32)).astype(BF)
        here = (
            dot(second_own[:, band], gate_slope),
            dot(second_own[:, band], up_slope),
            dot(mine[:, band], active[band]),
        )
        parts = here if parts is None else [a + b for a, b in zip(parts, here)]
    for k, (ref, part) in enumerate(zip((gate, up, down), parts)):
        part = part[:own]
        if earlier:
            part = part + earlier[k][...]
        ref[...] = part
        if last:
            squares[...] += jnp.sum(part * part, axis=0, keepdims=True)


def feed(own, last, band, mixer_all, second_all, chosen, wdt, made, earlier):
    rows, width = BAND, mixer_all.shape[1]
    hidden = wdt.shape[1]
    piece = 512
    whole = lambda i: (0, 0)
    column = lambda i: (0, i)
    once = pl.Buffered(1)
    result = pl.BlockSpec((own, piece), column)
    return pl.pallas_call(
        functools.partial(feed_kernel, own, last),
        grid=(hidden // piece,),
        out_shape=[(jax.ShapeDtypeStruct if last else pltpu.HBM)((own, hidden), F32)] * 3
        + [jax.ShapeDtypeStruct((1, piece), F32)],
        in_specs=[pl.BlockSpec((rows, width), lambda i: (band, 0), pipeline_mode=once)] * 2
        + [pl.BlockSpec(chosen.shape, whole, pipeline_mode=once), pl.BlockSpec((width, piece), column)]
        + [pl.BlockSpec((rows, piece), column)] * 3
        + [result] * len(earlier),
        out_specs=[result] * 3 + [pl.BlockSpec((1, piece), whole)],
        scratch_shapes=[pltpu.VMEM((chosen.shape[1], rows), BF)] * 2,
        compiler_params=pltpu.CompilerParams(vmem_limit_bytes=16 * MEGA),
        cost_estimate=pl.CostEstimate(
            flops=2 * (rows + 3 * own) * wdt.size, bytes_accessed=8 * rows * hidden, transcendentals=0
        ),
        name="feed_gradient",
    )(mixer_all, second_all, chosen, *pinned((wdt, *made, *earlier)))


def finish_kernel(terms, squares, query, key, value, output, gains, total):
    edge = QUERY + 2 * PAIR
    whole = terms[...].astype(F32)
    query[...] = whole[:, :QUERY]
    key[...] = whole[:, QUERY : QUERY + PAIR].T
    value[...] = whole[:, QUERY + PAIR : edge].T
    output[...] = whole[:, JOINED : JOINED + QUERY]
    gains[...] = whole[:, edge : edge + 2]
    sums = jnp.sum(whole * whole, axis=0, keepdims=True)
    total[...] = jnp.sum(sums, axis=1, keepdims=True) + jnp.sum(squares[...], axis=1, keepdims=True)


def finish(terms, squares):
    own = terms.shape[0]
    shapes = ((own, QUERY), (PAIR, own), (PAIR, own), (own, QUERY), (own, 2), (1, 1))
    return pl.pallas_call(
        finish_kernel,
        out_shape=[jax.ShapeDtypeStruct(shape, F32) for shape in shapes],
        in_specs=[vmem()] * 2,
        out_specs=[vmem()] * len(shapes),
        compiler_params=pltpu.CompilerParams(vmem_limit_bytes=16 * MEGA),
        name="finish",
    )(terms, squares)


def after(value, *tokens):
    return lax.optimization_barrier((value,) + tokens)[0]


def gathered_at(block, axis, target):
    count = lax.axis_size(axis)
    pieces = [block if s == target else lax.ppermute(block, axis, [(s, target)]) for s in range(count)]
    return pieces


def spread_from(whole, axis, source):
    count = lax.axis_size(axis)
    width = whole.shape[1] // count
    columns = [whole[:, s * width : (s + 1) * width] for s in range(count)]
    mine = jnp.where(lax.axis_index(axis) == source, columns[source], jnp.zeros_like(columns[source]))
    for s in range(count):
        if s != source:
            mine = mine + lax.ppermute(columns[s], axis, [(source, s)])
    return mine


class LineGather:
    def __init__(self, block, axis):
        self.axis, self.count = axis, lax.axis_size(axis)
        self.line, self.step = self.count // 2, 0
        self.held = [block] + [None] * (self.line - 1)
        self.moving = (block, block)

    def advance(self, *tokens):
        ahead = [(i, i + 2) for i in range(self.count - 2)]
        self.step += 1
        below, above = self.moving
        if tokens:
            below, above, *_ = lax.optimization_barrier((below, above, *tokens))
        below = lax.ppermute(below, self.axis, ahead)
        above = lax.ppermute(above, self.axis, [(b, a) for a, b in ahead])
        self.moving = (below, above)
        for k, item in ((self.step, below), (self.line - self.step, above)):
            self.held[k] = item if self.held[k] is None else self.held[k] + item

    def finish(self):
        while self.step < self.line - 1:
            self.advance()
        mine = jnp.concatenate(self.held)
        other = lax.ppermute(mine, self.axis, [(i, i ^ 1) for i in range(self.count)])
        bands = [slice(start, start + BAND) for start in range(0, mine.shape[0], BAND)]
        return [half[band] for half in (mine, other) for band in bands]


def summed(value, axis):
    count, distance = lax.axis_size(axis), 1
    while distance < count:
        value = value + lax.ppermute(value, axis, [(i, i ^ distance) for i in range(count)])
        distance *= 2
    return value


def per_device(
    inputs, cotangent, first_gain, w_query, w_key, w_value, w_output, second_gain, w_gate, w_up, w_down
):
    sections = lax.axis_size("section")
    replicas = lax.axis_size("dp")
    section = lax.axis_index("section")
    micro, length, part = inputs.shape
    rows, width = micro * length, part * sections
    hidden = w_gate.shape[2]
    own = width // replicas
    w_query, w_key, w_value, w_output = w_query[0], w_key[0], w_value[0], w_output[0]
    w_gate, w_up, w_down = w_gate[0], w_up[0], w_down[0]
    gains = (first_gain, second_gain)
    tables = tuple(jnp.asarray(table) for table in rotary_tables(length, rows))
    place = section.astype(jnp.int32).reshape(1)
    w_query, place = lax.optimization_barrier((w_query, place))
    own_rows = -(-own // 16) * 16
    at = lax.broadcasted_iota(jnp.int32, (width, own_rows), 1)
    chosen = jnp.logical_and(
        lax.broadcasted_iota(jnp.int32, (width, own_rows), 0) == at + own * lax.axis_index("dp"), at < own
    ).astype(BF)

    x = gathered_at(inputs.reshape(rows, part), "section", 0)
    w_down = w_down.T
    weights = load(w_query, w_key.T, w_value.T, w_output, w_gate, w_up, w_down)
    last_slope = gathered_at(cotangent.reshape(rows, part), "section", sections - 1)

    stash = lefts = ()
    for t in range(sections):
        leaving, weights, stash, lefts = forward_pass(
            t, place, x, gains, tables, weights, stash, lefts, length, hidden
        )
        if t < sections - 1:
            x = [lax.ppermute(leaving, "section", [(t, t + 1)])]
        if t == 0:
            *weights, output_back, back_far, joined_back = turned(*weights)
    normed, context, second = lefts
    streamed = (output_back, joined_back)
    weights = weights[:2]

    final = leaving
    slope = last_slope
    made = mixers = ()
    for t in reversed(range(sections)):
        leaving, weights, stash, made, mixers, far = backward_pass(
            t, place, slope, gains, tables, stash, streamed, weights, made, mixers, length, hidden, t == sections - 1
        )
        if t > 0:
            slope = [lax.ppermute(leaving, "section", [(t, t - 1)])]
        if t > 0:
            if t == sections - 1:
                second_all = lax.all_gather(after(second.reshape(2 * rows, width), far[0]), "dp", axis=0, tiled=True)
                near = moved((w_down, back_far, *far), True)
                weights, stash, made = near[:2], near[2:4], near[4:]
    mixer_all = lax.all_gather(mixers[0].reshape(2 * rows, width), "dp", axis=0, tiled=True)
    terms = parts(normed, context, made[0])
    index = after(lax.axis_index("dp"), leaving)
    pairs = terms.reshape(replicas // 2, 2, own, terms.shape[1])
    other = lax.dynamic_index_in_dim(pairs, 1 - lax.bitwise_and(index, 1), 1, keepdims=False)
    mine = lax.dynamic_index_in_dim(pairs, lax.bitwise_and(index, 1), 1, keepdims=False)
    swap = [(i, i ^ 1) for i in range(replicas)]
    other = lax.ppermute(other, "dp", swap)
    made = [factors(second_all, 0, w_gate, w_up)]
    other = after(other, made[0][0])
    terms = (mine + other).reshape(-1, terms.shape[1])
    groups = [list(range(core, replicas, 2)) for core in range(2)]
    reduced = lax.psum_scatter(terms, "dp", scatter_dimension=0, axis_index_groups=groups, tiled=True)
    made += [factors(second_all, band, w_gate, w_up) for band in range(1, 2 * rows * replicas // BAND)]
    feed_parts = ()
    for band, item in enumerate(made):
        last = band == len(made) - 1
        *feed_parts, squares = feed(own, last, band, mixer_all, second_all, chosen, w_down, item, feed_parts)
    gate, up, down = feed_parts
    outputs, delta_inputs = (
        spread_from(after(item, squares), "section", source)
        for item, source in ((final, sections - 1), (leaving, 0))
    )
    query, key, value, output, gain_terms, total = finish(reduced, squares)
    total = summed(summed(total, "dp"), "section")
    return (
        outputs.astype(F32).reshape(micro, length, part),
        delta_inputs.astype(F32).reshape(micro, length, part),
        gain_terms[:, 0][None],
        query[None],
        key.T[None],
        value.T[None],
        output[None],
        gain_terms[:, 1][None],
        gate[None],
        up[None],
        down.T[None],
        jnp.sqrt(total).reshape(()),
    )


def solution(mesh):
    stacked = P("section", None, None)
    rows = P("section", "dp", None)
    return jax.shard_map(
        per_device,
        mesh=mesh,
        in_specs=(P("dp", None, "section"),) * 2
        + (P("section", None),)
        + (stacked,) * 4
        + (P("section", None),)
        + (stacked,) * 3,
        out_specs=(P("dp", None, "section"),) * 2
        + (P("section", "dp"),)
        + (rows,) * 4
        + (P("section", "dp"),)
        + (rows,) * 2
        + (P("section", None, "dp"), P()),
        check_vma=False,
    )
```
